32 devices in a mesh: dp: 8 (over y, x, core), tensor: 4 (over z).
Axes of the slice: x: 2, y: 2, z: 4, core: 2. Of those that a mesh axis runs over, the one named last changes fastest.
Arguments:
- tokens: bfloat16 [36864, 512], P('dp'), may hold values from -6 to 6
- first_gain: float32 [512], replicated, may hold values from 0.5 to 1.5
- second_gain: float32 [512], replicated, may hold values from 0.5 to 1.5
- query_weight: bfloat16 [512, 512], P(None, 'tensor'), may hold values from -0.25 to 0.25
- key_weight: bfloat16 [512, 512], P(None, 'tensor'), may hold values from -0.25 to 0.25
- value_weight: bfloat16 [512, 512], P(None, 'tensor'), may hold values from -0.25 to 0.25
- out_weight: bfloat16 [512, 512], P('tensor'), may hold values from -1.5 to 1.5
- key_conv: bfloat16 [8, 192, 64], P('tensor'), may hold values from -0.4375 to 0.4375
- value_conv: bfloat16 [8, 192, 64], P('tensor'), may hold values from -0.4375 to 0.4375
- up_weight: bfloat16 [512, 2048], P(None, 'tensor'), may hold values from -0.25 to 0.25
- down_weight: bfloat16 [2048, 512], P('tensor'), may hold values from -0.125 to 0.125
- pad_mask: int32 [36864], P('dp'), may hold values 0 or 1
- item_lengths: int32 [8, 6], P('dp'), may hold values from 1 to 768, 1536 in all within a row
- cotangent: bfloat16 [36864, 512], P('dp'), may hold values from -6 to 6
Outputs:
- mixed_out: bfloat16 [36864, 512], P('dp')
- grad_tokens: bfloat16 [36864, 512], P('dp')
- grad_first_gain: float32 [512], P('dp')
- grad_second_gain: float32 [512], P('dp')
- grad_query: float32 [512, 512], P('dp', 'tensor')
- grad_key: float32 [512, 512], P('dp', 'tensor')
- grad_value: float32 [512, 512], P('dp', 'tensor')
- grad_out: float32 [512, 512], P('tensor', 'dp')
- grad_key_conv: float32 [8, 192, 64], P('tensor', 'dp')
- grad_value_conv: float32 [8, 192, 64], P('tensor', 'dp')
- grad_up: float32 [512, 2048], P('dp', 'tensor')
- grad_down: float32 [2048, 512], P('tensor', 'dp')
The draws below stay inside these ranges and needn't reach their ends.
Inputs may be any that keep to these rules, and one draw needn't show every extreme that they name: `item_lengths`: each row sums to 1536 and its largest entry is 768.
All inputs are finite; a program needn't handle non-finite values. No bound on the sum of `pad_mask` on one device may be relied on, other than what follows from the above.
Results may differ from the reference program's by a relative error of at most 0.019.
Values may be sent and summed in bfloat16 or wider, within the bound.
A program may use at most 256 MiB of HBM per device.

```python
import math
from functools import partial
import jax
import jax.numpy as jnp
import numpy as np
from jax import lax

D = 512
HEADS = 8
HD = 64
FF = 2048
TOK_DEV = 4608
ITEMS = 6
MOST = 768
QBLK = 512
TOKENS = 36864
N_DP = 8
N_TENSOR = 4


def place_ends(entries, key, low, high):
    index_at = [jax.random.randint(jax.random.fold_in(key, axis), (), 0, length) for axis, length in enumerate(entries.shape)]
    main_axis = entries.shape.index(max(entries.shape))
    beside = index_at[:main_axis] + [(index_at[main_axis] + 1) % entries.shape[main_axis]] + index_at[main_axis + 1:]
    return entries.at[tuple(index_at)].set(low).at[tuple(beside)].set(high)


def levels(rng, shape, cuts, low, top_value):
    level = 1.0
    for dim, blocks in cuts:
        steps = jax.random.uniform(jax.random.fold_in(jax.random.fold_in(rng, 6), dim), (blocks,), jnp.float32, low / len(cuts), top_value / len(cuts))
        level = level * jnp.repeat(jnp.exp(steps), shape[dim] // blocks).reshape((-1,) + (1,) * (len(shape) - 1 - dim))
    return level


def length_profile(number_of, total, limit, skew):
    portions = [(1 << 20) // math.isqrt(standing ** skew) + 1 for standing in range(2, number_of + 1)]
    surplus, counts = total - limit - (number_of - 1), [1] * (number_of - 1)
    while surplus > 0:
        free = [i for i in range(number_of - 1) if counts[i] < limit]
        mass, remaining = sum([portions[i] for i in free]), surplus
        for i in free:
            more = min(limit - counts[i], max(1, remaining * portions[i] // mass), surplus)
            counts[i] = counts[i] + more
            surplus = surplus - more
    return np.array([limit] + counts)


def ragged(stream_key, count, total, limit, slope):
    if count == 2:
        one = jax.random.randint(stream_key, (), max(1, total - limit), min(limit, total - 1) + 1)
        return jnp.stack([one, total - one])
    tallies = jnp.asarray(length_profile(count, total, limit, slope), jnp.int32)
    twos = (count - 1) // 2
    donor, sink = tallies[1:1 + 2 * twos:2], tallies[2:2 + 2 * twos:2]
    slack = jnp.minimum(donor - 1, limit - sink)
    passed = jax.random.randint(jax.random.fold_in(stream_key, 1), (twos,), 0, 1 << 20) % (slack + 1)
    tallies = tallies.at[1:1 + 2 * twos:2].set(donor - passed).at[2:2 + 2 * twos:2].set(sink + passed)
    return tallies[jax.random.permutation(jax.random.fold_in(stream_key, 2), count)]


def noise(own_key, dims, deviation, most, cuts=(), kind=jnp.bfloat16):
    gain = levels(own_key, dims, cuts, -0.22, 0.18) if cuts else 1.0
    drawn = jax.random.normal(own_key, dims, jnp.float32) * deviation * gain
    return jnp.minimum(jnp.maximum(drawn, -most), most).astype(kind)


def setup_inputs(seed: int = 0) -> dict:
    arg_keys = jax.random.split(jax.random.key(seed), 15)
    return {
        "tokens": noise(arg_keys[0], (TOKENS, D), 1.0, 6.0, ((0, 8),)),
        "first_gain": jnp.clip(1.0 + 0.1 * jax.random.normal(arg_keys[1], (D,), jnp.float32), 0.5, 1.5),
        "second_gain": jnp.clip(1.0 + 0.1 * jax.random.normal(arg_keys[2], (D,), jnp.float32), 0.5, 1.5),
        "query_weight": noise(arg_keys[3], (D, D), D ** -0.5, 0.25, ((1, 4),)),
        "key_weight": noise(arg_keys[4], (D, D), D ** -0.5, 0.25, ((1, 4),)),
        "value_weight": noise(arg_keys[5], (D, D), D ** -0.5, 0.25, ((1, 4),)),
        "out_weight": noise(arg_keys[6], (D, D), 16 ** -0.5, 1.5, ((0, 4),)),
        "key_conv": noise(arg_keys[7], (HEADS, 3 * HD, HD), (3 * HD) ** -0.5, 0.4375, ((0, 4),)),
        "value_conv": noise(arg_keys[8], (HEADS, 3 * HD, HD), (3 * HD) ** -0.5, 0.4375, ((0, 4),)),
        "up_weight": noise(arg_keys[9], (D, FF), D ** -0.5, 0.25, ((1, 4),)),
        "down_weight": noise(arg_keys[10], (FF, D), FF ** -0.5, 0.125, ((0, 4),)),
        "pad_mask": place_ends((jax.random.randint(arg_keys[11], (TOKENS,), 0, 8) < 7).astype(jnp.int32), jax.random.fold_in(arg_keys[11], 1), 0, 1),
        "item_lengths": jax.vmap(lambda own: ragged(own, ITEMS, TOK_DEV // 3, MOST, 2))(jax.random.split(arg_keys[12], N_DP)).reshape((N_DP, ITEMS)).astype(jnp.int32),
        "cotangent": noise(arg_keys[13], (TOKENS, D), 1.0, 6.0, ((0, 8),)),
    }


highest = lax.Precision.HIGHEST

@jax.custom_vjp
def low(v):
    return lax.optimization_barrier(v.astype(jnp.bfloat16)).astype(jnp.float32)

@jax.custom_vjp
def low_back(v):
    return v

def low_keep(v):
    return (low(v), None)

def low_pass(kept, grad):
    return (grad,)

def back_keep(v):
    return (v, None)

def back_low(kept, grad):
    return (low(grad),)
low.defvjp(low_keep, low_pass)
low_back.defvjp(back_keep, back_low)

def matmul(left_side, right_side):
    return jnp.dot(left_side, right_side, precision=highest)

def layer_norm(values, gains):
    centred = values - lax.optimization_barrier(jnp.mean(values, -1, keepdims=True))
    variance = lax.optimization_barrier(jnp.mean(centred * centred, -1, keepdims=True))
    return centred * lax.rsqrt(variance + 1e-05) * gains

def items_of(lengths, count):
    ends = jnp.cumsum(lengths * 3)
    places = jnp.arange(count, dtype=jnp.int32)
    return lax.optimization_barrier(jnp.sum((places[:, None] >= ends[None, :]).astype(jnp.int32), axis=1))

def block_attend(inputs, comp_keys, comp_values, group_item):
    queries, own_keys, own_values, places, item_rows = inputs
    factor = 1.0 / math.sqrt(HD)
    own_score = lax.optimization_barrier(jnp.sum(queries * own_keys, -1)).T * factor
    key_score = low_back(jnp.einsum('qhd,hjd->hqj', queries, comp_keys, precision=highest) * factor)
    starts = 3 * jnp.arange(group_item.shape[0], dtype=jnp.int32)
    allowed = (item_rows[:, None] == group_item[None, :]) & (starts[None, :] + 2 < places[:, None])
    key_score = jnp.where(allowed[None], key_score, -1e+30)
    top_score = jnp.maximum(own_score, lax.optimization_barrier(jnp.max(key_score, -1)))
    own_prob = jnp.exp(own_score - top_score)
    key_prob = jnp.exp(key_score - top_score[..., None])
    total = own_prob + lax.optimization_barrier(jnp.sum(key_prob, -1))
    own_prob = own_prob / total
    key_prob = key_prob / total[..., None]
    context = own_prob[..., None] * own_values.transpose(1, 0, 2)
    context = context + jnp.einsum('hqj,hjd->hqd', low(key_prob), comp_values, precision=highest)
    return context.transpose(1, 0, 2)

def pack_forward(params, inputs, real_mask, item_tok):
    first_gain, second_gain, query_w, key_w, value_w, out_w, key_conv, value_conv, up_w, down_w = params
    tok_rows = inputs.shape[0]
    key_groups = tok_rows // 3
    block_count = tok_rows // QBLK
    head_cols = D // N_TENSOR
    unit_cols = FF // N_TENSOR
    normed = low(layer_norm(inputs, first_gain))
    query_parts, key_parts, value_parts = ([], [], [])
    for group in range(N_TENSOR):
        shared = low_back(normed)
        cols = slice(group * head_cols, (group + 1) * head_cols)
        query_parts.append(matmul(shared, query_w[:, cols]))
        key_parts.append(matmul(shared, key_w[:, cols]))
        value_parts.append(matmul(shared, value_w[:, cols]))
    queries = low(low_back(jnp.concatenate(query_parts, 1))).reshape(tok_rows, HEADS, HD)
    keys = low(low_back(jnp.concatenate(key_parts, 1) * real_mask[:, None])).reshape(tok_rows, HEADS, HD)
    values = low(low_back(jnp.concatenate(value_parts, 1) * real_mask[:, None])).reshape(tok_rows, HEADS, HD)

    def compress(sequence, kernel):
        grouped = sequence.reshape(key_groups, 3, HEADS, HD).transpose(2, 0, 1, 3).reshape(HEADS, key_groups, 3 * HD)
        return low(low_back(jnp.einsum('hjc,hcd->hjd', grouped, kernel, precision=highest)))
    comp_keys = compress(keys, key_conv)
    comp_values = compress(values, value_conv)
    group_item = item_tok.reshape(key_groups, 3)[:, 0]
    places = jnp.arange(tok_rows, dtype=jnp.int32).reshape(block_count, QBLK)
    attend = jax.checkpoint(partial(block_attend, comp_keys=comp_keys, comp_values=comp_values, group_item=group_item))
    context = lax.map(attend, (queries.reshape(block_count, QBLK, HEADS, HD), keys.reshape(block_count, QBLK, HEADS, HD), values.reshape(block_count, QBLK, HEADS, HD), places, item_tok.reshape(block_count, QBLK)))
    context = low(low_back(context.reshape(tok_rows, D)))
    attended = jnp.zeros_like(inputs)
    for group in range(N_TENSOR):
        cols = slice(group * head_cols, (group + 1) * head_cols)
        attended = attended + low(matmul(context[:, cols], out_w[cols, :]))
    resid = inputs + low_back(attended)
    second = low(layer_norm(resid, second_gain))
    ffn_total = jnp.zeros_like(inputs)
    for group in range(N_TENSOR):
        shared = low_back(second)
        cols = slice(group * unit_cols, (group + 1) * unit_cols)
        hidden_pre = low_back(matmul(shared, up_w[:, cols]))
        activated = low(jax.nn.gelu(hidden_pre, approximate=False))
        ffn_total = ffn_total + low(matmul(activated, down_w[cols, :]))
    return resid + low_back(ffn_total)

def reference(tokens, first_gain, second_gain, query_weight, key_weight, value_weight, out_weight, key_conv, value_conv, up_weight, down_weight, pad_mask, item_lengths, cotangent):
    params = tuple((array.astype(jnp.float32) for array in (first_gain, second_gain, query_weight, key_weight, value_weight, out_weight, key_conv, value_conv, up_weight, down_weight)))
    packs = (tokens.astype(jnp.float32).reshape(N_DP, TOK_DEV, D), cotangent.astype(jnp.float32).reshape(N_DP, TOK_DEV, D), pad_mask.astype(jnp.float32).reshape(N_DP, TOK_DEV), item_lengths)

    def scan_step(totals, pack):
        inputs, upstream, real_mask, lengths = pack
        item_tok = items_of(lengths, TOK_DEV)
        outputs, backward = jax.vjp(lambda weights, acts: pack_forward(weights, acts, real_mask, item_tok), params, inputs)
        weight_grads, input_grad = backward(upstream)
        totals = jax.tree.map(lambda summed, added: summed + added, totals, weight_grads)
        return (totals, (outputs.astype(jnp.bfloat16), input_grad.astype(jnp.bfloat16)))
    initial = jax.tree.map(jnp.zeros_like, params)
    totals, (mixed, grads) = lax.scan(scan_step, initial, packs)
    return (mixed.reshape(TOKENS, D), grads.reshape(TOKENS, D), totals[0], totals[1], totals[2], totals[3], totals[4], totals[5], totals[6], totals[7], totals[8], totals[9])
```

```python
import functools
import math

import jax
import jax.numpy as jnp
from jax import lax
from jax.experimental import pallas as pl
from jax.experimental.pallas import tpu as pltpu
from jax.sharding import PartitionSpec as P

F32 = jnp.float32
BF16 = jnp.bfloat16
GB = 128
TB = 3 * GB
NEG = -1e30
LOG2E = 1.0 / math.log(2.0)
VMEM = 60 * 1024 * 1024

ERF_P = 0.43
ERF_C = (
    0.24255178053871013,
    0.24376598744271377,
    0.2089868288055898,
    0.23281685899157548,
    -0.05797941172752005,
    0.3523368029188165,
    -0.2915198548110903,
    0.06904073943922798,
)


def nn(a, b):
    return lax.dot_general(a, b, (((1,), (0,)), ((), ())), preferred_element_type=F32)


def nt(a, b):
    return lax.dot_general(a, b, (((1,), (1,)), ((), ())), preferred_element_type=F32)


def tn(a, b):
    return lax.dot_general(a, b, (((0,), (0,)), ((), ())), preferred_element_type=F32)


def norm_rows(values):
    centred = values - jnp.mean(values, -1, keepdims=True)
    inv_std = lax.rsqrt(jnp.mean(centred * centred, -1, keepdims=True) + 1e-05)
    return centred * inv_std, inv_std


def norm_back(grad_out, gains, normed, inv_std):
    scaled = grad_out * gains
    return inv_std * (
        scaled
        - jnp.mean(scaled, -1, keepdims=True)
        - normed * jnp.mean(scaled * normed, -1, keepdims=True)
    )


def tap_major(scratch, values):
    lanes = scratch.shape[2]
    parts = []
    for c in range(scratch.shape[0]):
        scratch[c] = values[:, c * lanes : (c + 1) * lanes]
        taps = [scratch[c, pl.ds(r, GB, stride=3), :] for r in range(3)]
        parts.append(jnp.concatenate(taps, axis=0))
    return jnp.concatenate(parts, axis=1)


def token_major(scratch, values):
    lanes = scratch.shape[2]
    parts = []
    for c in range(scratch.shape[0]):
        for r in range(3):
            scratch[c, pl.ds(r, GB, stride=3), :] = values[
                r * GB : (r + 1) * GB, c * lanes : (c + 1) * lanes
            ]
        parts.append(scratch[c])
    return jnp.concatenate(parts, axis=1)


def gelu_and_slope(h):
    z = jnp.abs(h) * math.sqrt(0.5)
    t = 1.0 / (1.0 + ERF_P * z)
    poly = jnp.full_like(t, ERF_C[-1])
    for c in ERF_C[-2::-1]:
        poly = poly * t + c
    e = jnp.exp(-z * z)
    tail = (0.5 * e) * (poly * t)
    cdf = jnp.where(h >= 0, 1.0 - tail, tail)
    return h * cdf, cdf + h * (e * (1.0 / math.sqrt(2.0 * math.pi)))


def item_starts(lens_ref, block):
    places = block * GB + lax.broadcasted_iota(jnp.int32, (1, GB), 1)
    starts = jnp.zeros((1, GB), jnp.int32)
    least = jnp.int32(0)
    end = jnp.int32(0)
    for i in range(lens_ref.shape[0] - 1):
        end = end + lens_ref[i]
        starts = jnp.where(places >= end, end, starts)
        least = jnp.where(block * GB >= end, end, least)
    return places, starts, least // GB


def mask_bias(places, starts, kb):
    keys = kb * GB + lax.broadcasted_iota(jnp.int32, (GB, GB), 0)
    bias = jnp.where((keys >= starts) & (keys < places), 0.0, NEG)
    return jnp.concatenate([bias] * 3, axis=1)


def key_rows(kb):
    return pl.ds(pl.multiple_of(kb * GB, GB), GB)


def forward_kernel(
    heads, hd, lens_ref, x_ref, gain_ref, w_ref, kconv_ref, vconv_ref, mask_ref,
    q_ref, k_ref, v_ref, ctx_ref, lse_ref, ck_ref, ckt_ref, cv_ref,
    xs, cvt_ref, m_ref, l_ref, acc_ref,
):
    block = pl.program_id(0)
    width = heads * hd
    scale = LOG2E / math.sqrt(hd)
    normed, _ = norm_rows(x_ref[...].astype(F32))
    first_in = tap_major(xs, normed * gain_ref[...]).astype(BF16)
    mask = mask_ref[0, 0:1, :]
    q_ref[...] = nt(w_ref[0:width], first_in).astype(BF16)
    k_ref[...] = (nt(w_ref[width : 2 * width], first_in) * mask).astype(BF16)
    v_ref[...] = (nt(w_ref[2 * width : 3 * width], first_in) * mask).astype(BF16)
    rows = key_rows(block)
    for h in range(heads):
        band = slice(h * hd, (h + 1) * hd)
        for src, conv, plain, trans in ((k_ref, kconv_ref, ck_ref, ckt_ref), (v_ref, vconv_ref, cv_ref, cvt_ref)):
            taps = jnp.concatenate([src[band, r * GB : (r + 1) * GB] for r in range(3)], axis=0)
            comp = nn(conv[h], taps)
            trans[band, rows] = comp.astype(BF16)
            plain[h, rows, :] = comp.T.astype(BF16)
        q, k = q_ref[band, :].astype(F32), k_ref[band, :].astype(F32)
        m_ref[h : h + 1, :] = jnp.sum(q * k, axis=0, keepdims=True) * scale
        acc_ref[band, :] = v_ref[band, :].astype(F32)
    l_ref[...] = jnp.ones_like(l_ref)
    places, starts, low = item_starts(lens_ref, block)

    def step(kb, carry):
        bias = mask_bias(places, starts, kb)
        cols = key_rows(kb)
        for h in range(heads):
            band = slice(h * hd, (h + 1) * hd)
            one = slice(h, h + 1)
            s = nn(ck_ref[h, cols, :], q_ref[band, :]) * scale + bias
            old = m_ref[one, :]
            new = jnp.maximum(old, jnp.max(s, axis=0, keepdims=True))
            p = jnp.exp2(s - new)
            keep = jnp.exp2(old - new)
            m_ref[one, :] = new
            l_ref[one, :] = l_ref[one, :] * keep + jnp.sum(p, axis=0, keepdims=True)
            acc_ref[band, :] = acc_ref[band, :] * keep + nn(cvt_ref[band, cols], p.astype(BF16))
        return carry

    lax.fori_loop(low, block + 1, step, 0)
    lse_ref[...] = m_ref[...] + jnp.log(l_ref[...]) * LOG2E
    inv = 1.0 / l_ref[...]
    for h in range(heads):
        band = slice(h * hd, (h + 1) * hd)
        ctx_ref[band, :] = (acc_ref[band, :] * inv[h : h + 1, :]).astype(BF16)


def middle_kernel(
    heads, hd, x_ref, g_ref, gain_ref, ctx_ref, out_ref, up_ref, down_ref,
    mixed_ref, resid_grad_ref, dctx_ref, delta_ref, grads_ref,
    xs, down_sum, up_sum, out_sum, gain_sum,
):
    block = pl.program_id(0)
    own = out_sum.shape[0]

    @pl.when(block == 0)
    def _():
        down_sum[...] = jnp.zeros_like(down_sum)
        up_sum[...] = jnp.zeros_like(up_sum)
        out_sum[...] = jnp.zeros_like(out_sum)
        gain_sum[...] = jnp.zeros_like(gain_sum)

    gain = gain_ref[...]
    x = tap_major(xs, x_ref[...].astype(F32))
    g = tap_major(xs, g_ref[...].astype(F32))
    g_low = g.astype(BF16)
    resid = x + tn(ctx_ref[...], out_ref[...])
    hat, inv_std = norm_rows(resid)
    second_in = (hat * gain).astype(BF16)
    ffn = jnp.zeros_like(resid)
    back = jnp.zeros_like(resid)
    for c in range(up_ref.shape[0]):
        hidden = nn(second_in, up_ref[c])
        act_grad = nt(g_low, down_ref[c])
        act, slope = gelu_and_slope(hidden)
        act = act.astype(BF16)
        hidden_grad = (act_grad * slope).astype(BF16)
        ffn = ffn + nn(act, down_ref[c])
        back = back + nt(hidden_grad, up_ref[c])
        if c == 0:
            down_sum[...] += tn(act, g_low)
            up_sum[...] += tn(second_in, hidden_grad)
    mixed_ref[...] = token_major(xs, resid + ffn).astype(BF16)
    gain_sum[...] += jnp.sum(back * hat, axis=0, keepdims=True)
    resid_grad = g + norm_back(back, gain, hat, inv_std)
    attn_grad = resid_grad.astype(BF16)
    resid_grad_ref[...] = attn_grad
    out_sum[...] += nn(ctx_ref[0:own, :], attn_grad)
    dctx = nt(out_ref[...], attn_grad).astype(BF16)
    dctx_ref[...] = dctx
    dots = dctx.astype(F32) * ctx_ref[...].astype(F32)
    for h in range(heads):
        delta_ref[h : h + 1, :] = jnp.sum(dots[h * hd : (h + 1) * hd], axis=0, keepdims=True)

    @pl.when(block == pl.num_programs(0) - 1)
    def _():
        units = up_sum.shape[1]
        grads_ref[:, 0:units] = up_sum[...].astype(BF16)
        grads_ref[:, units : 2 * units] = down_sum[...].T.astype(BF16)
        grads_ref[:, 2 * units : 2 * units + own] = out_sum[...].T.astype(BF16)
        grads_ref[:, 2 * units + own :] = jnp.broadcast_to(gain_sum[...], (GB, gain.shape[1])).T.astype(BF16)


def backward_kernel(
    heads, hd, own_heads, lens_ref, x_ref, gain_ref, w_ref, kconv_ref, vconv_ref, mask_ref,
    q_ref, k_ref, v_ref, lse_ref, dctx_ref, delta_ref, resid_grad_ref, ck_ref, ckt_ref, cv_ref,
    tokens_ref, grads_ref, conv_ref,
    xs, dck_sum, dcv_sum, dq_sum, dqkv, weight_sum, kconv_sum, vconv_sum, gain_sum,
):
    step_id = pl.program_id(0)
    block = pl.num_programs(0) - 1 - step_id
    width = heads * hd
    own = own_heads * hd
    factor = 1.0 / math.sqrt(hd)
    scale = LOG2E * factor

    @pl.when(step_id == 0)
    def _():
        dck_sum[...] = jnp.zeros_like(dck_sum)
        dcv_sum[...] = jnp.zeros_like(dcv_sum)
        weight_sum[...] = jnp.zeros_like(weight_sum)
        kconv_sum[...] = jnp.zeros_like(kconv_sum)
        vconv_sum[...] = jnp.zeros_like(vconv_sum)
        gain_sum[...] = jnp.zeros_like(gain_sum)

    dq_sum[...] = jnp.zeros_like(dq_sum)
    places, starts, low = item_starts(lens_ref, block)

    def step(kb, carry):
        bias = mask_bias(places, starts, kb)
        cols = key_rows(kb)
        for h in range(heads):
            band = slice(h * hd, (h + 1) * hd)
            one = slice(h, h + 1)
            q, dctx = q_ref[band, :], dctx_ref[band, :]
            s = nn(ck_ref[h, cols, :], q) * scale + bias
            p = jnp.exp2(s - lse_ref[one, :])
            dp = nn(cv_ref[h, cols, :], dctx)
            ds = (p * (dp - delta_ref[one, :])).astype(BF16)
            dcv_sum[h, cols, :] += nt(p.astype(BF16), dctx)
            dck_sum[h, cols, :] += nt(ds, q)
            dq_sum[band, :] += nn(ckt_ref[band, cols], ds)
        return carry

    lax.fori_loop(low, block + 1, step, 0)
    mask = mask_ref[0, 0:1, :]
    rows = key_rows(block)
    for h in range(heads):
        band = slice(h * hd, (h + 1) * hd)
        one = slice(h, h + 1)
        q, k = q_ref[band, :].astype(F32), k_ref[band, :].astype(F32)
        v, dctx = v_ref[band, :].astype(F32), dctx_ref[band, :].astype(F32)
        own_prob = jnp.exp2(jnp.sum(q * k, axis=0, keepdims=True) * scale - lse_ref[one, :])
        own_dprob = jnp.sum(dctx * v, axis=0, keepdims=True)
        own_dscore = own_prob * (own_dprob - delta_ref[one, :]) * factor
        dqkv[band, :] = (dq_sum[band, :] * factor + own_dscore * k).astype(BF16)
        dck = (dck_sum[h, rows, :] * factor).astype(BF16)
        dcv = dcv_sum[h, rows, :].astype(BF16)
        for at, src, conv, total, grad, beside in (
            (width, k_ref, kconv_ref, kconv_sum, dck, own_dscore * q),
            (2 * width, v_ref, vconv_ref, vconv_sum, dcv, own_prob * dctx),
        ):
            spread = nt(conv[h], grad)
            spread = jnp.concatenate([spread[r * hd : (r + 1) * hd] for r in range(3)], axis=1)
            dqkv[at + h * hd : at + (h + 1) * hd, :] = ((spread + beside) * mask).astype(BF16)
            if h < own_heads:
                taps = jnp.concatenate([src[band, r * GB : (r + 1) * GB] for r in range(3)], axis=0)
                total[h] += nn(taps, grad)
    x = tap_major(xs, x_ref[...].astype(F32))
    hat, inv_std = norm_rows(x)
    gain = gain_ref[...]
    first_in = (hat * gain).astype(BF16)
    for part in range(3):
        weight_sum[part * own : (part + 1) * own, :] += nn(dqkv[part * width : part * width + own, :], first_in)
    back = tn(dqkv[...], w_ref[...])
    gain_sum[...] += jnp.sum(back * hat, axis=0, keepdims=True)
    total = resid_grad_ref[...].astype(F32) + norm_back(back, gain, hat, inv_std)
    tokens_ref[...] = token_major(xs, total).astype(BF16)

    @pl.when(block == 0)
    def _():
        grads_ref[:, 0 : 3 * own] = weight_sum[...].T.astype(BF16)
        grads_ref[:, 3 * own :] = jnp.broadcast_to(gain_sum[...], (GB, gain.shape[1])).T.astype(BF16)
        for h in range(own_heads):
            conv_ref[:, h * hd : (h + 1) * hd] = kconv_sum[h].astype(BF16)
            conv_ref[:, (own_heads + h) * hd : (own_heads + h + 1) * hd] = vconv_sum[h].astype(BF16)


def whole(shape):
    return pl.BlockSpec(shape, lambda *_: (0,) * len(shape))


def params():
    return pltpu.CompilerParams(vmem_limit_bytes=VMEM, dimension_semantics=("arbitrary",))


def gathered(shard):
    half = shard.shape[0] // 2
    core = lax.rem(lax.axis_index("dp"), 2)
    peers = lax.axis_size("tensor")
    pairs = [(i, i ^ 1) for i in range(lax.axis_size("dp"))]
    mine = lax.dynamic_slice_in_dim(shard, core * half, half, 0)
    got = jnp.stack(
        [lax.ppermute(mine, "tensor", [(i, i ^ s) for i in range(peers)]) for s in range(1, peers)]
    )
    other = lax.ppermute(got, "dp", pairs)
    both = jnp.where(
        core == 0, jnp.concatenate([got, other], axis=1), jnp.concatenate([other, got], axis=1)
    )
    return jnp.concatenate([shard[None], both], axis=0)


def sent_and_summed(array):
    count = lax.axis_size("dp")
    parts = array.reshape(count, array.shape[0] // count, *array.shape[1:])
    parts = lax.all_to_all(parts, "dp", 0, 0, tiled=True)
    return jnp.sum(parts.astype(F32), axis=0)


def on_device(
    tokens, first_gain, second_gain, query_weight, key_weight, value_weight, out_weight,
    key_conv, value_conv, up_weight, down_weight, pad_mask, item_lengths, cotangent,
):
    rows, dim = tokens.shape
    blocks = rows // TB
    groups = rows // 3
    own_heads, taps, hd = key_conv.shape
    peers = lax.axis_size("tensor")
    heads = own_heads * peers
    width = heads * hd
    own = own_heads * hd
    units = up_weight.shape[1]
    lens = item_lengths[0]
    mask = pad_mask.reshape(blocks, GB, 3).transpose(0, 2, 1).reshape(blocks, 1, TB).astype(F32)
    gain1, gain2 = first_gain[None], second_gain[None]

    proj = jnp.concatenate([query_weight.T, key_weight.T, value_weight.T], axis=0)
    convs = jnp.concatenate(
        [
            key_conv.transpose(0, 2, 1).reshape(own, taps),
            value_conv.transpose(0, 2, 1).reshape(own, taps),
        ],
        axis=1,
    )
    proj_all = gathered(proj)
    convs_all = gathered(convs)
    w_all = proj_all.reshape(peers, 3, own, dim).transpose(1, 0, 2, 3).reshape(3 * width, dim)
    kconv_t = convs_all[:, :, :taps].reshape(heads, hd, taps)
    vconv_t = convs_all[:, :, taps:].reshape(heads, hd, taps)
    kconv, vconv = kconv_t.transpose(0, 2, 1), vconv_t.transpose(0, 2, 1)
    out_all = gathered(out_weight).reshape(width, dim)
    up_all = gathered(up_weight)
    down_all = gathered(down_weight)

    rows_spec = pl.BlockSpec((TB, dim), lambda b, *_: (b, 0))
    cols_spec = pl.BlockSpec((width, TB), lambda b, *_: (0, b))
    stat_spec = pl.BlockSpec((heads, TB), lambda b, *_: (0, b))
    mask_spec = pl.BlockSpec((1, 1, TB), lambda b, *_: (b, 0, 0))
    q, k, v, ctx, lse, ck, ckt, cv = pl.pallas_call(
        functools.partial(forward_kernel, heads, hd),
        grid_spec=pltpu.PrefetchScalarGridSpec(
            num_scalar_prefetch=1,
            grid=(blocks,),
            in_specs=[
                rows_spec, whole((1, dim)), whole((3 * width, dim)), whole((heads, hd, taps)),
                whole((heads, hd, taps)), mask_spec,
            ],
            out_specs=[
                cols_spec, cols_spec, cols_spec, cols_spec, stat_spec,
                whole((heads, groups, hd)), whole((width, groups)), whole((heads, groups, hd)),
            ],
            scratch_shapes=[
                pltpu.VMEM((dim // 128, TB, 128), F32), pltpu.VMEM((width, groups), BF16), pltpu.VMEM((heads, TB), F32),
                pltpu.VMEM((heads, TB), F32), pltpu.VMEM((width, TB), F32),
            ],
        ),
        out_shape=[jax.ShapeDtypeStruct((width, rows), BF16)] * 4
        + [
            jax.ShapeDtypeStruct((heads, rows), F32),
            jax.ShapeDtypeStruct((heads, groups, hd), BF16),
            jax.ShapeDtypeStruct((width, groups), BF16),
            jax.ShapeDtypeStruct((heads, groups, hd), BF16),
        ],
        compiler_params=params(),
        name="attention_forward",
    )(lens, tokens, gain1, w_all, kconv_t, vconv_t, mask)

    mixed, resid_grad, dctx, delta, middle_grads = pl.pallas_call(
        functools.partial(middle_kernel, heads, hd),
        grid=(blocks,),
        in_specs=[
            rows_spec, rows_spec, whole((1, dim)), cols_spec, whole((width, dim)),
            whole((peers, dim, units)), whole((peers, units, dim)),
        ],
        out_specs=[rows_spec, rows_spec, cols_spec, stat_spec, whole((dim, 2 * units + own + GB))],
        out_shape=[
            jax.ShapeDtypeStruct((rows, dim), BF16),
            jax.ShapeDtypeStruct((rows, dim), BF16),
            jax.ShapeDtypeStruct((width, rows), BF16),
            jax.ShapeDtypeStruct((heads, rows), F32),
            jax.ShapeDtypeStruct((dim, 2 * units + own + GB), BF16),
        ],
        scratch_shapes=[
            pltpu.VMEM((dim // 128, TB, 128), F32), pltpu.VMEM((units, dim), F32), pltpu.VMEM((dim, units), F32),
            pltpu.VMEM((own, dim), F32), pltpu.VMEM((1, dim), F32),
        ],
        compiler_params=params(),
        name="feed_forward",
    )(tokens, cotangent, gain2, ctx, out_all, up_all, down_all)
    middle_share = sent_and_summed(middle_grads)

    back_rows = pl.BlockSpec((TB, dim), lambda b, *_: (blocks - 1 - b, 0))
    back_cols = pl.BlockSpec((width, TB), lambda b, *_: (0, blocks - 1 - b))
    back_stat = pl.BlockSpec((heads, TB), lambda b, *_: (0, blocks - 1 - b))
    back_mask = pl.BlockSpec((1, 1, TB), lambda b, *_: (blocks - 1 - b, 0, 0))
    grad_tokens, last_grads, conv_grads = pl.pallas_call(
        functools.partial(backward_kernel, heads, hd, own_heads),
        grid_spec=pltpu.PrefetchScalarGridSpec(
            num_scalar_prefetch=1,
            grid=(blocks,),
            in_specs=[
                back_rows, whole((1, dim)), whole((3 * width, dim)), whole((heads, taps, hd)),
                whole((heads, taps, hd)), back_mask, back_cols, back_cols, back_cols, back_stat,
                back_cols, back_stat, back_rows, whole((heads, groups, hd)), whole((width, groups)),
                whole((heads, groups, hd)),
            ],
            out_specs=[back_rows, whole((dim, 3 * own + GB)), whole((taps, 2 * own))],
            scratch_shapes=[
                pltpu.VMEM((dim // 128, TB, 128), F32), pltpu.VMEM((heads, groups, hd), F32),
                pltpu.VMEM((heads, groups, hd), F32), pltpu.VMEM((width, TB), F32),
                pltpu.VMEM((3 * width, TB), BF16), pltpu.VMEM((3 * own, dim), F32),
                pltpu.VMEM((own_heads, taps, hd), F32), pltpu.VMEM((own_heads, taps, hd), F32),
                pltpu.VMEM((1, dim), F32),
            ],
        ),
        out_shape=[
            jax.ShapeDtypeStruct((rows, dim), BF16),
            jax.ShapeDtypeStruct((dim, 3 * own + GB), BF16),
            jax.ShapeDtypeStruct((taps, 2 * own), BF16),
        ],
        compiler_params=params(),
        name="attention_backward",
    )(lens, tokens, gain1, w_all, kconv, vconv, mask, q, k, v, lse, dctx, delta, resid_grad, ck, ckt, cv)
    last_share = sent_and_summed(last_grads)
    conv_share = sent_and_summed(conv_grads)
    conv_share = conv_share.reshape(-1, 2, own_heads, hd).transpose(1, 2, 0, 3)

    return (
        mixed,
        grad_tokens,
        last_share[:, 3 * own],
        middle_share[:, 2 * units + own],
        last_share[:, :own],
        last_share[:, own : 2 * own],
        last_share[:, 2 * own : 3 * own],
        middle_share[:, 2 * units : 2 * units + own].T,
        conv_share[0],
        conv_share[1],
        middle_share[:, :units],
        middle_share[:, units : 2 * units].T,
    )


def solution(mesh):
    in_specs = (
        P("dp", None),
        P(),
        P(),
        P(None, "tensor"),
        P(None, "tensor"),
        P(None, "tensor"),
        P("tensor", None),
        P("tensor", None, None),
        P("tensor", None, None),
        P(None, "tensor"),
        P("tensor", None),
        P("dp"),
        P("dp", None),
        P("dp", None),
    )
    out_specs = (
        P("dp", None),
        P("dp", None),
        P("dp"),
        P("dp"),
        P("dp", "tensor"),
        P("dp", "tensor"),
        P("dp", "tensor"),
        P("tensor", "dp"),
        P("tensor", "dp", None),
        P("tensor", "dp", None),
        P("dp", "tensor"),
        P("tensor", "dp"),
    )
    return jax.shard_map(
        on_device, mesh=mesh, in_specs=in_specs, out_specs=out_specs, check_vma=False
    )
```

```python
import functools
import math

import jax
import jax.numpy as jnp
from jax import lax
from jax.experimental import pallas as pl
from jax.experimental.pallas import tpu as pltpu
from jax.sharding import PartitionSpec as P

F32 = jnp.float32
BF16 = jnp.bfloat16
GB = 128
TB = 3 * GB
NEG = -1e30
LOG2E = 1.0 / math.log(2.0)
VMEM = 60 * 1024 * 1024

ERF_P = 0.43
ERF_C = (
    0.24255178053871013,
    0.24376598744271377,
    0.2089868288055898,
    0.23281685899157548,
    -0.05797941172752005,
    0.3523368029188165,
    -0.2915198548110903,
    0.06904073943922798,
)


def nn(a, b):
    return lax.dot_general(a, b, (((1,), (0,)), ((), ())), preferred_element_type=F32)


def nt(a, b):
    return lax.dot_general(a, b, (((1,), (1,)), ((), ())), preferred_element_type=F32)


def tn(a, b):
    return lax.dot_general(a, b, (((0,), (0,)), ((), ())), preferred_element_type=F32)


def norm_rows(values):
    centred = values - jnp.mean(values, -1, keepdims=True)
    inv_std = lax.rsqrt(jnp.mean(centred * centred, -1, keepdims=True) + 1e-05)
    return centred * inv_std, inv_std


def norm_back(grad_out, gains, normed, inv_std):
    scaled = grad_out * gains
    return inv_std * (
        scaled
        - jnp.mean(scaled, -1, keepdims=True)
        - normed * jnp.mean(scaled * normed, -1, keepdims=True)
    )


def tap_major(scratch, values):
    lanes = scratch.shape[2]
    parts = []
    for c in range(scratch.shape[0]):
        scratch[c] = values[:, c * lanes : (c + 1) * lanes]
        taps = [scratch[c, pl.ds(r, GB, stride=3), :] for r in range(3)]
        parts.append(jnp.concatenate(taps, axis=0))
    return jnp.concatenate(parts, axis=1)


def token_major(scratch, values):
    lanes = scratch.shape[2]
    parts = []
    for c in range(scratch.shape[0]):
        for r in range(3):
            scratch[c, pl.ds(r, GB, stride=3), :] = values[
                r * GB : (r + 1) * GB, c * lanes : (c + 1) * lanes
            ]
        parts.append(scratch[c])
    return jnp.concatenate(parts, axis=1)


def gelu_and_slope(h):
    z = jnp.abs(h) * math.sqrt(0.5)
    t = 1.0 / (1.0 + ERF_P * z)
    poly = jnp.full_like(t, ERF_C[-1])
    for c in ERF_C[-2::-1]:
        poly = poly * t + c
    e = jnp.exp(-z * z)
    tail = (0.5 * e) * (poly * t)
    cdf = jnp.where(h >= 0, 1.0 - tail, tail)
    return h * cdf, cdf + h * (e * (1.0 / math.sqrt(2.0 * math.pi)))


def item_starts(lens_ref, block, longest_here, half):
    places = block * GB + lax.broadcasted_iota(jnp.int32, (1, GB), 1)
    starts = jnp.zeros((1, GB), jnp.int32)
    end = jnp.int32(0)
    for i in range(lens_ref.shape[0] - 1):
        end = end + jnp.where((lens_ref[i] == half) == longest_here, lens_ref[i], 0)
        starts = jnp.where(places >= end, end, starts)
    return places, starts


def longest_first(lens_ref, half):
    first, ahead = jnp.int32(0), jnp.int32(1)
    for i in range(lens_ref.shape[0]):
        ahead = jnp.where(lens_ref[i] == half, 0, ahead)
        first = first + ahead * lens_ref[i]
    return 3 * first


def own_taps(source, block, first, longest_here):
    half = source.shape[1] // 2
    base = block * TB
    parts = []
    for c in range(source.shape[0]):
        for r in range(3):
            inside = source[c, pl.ds(first + base + r, GB, stride=3), :]
            low = source[c, pl.ds(base + r, GB, stride=3), :]
            high = source[c, pl.ds(half + base + r, GB, stride=3), :]
            place = base + r + 3 * lax.broadcasted_iota(jnp.int32, (GB, 1), 0)
            parts.append(jnp.where(longest_here, inside, jnp.where(place < first, low, high)))
    return jnp.concatenate(
        [jnp.concatenate(parts[3 * c : 3 * c + 3], axis=0) for c in range(source.shape[0])], axis=1
    )


def mask_bias(places, starts, kb):
    keys = kb * GB + lax.broadcasted_iota(jnp.int32, (GB, GB), 0)
    bias = jnp.where((keys >= starts) & (keys < places), 0.0, NEG)
    return jnp.concatenate([bias] * 3, axis=1)


def key_rows(kb):
    return pl.ds(pl.multiple_of(kb * GB, GB), GB)


def remote(src, dst, sems, at, device):
    return pltpu.make_async_remote_copy(
        src_ref=src, dst_ref=dst, send_sem=sems.at[(0, *at)], recv_sem=sems.at[(1, *at)],
        device_id=device, device_id_type=pl.DeviceIdType.MESH,
    )


class Gather:
    def __init__(self, arrays, sems):
        self.arrays, self.sems = arrays, sems
        self.dp, self.tensor = lax.axis_index("dp"), lax.axis_index("tensor")
        self.peers = lax.axis_size("tensor")

    def half(self, array, slot):
        rows = array.shape[1] // 2
        start = pl.multiple_of(lax.rem(self.dp, 2) * rows, rows)
        return array.at[slot, pl.ds(start, rows)]

    def across(self, n, s):
        array = self.arrays[n]
        return remote(
            self.half(array, 0), self.half(array, s), self.sems, (n, 0, s - 1), (self.dp, self.tensor ^ s)
        )

    def beside(self, n, s):
        half = self.half(self.arrays[n], s)
        return remote(half, half, self.sems, (n, 1, s - 1), (self.dp ^ 1, self.tensor))

    def each(self):
        return [(n, s) for s in range(self.peers - 1, 0, -1) for n in range(len(self.arrays))]

    def start(self):
        for n, s in self.each():
            self.across(n, s).start()

    def pass_on(self):
        for n, s in self.each():
            self.across(n, s).wait_recv()
            self.beside(n, s).start()

    def arrive(self):
        for n, s in self.each():
            self.beside(n, s).wait_recv()

    def finish(self):
        for n, s in self.each():
            self.across(n, s).wait_send()
            self.beside(n, s).wait_send()


def forward_kernel(
    heads, hd, lens_ref, x_ref, g_ref, gain_ref, mask_ref, query_ref, key_ref, value_ref, kconv_ref, vconv_ref,
    out_ref, up_ref, down_ref,
    x_own, g_own, q_ref, k_ref, v_ref, ctx_ref, lse_ref, ck_ref, ckt_ref, cv_ref, w_all, conv_all,
    out_all, up_all, down_all,
    xs, gs, w_ref, conv_ref, cvt_ref, m_ref, l_ref, acc_ref, first_sems, last_sems, local_sems,
):
    block = pl.program_id(0)
    blocks = pl.num_programs(0)
    own_heads = kconv_ref.shape[0]
    own = own_heads * hd
    taps = kconv_ref.shape[1]
    scale = LOG2E / math.sqrt(hd)
    me, peer = lax.axis_index("dp"), lax.axis_index("tensor")
    first_gather = Gather((w_ref, conv_ref), first_sems)
    last_gather = Gather((out_all, up_all, down_all), last_sems)
    keep_copies = [
        pltpu.make_async_copy(w_ref, w_all, local_sems.at[3]), pltpu.make_async_copy(conv_ref, conv_all, local_sems.at[4])
    ]

    @pl.when(block == 0)
    def _():
        barrier = pltpu.get_barrier_semaphore()
        others = [(me, peer ^ s) for s in range(1, lax.axis_size("tensor"))] + [(me ^ 1, peer)]
        for device in others:
            pl.semaphore_signal(barrier, inc=1, device_id=device, device_id_type=pl.DeviceIdType.MESH)
        for n, src in enumerate((query_ref, key_ref, value_ref)):
            w_ref[0, n * own : (n + 1) * own, :] = src[...].T
        for n, src in enumerate((kconv_ref, vconv_ref)):
            conv_ref[0, n * taps : (n + 1) * taps, :] = jnp.concatenate([src[h] for h in range(own_heads)], axis=1)
        pl.semaphore_wait(barrier, len(others))
        first_gather.start()
        own_copies = [
            pltpu.make_async_copy(src, dst.at[0], local_sems.at[n])
            for n, (src, dst) in enumerate(((out_ref, out_all), (up_ref, up_all), (down_ref, down_all)))
        ]
        for copy in own_copies:
            copy.start()
        for src, dst in ((x_ref, xs), (g_ref, gs)):
            for c in range(dst.shape[0]):
                dst[c] = src[:, c * 128 : (c + 1) * 128].astype(F32)
        for copy in own_copies:
            copy.wait()
        first_gather.pass_on()
        last_gather.start()
        first_gather.arrive()
        first_gather.finish()
        for copy in keep_copies:
            copy.start()

    half = x_ref.shape[0] // 2
    longest_here = lax.rem(peer, 2) == 0
    first = longest_first(lens_ref, half // 3)
    x = own_taps(xs, block, first, longest_here)
    x_own[...] = x.astype(BF16)
    g_own[...] = own_taps(gs, block, first, longest_here).astype(BF16)
    normed, _ = norm_rows(x)
    first_in = (normed * gain_ref[...]).astype(BF16)
    mask = mask_ref[0, 0:1, :]
    for slot in range(w_ref.shape[0]):
        at = slice(slot * own, (slot + 1) * own)
        part = nt(w_ref[slot], first_in)
        q_ref[at, :] = part[0:own].astype(BF16)
        k_ref[at, :] = (part[own : 2 * own] * mask).astype(BF16)
        v_ref[at, :] = (part[2 * own : 3 * own] * mask).astype(BF16)
    rows = key_rows(block)
    for h in range(heads):
        band = slice(h * hd, (h + 1) * hd)
        slot, i = divmod(h, own_heads)
        for n, src, plain, trans in ((0, k_ref, ck_ref, ckt_ref), (1, v_ref, cv_ref, cvt_ref)):
            grouped = jnp.concatenate([src[band, r * GB : (r + 1) * GB] for r in range(3)], axis=0)
            comp = tn(conv_ref[slot, n * taps : (n + 1) * taps, i * hd : (i + 1) * hd], grouped)
            trans[band, rows] = comp.astype(BF16)
            plain[h, rows, :] = comp.T.astype(BF16)
        q, k = q_ref[band, :].astype(F32), k_ref[band, :].astype(F32)
        m_ref[h : h + 1, :] = jnp.sum(q * k, axis=0, keepdims=True) * scale
        acc_ref[band, :] = v_ref[band, :].astype(F32)
    l_ref[...] = jnp.ones_like(l_ref)
    places, starts = item_starts(lens_ref, block, longest_here, half // 3)

    def step(kb, carry):
        bias = mask_bias(places, starts, kb)
        cols = key_rows(kb)
        for h in range(heads):
            band = slice(h * hd, (h + 1) * hd)
            one = slice(h, h + 1)
            s = nn(ck_ref[h, cols, :], q_ref[band, :]) * scale + bias
            old = m_ref[one, :]
            new = jnp.maximum(old, jnp.max(s, axis=0, keepdims=True))
            p = jnp.exp2(s - new)
            keep = jnp.exp2(old - new)
            m_ref[one, :] = new
            l_ref[one, :] = l_ref[one, :] * keep + jnp.sum(p, axis=0, keepdims=True)
            acc_ref[band, :] = acc_ref[band, :] * keep + nn(cvt_ref[band, cols], p.astype(BF16))
        return carry

    lax.fori_loop(0, block + 1, step, 0)
    lse_ref[...] = m_ref[...] + jnp.log(l_ref[...]) * LOG2E
    inv = 1.0 / l_ref[...]
    for h in range(heads):
        band = slice(h * hd, (h + 1) * hd)
        ctx_ref[band, :] = (acc_ref[band, :] * inv[h : h + 1, :]).astype(BF16)

    @pl.when(block == blocks - 2)
    def _():
        last_gather.pass_on()

    @pl.when(block == blocks - 1)
    def _():
        last_gather.arrive()
        last_gather.finish()
        for copy in keep_copies:
            copy.wait()


def middle_kernel(
    heads, hd, x_ref, g_ref, gain_ref, ctx_ref, out_ref, up_ref, down_ref,
    mixed_ref, resid_grad_ref, dctx_ref, delta_ref, grads_ref,
    xs, down_sum, up_sum, out_sum, gain_sum,
):
    block = pl.program_id(0)
    own = out_sum.shape[0]

    @pl.when(block == 0)
    def _():
        down_sum[...] = jnp.zeros_like(down_sum)
        up_sum[...] = jnp.zeros_like(up_sum)
        out_sum[...] = jnp.zeros_like(out_sum)
        gain_sum[...] = jnp.zeros_like(gain_sum)

    gain = gain_ref[...]
    x = x_ref[...].astype(F32)
    g_low = g_ref[...]
    g = g_low.astype(F32)
    resid = x + tn(ctx_ref[...], out_ref[...])
    hat, inv_std = norm_rows(resid)
    second_in = (hat * gain).astype(BF16)
    ffn = jnp.zeros_like(resid)
    back = jnp.zeros_like(resid)
    for c in range(up_ref.shape[0]):
        hidden = nn(second_in, up_ref[c])
        act_grad = nt(g_low, down_ref[c])
        act, slope = gelu_and_slope(hidden)
        act = act.astype(BF16)
        hidden_grad = (act_grad * slope).astype(BF16)
        ffn = ffn + nn(act, down_ref[c])
        back = back + nt(hidden_grad, up_ref[c])
        if c < down_sum.shape[0]:
            down_sum[c] += tn(act, g_low)
            up_sum[c] += tn(second_in, hidden_grad)
    mixed_ref[...] = token_major(xs, resid + ffn).astype(BF16)
    gain_sum[...] += jnp.sum(back * hat, axis=0, keepdims=True)
    resid_grad = g + norm_back(back, gain, hat, inv_std)
    attn_grad = resid_grad.astype(BF16)
    resid_grad_ref[...] = attn_grad
    out_sum[...] += nn(ctx_ref[0:own, :], attn_grad)
    dctx = nt(out_ref[...], attn_grad).astype(BF16)
    dctx_ref[...] = dctx
    dots = dctx.astype(F32) * ctx_ref[...].astype(F32)
    for h in range(heads):
        delta_ref[h : h + 1, :] = jnp.sum(dots[h * hd : (h + 1) * hd], axis=0, keepdims=True)

    @pl.when(block == pl.num_programs(0) - 1)
    def _():
        units = up_sum.shape[2]
        at = 0
        for c in range(up_sum.shape[0]):
            grads_ref[:, at : at + units] = up_sum[c].astype(BF16)
            grads_ref[:, at + units : at + 2 * units] = down_sum[c].T.astype(BF16)
            at += 2 * units
        grads_ref[:, at : at + own] = out_sum[...].T.astype(BF16)
        grads_ref[:, at + own :] = jnp.broadcast_to(gain_sum[...], (GB, gain.shape[1])).T.astype(BF16)


def backward_kernel(
    heads, hd, own_heads, lens_ref, x_ref, gain_ref, w_ref, conv_ref, mask_ref,
    q_ref, k_ref, v_ref, lse_ref, dctx_ref, delta_ref, resid_grad_ref, ck_ref, ckt_ref, cv_ref,
    tokens_ref, grads_ref, conv_grads_ref,
    xs, dck_sum, dcv_sum, dq_sum, dqkv, weight_sum, kconv_sum, vconv_sum, gain_sum,
):
    step_id = pl.program_id(0)
    block = pl.num_programs(0) - 1 - step_id
    own = own_heads * hd
    slots, _, dim = w_ref.shape
    taps = conv_ref.shape[1] // 2
    slot_heads = heads // slots
    lanes = slot_heads * hd
    factor = 1.0 / math.sqrt(hd)
    scale = LOG2E * factor

    @pl.when(step_id == 0)
    def _():
        dck_sum[...] = jnp.zeros_like(dck_sum)
        dcv_sum[...] = jnp.zeros_like(dcv_sum)
        weight_sum[...] = jnp.zeros_like(weight_sum)
        kconv_sum[...] = jnp.zeros_like(kconv_sum)
        vconv_sum[...] = jnp.zeros_like(vconv_sum)
        gain_sum[...] = jnp.zeros_like(gain_sum)

    dq_sum[...] = jnp.zeros_like(dq_sum)
    longest_here = lax.rem(lax.axis_index("tensor"), 2) == 0
    places, starts = item_starts(lens_ref, block, longest_here, ck_ref.shape[1])

    def step(kb, carry):
        bias = mask_bias(places, starts, kb)
        cols = key_rows(kb)
        for h in range(heads):
            band = slice(h * hd, (h + 1) * hd)
            one = slice(h, h + 1)
            q, dctx = q_ref[band, :], dctx_ref[band, :]
            s = nn(ck_ref[h, cols, :], q) * scale + bias
            p = jnp.exp2(s - lse_ref[one, :])
            dp = nn(cv_ref[h, cols, :], dctx)
            ds = (p * (dp - delta_ref[one, :])).astype(BF16)
            dcv_sum[h, cols, :] += nt(p.astype(BF16), dctx)
            dck_sum[h, cols, :] += nt(ds, q)
            dq_sum[band, :] += nn(ckt_ref[band, cols], ds)
        return carry

    lax.fori_loop(0, block + 1, step, 0)
    mask = mask_ref[0, 0:1, :]
    rows = key_rows(block)
    for h in range(heads):
        band = slice(h * hd, (h + 1) * hd)
        one = slice(h, h + 1)
        q, k = q_ref[band, :].astype(F32), k_ref[band, :].astype(F32)
        v, dctx = v_ref[band, :].astype(F32), dctx_ref[band, :].astype(F32)
        own_prob = jnp.exp2(jnp.sum(q * k, axis=0, keepdims=True) * scale - lse_ref[one, :])
        own_dprob = jnp.sum(dctx * v, axis=0, keepdims=True)
        own_dscore = own_prob * (own_dprob - delta_ref[one, :]) * factor
        slot, i = divmod(h, slot_heads)
        base = slot * 3 * lanes + i * hd
        dqkv[base : base + hd, :] = (dq_sum[band, :] * factor + own_dscore * k).astype(BF16)
        dck = (dck_sum[h, rows, :] * factor).astype(BF16)
        dcv = dcv_sum[h, rows, :].astype(BF16)
        for n, src, total, grad, beside in (
            (0, k_ref, kconv_sum, dck, own_dscore * q),
            (1, v_ref, vconv_sum, dcv, own_prob * dctx),
        ):
            spread = nt(conv_ref[slot, n * taps : (n + 1) * taps, i * hd : (i + 1) * hd], grad)
            spread = jnp.concatenate([spread[r * hd : (r + 1) * hd] for r in range(3)], axis=1)
            at = base + (n + 1) * lanes
            dqkv[at : at + hd, :] = ((spread + beside) * mask).astype(BF16)
            if h < own_heads:
                grouped = jnp.concatenate([src[band, r * GB : (r + 1) * GB] for r in range(3)], axis=0)
                total[h] += nn(grouped, grad)
    hat, inv_std = norm_rows(x_ref[...].astype(F32))
    gain = gain_ref[...]
    first_in = (hat * gain).astype(BF16)
    weight_sum[...] += nn(dqkv[0 : 3 * own, :], first_in)
    back = tn(dqkv[...], w_ref[...].reshape(slots * 3 * lanes, dim))
    gain_sum[...] += jnp.sum(back * hat, axis=0, keepdims=True)
    total = resid_grad_ref[...].astype(F32) + norm_back(back, gain, hat, inv_std)
    tokens_ref[...] = token_major(xs, total).astype(BF16)

    @pl.when(block == 0)
    def _():
        grads_ref[:, 0 : 3 * own] = weight_sum[...].T.astype(BF16)
        grads_ref[:, 3 * own :] = jnp.broadcast_to(gain_sum[...], (GB, dim)).T.astype(BF16)
        for h in range(own_heads):
            conv_grads_ref[:, h * hd : (h + 1) * hd] = kconv_sum[h].astype(BF16)
            conv_grads_ref[:, (own_heads + h) * hd : (own_heads + h + 1) * hd] = vconv_sum[h].astype(BF16)


def whole(shape):
    return pl.BlockSpec(shape, lambda *_: (0,) * len(shape))


def cost(micros):
    return pl.CostEstimate(flops=int(micros * 1e9), bytes_accessed=1 << 20, transcendentals=0)


def params():
    return pltpu.CompilerParams(vmem_limit_bytes=VMEM, dimension_semantics=("arbitrary",))


def sent_and_summed(array):
    count = lax.axis_size("dp")
    parts = array.reshape(count, array.shape[0] // count, *array.shape[1:])
    parts = lax.all_to_all(parts, "dp", 0, 0, tiled=True)
    return jnp.sum(parts.astype(F32), axis=0)


def halves(lengths, rows):
    longest = jnp.argmax(lengths)
    before = jnp.arange(lengths.shape[0]) < longest
    first = 3 * jnp.sum(jnp.where(before, lengths, 0))
    return longest, first, jnp.arange(rows // 2, dtype=jnp.int32)


def own_rows(array, place, first, longest_here):
    half = place.shape[0]
    inside = lax.dynamic_slice_in_dim(array, first, half, 0)
    others = jnp.where(place < first, array[:half], array[half:])
    return jnp.where(longest_here, inside, others)


def all_rows(own, place, first, longest_here):
    half = place.shape[0]
    place = place[:, None]
    theirs = lax.ppermute(own, "tensor", neighbours("tensor"))
    inside = jnp.where(longest_here, own, theirs)
    others = jnp.where(longest_here, theirs, own)
    turned = lax.dynamic_slice_in_dim(jnp.concatenate([inside, inside]), half - first, half, 0)
    return jnp.concatenate(
        [jnp.where(place < first, others, turned), jnp.where(place < first, turned, others)]
    )


def neighbours(axis):
    return [(i, i ^ 1) for i in range(lax.axis_size(axis))]


def on_device(
    tokens, first_gain, second_gain, query_weight, key_weight, value_weight, out_weight,
    key_conv, value_conv, up_weight, down_weight, pad_mask, item_lengths, cotangent,
):
    dim = tokens.shape[1]
    own_heads, taps, hd = key_conv.shape
    peers = lax.axis_size("tensor")
    heads = own_heads * peers
    width = heads * hd
    own = own_heads * hd
    units = up_weight.shape[1]
    longest_here = lax.rem(lax.axis_index("tensor"), 2) == 0
    longest, first, place = halves(item_lengths[0], tokens.shape[0])
    lens = item_lengths[0]
    pack = (place, first, longest_here)
    rows = tokens.shape[0] // 2
    blocks = rows // TB
    groups = rows // 3
    mask = own_rows(pad_mask, *pack)
    mask = mask.reshape(blocks, GB, 3).transpose(0, 2, 1).reshape(blocks, 1, TB).astype(F32)
    gain1, gain2 = first_gain[None], second_gain[None]

    rows_spec = pl.BlockSpec((TB, dim), lambda b, *_: (b, 0))
    cols_spec = pl.BlockSpec((width, TB), lambda b, *_: (0, b))
    stat_spec = pl.BlockSpec((heads, TB), lambda b, *_: (0, b))
    mask_spec = pl.BlockSpec((1, 1, TB), lambda b, *_: (b, 0, 0))
    anywhere = pl.BlockSpec(memory_space=pl.ANY)
    inside = pl.BlockSpec(memory_space=pltpu.VMEM)
    x, g, q, k, v, ctx, lse, ck, ckt, cv, w_all, conv_all, out_all, up_all, down_all = pl.pallas_call(
        functools.partial(forward_kernel, heads, hd),
        grid_spec=pltpu.PrefetchScalarGridSpec(
            num_scalar_prefetch=1,
            grid=(blocks,),
            in_specs=[inside, inside, whole((1, dim)), mask_spec] + [inside] * 5 + [anywhere] * 3,
            out_specs=[
                rows_spec, rows_spec, cols_spec, cols_spec, cols_spec, cols_spec, stat_spec,
                whole((heads, groups, hd)), whole((width, groups)), whole((heads, groups, hd)),
                anywhere, anywhere, anywhere, anywhere, anywhere,
            ],
            scratch_shapes=[
                pltpu.VMEM((dim // 128, 2 * rows, 128), F32), pltpu.VMEM((dim // 128, 2 * rows, 128), F32),
                pltpu.VMEM((peers, 3 * own, dim), BF16), pltpu.VMEM((peers, 2 * taps, own), BF16),
                pltpu.VMEM((width, groups), BF16),
                pltpu.VMEM((heads, TB), F32), pltpu.VMEM((heads, TB), F32), pltpu.VMEM((width, TB), F32),
                pltpu.SemaphoreType.DMA((2, 2, 2, peers - 1)), pltpu.SemaphoreType.DMA((2, 3, 2, peers - 1)),
                pltpu.SemaphoreType.DMA((5,)),
            ],
        ),
        out_shape=[jax.ShapeDtypeStruct((rows, dim), BF16)] * 2
        + [jax.ShapeDtypeStruct((width, rows), BF16)] * 4
        + [
            jax.ShapeDtypeStruct((heads, rows), F32),
            jax.ShapeDtypeStruct((heads, groups, hd), BF16),
            jax.ShapeDtypeStruct((width, groups), BF16),
            jax.ShapeDtypeStruct((heads, groups, hd), BF16),
            jax.ShapeDtypeStruct((peers, 3 * own, dim), BF16),
            jax.ShapeDtypeStruct((peers, 2 * taps, own), BF16),
            jax.ShapeDtypeStruct((peers, own, dim), BF16),
            jax.ShapeDtypeStruct((peers, dim, units), BF16),
            jax.ShapeDtypeStruct((peers, units, dim), BF16),
        ],
        compiler_params=pltpu.CompilerParams(
            vmem_limit_bytes=VMEM, dimension_semantics=("arbitrary",), collective_id=0, has_side_effects=True
        ),
        cost_estimate=cost(55),
        name="attention_forward",
    )(
        lens, tokens, cotangent, gain1, mask, query_weight, key_weight, value_weight, key_conv, value_conv,
        out_weight, up_weight, down_weight,
    )

    mid_cols = 4 * units + 2 * own + GB
    mixed, resid_grad, dctx, delta, middle_grads = pl.pallas_call(
        functools.partial(middle_kernel, heads, hd),
        grid=(blocks,),
        in_specs=[
            rows_spec, rows_spec, whole((1, dim)), cols_spec, whole((width, dim)),
            whole((peers, dim, units)), whole((peers, units, dim)),
        ],
        out_specs=[rows_spec, rows_spec, cols_spec, stat_spec, whole((dim, mid_cols))],
        out_shape=[
            jax.ShapeDtypeStruct((rows, dim), BF16),
            jax.ShapeDtypeStruct((rows, dim), BF16),
            jax.ShapeDtypeStruct((width, rows), BF16),
            jax.ShapeDtypeStruct((heads, rows), F32),
            jax.ShapeDtypeStruct((dim, mid_cols), BF16),
        ],
        scratch_shapes=[
            pltpu.VMEM((dim // 128, TB, 128), F32), pltpu.VMEM((2, units, dim), F32),
            pltpu.VMEM((2, dim, units), F32), pltpu.VMEM((2 * own, dim), F32), pltpu.VMEM((1, dim), F32),
        ],
        compiler_params=params(),
        cost_estimate=cost(55),
        name="feed_forward",
    )(x, g, gain2, ctx, out_all.reshape(width, dim), up_all, down_all)
    mixed_out = all_rows(mixed, *pack)
    middle_share = sent_and_summed(middle_grads)

    back_rows = pl.BlockSpec((TB, dim), lambda b, *_: (blocks - 1 - b, 0))
    back_cols = pl.BlockSpec((width, TB), lambda b, *_: (0, blocks - 1 - b))
    back_stat = pl.BlockSpec((heads, TB), lambda b, *_: (0, blocks - 1 - b))
    back_mask = pl.BlockSpec((1, 1, TB), lambda b, *_: (blocks - 1 - b, 0, 0))
    two = 2 * own_heads
    grad_rows, last_grads, conv_grads = pl.pallas_call(
        functools.partial(backward_kernel, heads, hd, two),
        grid_spec=pltpu.PrefetchScalarGridSpec(
            num_scalar_prefetch=1,
            grid=(blocks,),
            in_specs=[
                back_rows, whole((1, dim)), whole((peers, 3 * own, dim)), whole((peers, 2 * taps, own)), back_mask, back_cols, back_cols, back_cols, back_stat,
                back_cols, back_stat, back_rows, whole((heads, groups, hd)), whole((width, groups)),
                whole((heads, groups, hd)),
            ],
            out_specs=[back_rows, whole((dim, 6 * own + GB)), whole((taps, 4 * own))],
            scratch_shapes=[
                pltpu.VMEM((dim // 128, TB, 128), F32), pltpu.VMEM((heads, groups, hd), F32),
                pltpu.VMEM((heads, groups, hd), F32), pltpu.VMEM((width, TB), F32),
                pltpu.VMEM((3 * width, TB), BF16), pltpu.VMEM((6 * own, dim), F32),
                pltpu.VMEM((two, taps, hd), F32), pltpu.VMEM((two, taps, hd), F32),
                pltpu.VMEM((1, dim), F32),
            ],
        ),
        out_shape=[
            jax.ShapeDtypeStruct((rows, dim), BF16),
            jax.ShapeDtypeStruct((dim, 6 * own + GB), BF16),
            jax.ShapeDtypeStruct((taps, 4 * own), BF16),
        ],
        compiler_params=params(),
        cost_estimate=cost(60),
        name="attention_backward",
    )(lens, x, gain1, w_all, conv_all, mask, q, k, v, lse, dctx, delta, resid_grad, ck, ckt, cv)
    grad_tokens = all_rows(grad_rows, *pack)
    last_share = sent_and_summed(last_grads)
    conv_share = sent_and_summed(conv_grads).reshape(-1, 2, 2, own)

    def parts(slot):
        half = 2 * units
        return (
            middle_share[:, slot * half : slot * half + half],
            middle_share[:, 2 * half + slot * own : 2 * half + slot * own + own],
            middle_share[:, 2 * half + 2 * own],
            *(last_share[:, (3 * slot + n) * own : (3 * slot + n + 1) * own] for n in range(3)),
            last_share[:, 6 * own],
            conv_share[:, :, slot],
        )

    shapes = [p.shape for p in parts(1)]
    sizes = [math.prod(d) for d in shapes]
    ends = [sum(sizes[: n + 1]) for n in range(len(sizes))]
    theirs = lax.ppermute(
        jnp.concatenate([p.reshape(-1) for p in parts(1)]).astype(BF16), "tensor", neighbours("tensor")
    ).astype(F32)
    ff, out, gain2_grad, query, key, value, gain1_grad, conv = (
        p + t.reshape(d) for p, t, d in zip(parts(0), jnp.split(theirs, ends[:-1]), shapes)
    )
    conv = conv.reshape(-1, 2, own_heads, hd).transpose(1, 2, 0, 3)
    return (
        mixed_out,
        grad_tokens,
        gain1_grad,
        gain2_grad,
        query,
        key,
        value,
        out.T,
        conv[0],
        conv[1],
        ff[:, :units],
        ff[:, units:].T,
    )


def solution(mesh):
    in_specs = (
        P("dp", None),
        P(),
        P(),
        P(None, "tensor"),
        P(None, "tensor"),
        P(None, "tensor"),
        P("tensor", None),
        P("tensor", None, None),
        P("tensor", None, None),
        P(None, "tensor"),
        P("tensor", None),
        P("dp"),
        P("dp", None),
        P("dp", None),
    )
    out_specs = (
        P("dp", None),
        P("dp", None),
        P("dp"),
        P("dp"),
        P("dp", "tensor"),
        P("dp", "tensor"),
        P("dp", "tensor"),
        P("tensor", "dp"),
        P("tensor", "dp", None),
        P("tensor", "dp", None),
        P("dp", "tensor"),
        P("tensor", "dp"),
    )
    return jax.shard_map(
        on_device, mesh=mesh, in_specs=in_specs, out_specs=out_specs, check_vma=False
    )
```

```python
import functools
import math

import jax
import jax.numpy as jnp
from jax import lax
from jax.experimental import pallas as pl
from jax.experimental.pallas import tpu as pltpu
from jax.sharding import PartitionSpec as P

F32 = jnp.float32
BF16 = jnp.bfloat16
GB = 128
TB = 3 * GB
NEG = -1e30
LOG2E = 1.0 / math.log(2.0)
VMEM = 60 * 1024 * 1024

ERF_P = 0.43
ERF_C = (
    0.24255178053871013,
    0.24376598744271377,
    0.2089868288055898,
    0.23281685899157548,
    -0.05797941172752005,
    0.3523368029188165,
    -0.2915198548110903,
    0.06904073943922798,
)


def nn(a, b):
    return lax.dot_general(a, b, (((1,), (0,)), ((), ())), preferred_element_type=F32)


def nt(a, b):
    return lax.dot_general(a, b, (((1,), (1,)), ((), ())), preferred_element_type=F32)


def tn(a, b):
    return lax.dot_general(a, b, (((0,), (0,)), ((), ())), preferred_element_type=F32)


def norm_rows(values):
    centred = values - jnp.mean(values, -1, keepdims=True)
    inv_std = lax.rsqrt(jnp.mean(centred * centred, -1, keepdims=True) + 1e-05)
    return centred * inv_std, inv_std


def norm_back(grad_out, gains, normed, inv_std):
    scaled = grad_out * gains
    return inv_std * (
        scaled
        - jnp.mean(scaled, -1, keepdims=True)
        - normed * jnp.mean(scaled * normed, -1, keepdims=True)
    )


def tap_major(scratch, values):
    lanes = scratch.shape[2]
    parts = []
    for c in range(scratch.shape[0]):
        scratch[c] = values[:, c * lanes : (c + 1) * lanes]
        taps = [scratch[c, pl.ds(r, GB, stride=3), :] for r in range(3)]
        parts.append(jnp.concatenate(taps, axis=0))
    return jnp.concatenate(parts, axis=1)


def token_major(scratch, values):
    lanes = scratch.shape[2]
    parts = []
    for c in range(scratch.shape[0]):
        for r in range(3):
            scratch[c, pl.ds(r, GB, stride=3), :] = values[
                r * GB : (r + 1) * GB, c * lanes : (c + 1) * lanes
            ]
        parts.append(scratch[c])
    return jnp.concatenate(parts, axis=1)


def gelu_and_slope(h):
    z = jnp.abs(h) * math.sqrt(0.5)
    t = 1.0 / (1.0 + ERF_P * z)
    poly = jnp.full_like(t, ERF_C[-1])
    for c in ERF_C[-2::-1]:
        poly = poly * t + c
    e = jnp.exp(-z * z)
    tail = (0.5 * e) * (poly * t)
    cdf = jnp.where(h >= 0, 1.0 - tail, tail)
    return h * cdf, cdf + h * (e * (1.0 / math.sqrt(2.0 * math.pi)))


def item_starts(lens_ref, block, longest_here, half):
    places = block * GB + lax.broadcasted_iota(jnp.int32, (1, GB), 1)
    starts = jnp.zeros((1, GB), jnp.int32)
    end = jnp.int32(0)
    for i in range(lens_ref.shape[0] - 1):
        end = end + jnp.where((lens_ref[i] == half) == longest_here, lens_ref[i], 0)
        starts = jnp.where(places >= end, end, starts)
    return places, starts


def longest_first(lens_ref, half):
    first, ahead = jnp.int32(0), jnp.int32(1)
    for i in range(lens_ref.shape[0]):
        ahead = jnp.where(lens_ref[i] == half, 0, ahead)
        first = first + ahead * lens_ref[i]
    return 3 * first


def own_taps(source, block, first, longest_here):
    half = source.shape[1] // 2
    base = block * TB
    parts = []
    for c in range(source.shape[0]):
        for r in range(3):
            inside = source[c, pl.ds(first + base + r, GB, stride=3), :]
            low = source[c, pl.ds(base + r, GB, stride=3), :]
            high = source[c, pl.ds(half + base + r, GB, stride=3), :]
            place = base + r + 3 * lax.broadcasted_iota(jnp.int32, (GB, 1), 0)
            parts.append(jnp.where(longest_here, inside, jnp.where(place < first, low, high)))
    return jnp.concatenate(
        [jnp.concatenate(parts[3 * c : 3 * c + 3], axis=0) for c in range(source.shape[0])], axis=1
    )


def mask_bias(places, starts, kb):
    keys = kb * GB + lax.broadcasted_iota(jnp.int32, (GB, GB), 0)
    bias = jnp.where((keys >= starts) & (keys < places), 0.0, NEG)
    return jnp.concatenate([bias] * 3, axis=1)


def key_rows(kb):
    return pl.ds(pl.multiple_of(kb * GB, GB), GB)


def remote(src, dst, sems, at, device):
    return pltpu.make_async_remote_copy(
        src_ref=src, dst_ref=dst, send_sem=sems.at[(0, *at)], recv_sem=sems.at[(1, *at)],
        device_id=device, device_id_type=pl.DeviceIdType.MESH,
    )


def meet(devices):
    barrier = pltpu.get_barrier_semaphore()
    for device in devices:
        pl.semaphore_signal(barrier, inc=1, device_id=device, device_id_type=pl.DeviceIdType.MESH)
    pl.semaphore_wait(barrier, len(devices))


def put_rows(ref, pieces):
    count, rows, _ = ref.shape
    at = 0
    for piece in pieces:
        cols = piece.shape[1]
        for d in range(count):
            ref[d, :, at : at + cols] = piece[d * rows : (d + 1) * rows].astype(ref.dtype)
        at += cols


class Swap:
    def __init__(self, staged, mine, theirs, sems, local_sems):
        self.staged, self.mine, self.theirs, self.sems, self.local_sems = staged, mine, theirs, sems, local_sems
        self.device = (lax.axis_index("dp"), lax.axis_index("tensor") ^ 1)
        self.blocks = mine.shape[0] // TB

    def rows(self, block):
        return pl.ds(pl.multiple_of(block * TB, TB), TB)

    def local(self, step, block):
        staged = self.staged.at[lax.rem(step, 2)]
        return pltpu.make_async_copy(staged, self.mine.at[self.rows(block)], self.local_sems.at[step])

    def far(self, step, block):
        staged = self.staged.at[lax.rem(step, 2)]
        return remote(staged, self.theirs.at[self.rows(block)], self.sems, (step,), self.device)

    def settle(self, step, block):
        self.local(step, block).wait()
        self.far(step, block).wait_send()

    def send(self, step, block, values):
        @pl.when(step >= 2)
        def _():
            self.settle(step - 2, block)

        self.staged[lax.rem(step, 2)] = values
        self.local(step, block).start()
        self.far(step, block).start()

    def finish(self, block):
        for step in range(max(self.blocks - 2, 0), self.blocks):
            self.settle(step, block)
        for step in range(self.blocks):
            self.far(step, block).wait_recv()


class Spread:
    def __init__(self, source, landed, total, sems, local_sem):
        self.source, self.landed, self.sums, self.sems, self.local_sem = source, landed, total, sems, local_sem
        self.me, self.peer = lax.axis_index("dp"), lax.axis_index("tensor")
        self.count = lax.axis_size("dp")

    def copy(self, s):
        there = lax.rem(self.me + s, self.count)
        return remote(self.source.at[there], self.landed.at[s], self.sems, (s,), (there, self.peer))

    def own(self):
        return pltpu.make_async_copy(self.source.at[self.me], self.landed.at[0], self.local_sem)

    def start(self):
        self.own().start()

        def step(s, carry):
            self.copy(s).start()
            return carry

        lax.fori_loop(1, self.count, step, 0)

    def total(self):
        self.own().wait()

        def step(s, carry):
            self.copy(s).wait()
            return carry

        lax.fori_loop(1, self.count, step, 0)

        self.sums[...] = self.landed[0].astype(F32)

        def add(s, carry):
            self.sums[...] += self.landed[s].astype(F32)
            return carry

        lax.fori_loop(1, self.count, add, 0)
        return self.sums


class Gather:
    def __init__(self, arrays, sems):
        self.arrays, self.sems = arrays, sems
        self.dp, self.tensor = lax.axis_index("dp"), lax.axis_index("tensor")
        self.peers = lax.axis_size("tensor")

    def half(self, array, slot):
        rows = array.shape[1] // 2
        start = pl.multiple_of(lax.rem(self.dp, 2) * rows, rows)
        return array.at[slot, pl.ds(start, rows)]

    def across(self, n, s):
        array = self.arrays[n]
        return remote(
            self.half(array, 0), self.half(array, s), self.sems, (n, 0, s - 1), (self.dp, self.tensor ^ s)
        )

    def beside(self, n, s):
        half = self.half(self.arrays[n], s)
        return remote(half, half, self.sems, (n, 1, s - 1), (self.dp ^ 1, self.tensor))

    def each(self):
        return [(n, s) for s in range(self.peers - 1, 0, -1) for n in range(len(self.arrays))]

    def start(self):
        for n, s in self.each():
            self.across(n, s).start()

    def pass_on(self):
        for n, s in self.each():
            self.across(n, s).wait_recv()
            self.beside(n, s).start()

    def arrive(self):
        for n, s in self.each():
            self.beside(n, s).wait_recv()

    def finish(self):
        for n, s in self.each():
            self.across(n, s).wait_send()
            self.beside(n, s).wait_send()


def forward_kernel(
    heads, hd, lens_ref, x_ref, g_ref, gain_ref, mask_ref, query_ref, key_ref, value_ref, kconv_ref, vconv_ref,
    out_ref, up_ref, down_ref,
    x_own, g_own, q_ref, k_ref, v_ref, ctx_ref, lse_ref, ck_ref, ckt_ref, cv_ref, w_all, conv_all,
    out_all, up_all, down_all,
    xs, gs, w_ref, conv_ref, cvt_ref, m_ref, l_ref, acc_ref, first_sems, last_sems, local_sems,
):
    block = pl.program_id(0)
    blocks = pl.num_programs(0)
    own_heads = kconv_ref.shape[0]
    own = own_heads * hd
    taps = kconv_ref.shape[1]
    scale = LOG2E / math.sqrt(hd)
    me, peer = lax.axis_index("dp"), lax.axis_index("tensor")
    first_gather = Gather((w_ref, conv_ref), first_sems)
    last_gather = Gather((out_all, up_all, down_all), last_sems)
    keep_copies = [
        pltpu.make_async_copy(w_ref, w_all, local_sems.at[3]), pltpu.make_async_copy(conv_ref, conv_all, local_sems.at[4])
    ]

    @pl.when(block == 0)
    def _():
        barrier = pltpu.get_barrier_semaphore()
        others = [(me, peer ^ s) for s in range(1, lax.axis_size("tensor"))] + [(me ^ 1, peer)]
        for device in others:
            pl.semaphore_signal(barrier, inc=1, device_id=device, device_id_type=pl.DeviceIdType.MESH)
        for n, src in enumerate((query_ref, key_ref, value_ref)):
            w_ref[0, n * own : (n + 1) * own, :] = src[...].T
        for n, src in enumerate((kconv_ref, vconv_ref)):
            conv_ref[0, n * taps : (n + 1) * taps, :] = jnp.concatenate([src[h] for h in range(own_heads)], axis=1)
        pl.semaphore_wait(barrier, len(others))
        first_gather.start()
        own_copies = [
            pltpu.make_async_copy(src, dst.at[0], local_sems.at[n])
            for n, (src, dst) in enumerate(((out_ref, out_all), (up_ref, up_all), (down_ref, down_all)))
        ]
        for copy in own_copies:
            copy.start()
        for src, dst in ((x_ref, xs), (g_ref, gs)):
            for c in range(dst.shape[0]):
                dst[c] = src[:, c * 128 : (c + 1) * 128].astype(F32)
        for copy in own_copies:
            copy.wait()
        first_gather.pass_on()
        last_gather.start()
        first_gather.arrive()
        first_gather.finish()
        for copy in keep_copies:
            copy.start()

    half = x_ref.shape[0] // 2
    longest_here = lax.rem(peer, 2) == 0
    first = longest_first(lens_ref, half // 3)
    x = own_taps(xs, block, first, longest_here)
    x_own[...] = x.astype(BF16)
    g_own[...] = own_taps(gs, block, first, longest_here).astype(BF16)
    normed, _ = norm_rows(x)
    first_in = (normed * gain_ref[...]).astype(BF16)
    mask = mask_ref[0, 0:1, :]
    for slot in range(w_ref.shape[0]):
        at = slice(slot * own, (slot + 1) * own)
        part = nt(w_ref[slot], first_in)
        q_ref[at, :] = part[0:own].astype(BF16)
        k_ref[at, :] = (part[own : 2 * own] * mask).astype(BF16)
        v_ref[at, :] = (part[2 * own : 3 * own] * mask).astype(BF16)
    rows = key_rows(block)
    for h in range(heads):
        band = slice(h * hd, (h + 1) * hd)
        slot, i = divmod(h, own_heads)
        for n, src, plain, trans in ((0, k_ref, ck_ref, ckt_ref), (1, v_ref, cv_ref, cvt_ref)):
            grouped = jnp.concatenate([src[band, r * GB : (r + 1) * GB] for r in range(3)], axis=0)
            comp = tn(conv_ref[slot, n * taps : (n + 1) * taps, i * hd : (i + 1) * hd], grouped)
            trans[band, rows] = comp.astype(BF16)
            plain[h, rows, :] = comp.T.astype(BF16)
        q, k = q_ref[band, :].astype(F32), k_ref[band, :].astype(F32)
        m_ref[h : h + 1, :] = jnp.sum(q * k, axis=0, keepdims=True) * scale
        acc_ref[band, :] = v_ref[band, :].astype(F32)
    l_ref[...] = jnp.ones_like(l_ref)
    places, starts = item_starts(lens_ref, block, longest_here, half // 3)

    def step(kb, carry):
        bias = mask_bias(places, starts, kb)
        cols = key_rows(kb)
        for h in range(heads):
            band = slice(h * hd, (h + 1) * hd)
            one = slice(h, h + 1)
            s = nn(ck_ref[h, cols, :], q_ref[band, :]) * scale + bias
            old = m_ref[one, :]
            new = jnp.maximum(old, jnp.max(s, axis=0, keepdims=True))
            p = jnp.exp2(s - new)
            keep = jnp.exp2(old - new)
            m_ref[one, :] = new
            l_ref[one, :] = l_ref[one, :] * keep + jnp.sum(p, axis=0, keepdims=True)
            acc_ref[band, :] = acc_ref[band, :] * keep + nn(cvt_ref[band, cols], p.astype(BF16))
        return carry

    lax.fori_loop(0, block + 1, step, 0)
    lse_ref[...] = m_ref[...] + jnp.log(l_ref[...]) * LOG2E
    inv = 1.0 / l_ref[...]
    for h in range(heads):
        band = slice(h * hd, (h + 1) * hd)
        ctx_ref[band, :] = (acc_ref[band, :] * inv[h : h + 1, :]).astype(BF16)

    @pl.when(block == blocks - 2)
    def _():
        last_gather.pass_on()

    @pl.when(block == blocks - 1)
    def _():
        last_gather.arrive()
        last_gather.finish()
        for copy in keep_copies:
            copy.wait()


def middle_kernel(
    heads, hd, x_ref, g_ref, gain_ref, ctx_ref, out_ref, up_ref, down_ref,
    mixed_ref, mixed_peer, resid_grad_ref, dctx_ref, delta_ref, grads_ref,
    staged, down_sum, up_sum, out_sum, gain_sum, sems, local_sems,
):
    block = pl.program_id(0)
    own = out_sum.shape[0]
    swap = Swap(staged, mixed_ref, mixed_peer, sems, local_sems)

    @pl.when(block == 0)
    def _():
        meet([swap.device])
        down_sum[...] = jnp.zeros_like(down_sum)
        up_sum[...] = jnp.zeros_like(up_sum)
        out_sum[...] = jnp.zeros_like(out_sum)
        gain_sum[...] = jnp.zeros_like(gain_sum)

    gain = gain_ref[...]
    x = x_ref[...].astype(F32)
    g_low = g_ref[...]
    g = g_low.astype(F32)
    resid = x + tn(ctx_ref[...], out_ref[...])
    hat, inv_std = norm_rows(resid)
    second_in = (hat * gain).astype(BF16)
    ffn = jnp.zeros_like(resid)
    back = jnp.zeros_like(resid)
    for c in range(up_ref.shape[0]):
        hidden = nn(second_in, up_ref[c])
        act_grad = nt(g_low, down_ref[c])
        act, slope = gelu_and_slope(hidden)
        act = act.astype(BF16)
        hidden_grad = (act_grad * slope).astype(BF16)
        ffn = ffn + nn(act, down_ref[c])
        back = back + nt(hidden_grad, up_ref[c])
        if c < down_sum.shape[0]:
            down_sum[c] += tn(act, g_low)
            up_sum[c] += tn(second_in, hidden_grad)
    swap.send(block, block, (resid + ffn).astype(BF16))
    gain_sum[...] += jnp.sum(back * hat, axis=0, keepdims=True)
    resid_grad = g + norm_back(back, gain, hat, inv_std)
    attn_grad = resid_grad.astype(BF16)
    resid_grad_ref[...] = attn_grad
    out_sum[...] += nn(ctx_ref[0:own, :], attn_grad)
    dctx = nt(out_ref[...], attn_grad).astype(BF16)
    dctx_ref[...] = dctx
    dots = dctx.astype(F32) * ctx_ref[...].astype(F32)
    for h in range(heads):
        delta_ref[h : h + 1, :] = jnp.sum(dots[h * hd : (h + 1) * hd], axis=0, keepdims=True)

    @pl.when(block == pl.num_programs(0) - 1)
    def _():
        put_rows(
            grads_ref,
            [
                piece
                for c in range(up_sum.shape[0])
                for piece in (up_sum[c], down_sum[c].T, out_sum[c * own // 2 : (c + 1) * own // 2].T)
            ]
            + [jnp.broadcast_to(gain_sum[...], (GB, gain.shape[1])).T],
        )
        swap.finish(block)


def backward_kernel(
    heads, hd, own_heads, lens_ref, x_ref, gain_ref, w_ref, conv_ref, mask_ref,
    q_ref, k_ref, v_ref, lse_ref, dctx_ref, delta_ref, resid_grad_ref, ck_ref, ckt_ref, cv_ref, middle_ref,
    tokens_ref, tokens_peer, middle_out, last_out, conv_out,
    staged, dck_sum, dcv_sum, dq_sum, dqkv, weight_sum, kconv_sum, vconv_sum, gain_sum,
    middle_in, last_parts, last_in, conv_parts, conv_in,
    middle_turn, last_turn, conv_turn, middle_sum, last_sum, conv_sum,
    swap_sems, swap_local, middle_sems, last_sems, conv_sems, turn_sems, local_sems,
):
    step_id = pl.program_id(0)
    block = pl.num_programs(0) - 1 - step_id
    own = own_heads * hd
    slots, _, dim = w_ref.shape
    taps = conv_ref.shape[1] // 2
    slot_heads = heads // slots
    lanes = slot_heads * hd
    factor = 1.0 / math.sqrt(hd)
    scale = LOG2E * factor
    swap = Swap(staged, tokens_ref, tokens_peer, swap_sems, swap_local)
    middle = Spread(middle_ref, middle_in, middle_sum, middle_sems, local_sems.at[0])
    last = Spread(last_parts, last_in, last_sum, last_sems, local_sems.at[1])
    convs = Spread(conv_parts, conv_in, conv_sum, conv_sems, local_sems.at[2])

    def turned(n, ref):
        return remote(ref.at[0], ref.at[1], turn_sems, (n,), swap.device)

    def turn(n, ref, total):
        ref[0] = total[:, total.shape[1] - ref.shape[2] :].astype(BF16)
        turned(n, ref).start()

    @pl.when(step_id == 0)
    def _():
        count = lax.axis_size("dp")
        meet([swap.device] + [(lax.rem(lax.axis_index("dp") + s, count), lax.axis_index("tensor")) for s in range(1, count)])
        middle.start()
        dck_sum[...] = jnp.zeros_like(dck_sum)
        dcv_sum[...] = jnp.zeros_like(dcv_sum)
        weight_sum[...] = jnp.zeros_like(weight_sum)
        kconv_sum[...] = jnp.zeros_like(kconv_sum)
        vconv_sum[...] = jnp.zeros_like(vconv_sum)
        gain_sum[...] = jnp.zeros_like(gain_sum)

    dq_sum[...] = jnp.zeros_like(dq_sum)
    longest_here = lax.rem(lax.axis_index("tensor"), 2) == 0
    places, starts = item_starts(lens_ref, block, longest_here, ck_ref.shape[1])

    def step(kb, carry):
        bias = mask_bias(places, starts, kb)
        cols = key_rows(kb)
        for h in range(heads):
            band = slice(h * hd, (h + 1) * hd)
            one = slice(h, h + 1)
            q, dctx = q_ref[band, :], dctx_ref[band, :]
            s = nn(ck_ref[h, cols, :], q) * scale + bias
            p = jnp.exp2(s - lse_ref[one, :])
            dp = nn(cv_ref[h, cols, :], dctx)
            ds = (p * (dp - delta_ref[one, :])).astype(BF16)
            dcv_sum[h, cols, :] += nt(p.astype(BF16), dctx)
            dck_sum[h, cols, :] += nt(ds, q)
            dq_sum[band, :] += nn(ckt_ref[band, cols], ds)
        return carry

    lax.fori_loop(0, block + 1, step, 0)
    mask = mask_ref[0, 0:1, :]
    rows = key_rows(block)
    for h in range(heads):
        band = slice(h * hd, (h + 1) * hd)
        one = slice(h, h + 1)
        q, k = q_ref[band, :].astype(F32), k_ref[band, :].astype(F32)
        v, dctx = v_ref[band, :].astype(F32), dctx_ref[band, :].astype(F32)
        own_prob = jnp.exp2(jnp.sum(q * k, axis=0, keepdims=True) * scale - lse_ref[one, :])
        own_dprob = jnp.sum(dctx * v, axis=0, keepdims=True)
        own_dscore = own_prob * (own_dprob - delta_ref[one, :]) * factor
        slot, i = divmod(h, slot_heads)
        base = slot * 3 * lanes + i * hd
        dqkv[base : base + hd, :] = (dq_sum[band, :] * factor + own_dscore * k).astype(BF16)
        dck = (dck_sum[h, rows, :] * factor).astype(BF16)
        dcv = dcv_sum[h, rows, :].astype(BF16)
        for n, src, total, grad, beside in (
            (0, k_ref, kconv_sum, dck, own_dscore * q),
            (1, v_ref, vconv_sum, dcv, own_prob * dctx),
        ):
            spread = nt(conv_ref[slot, n * taps : (n + 1) * taps, i * hd : (i + 1) * hd], grad)
            spread = jnp.concatenate([spread[r * hd : (r + 1) * hd] for r in range(3)], axis=1)
            at = base + (n + 1) * lanes
            dqkv[at : at + hd, :] = ((spread + beside) * mask).astype(BF16)
            if h < own_heads:
                grouped = jnp.concatenate([src[band, r * GB : (r + 1) * GB] for r in range(3)], axis=0)
                total[h] += nn(grouped, grad)
    hat, inv_std = norm_rows(x_ref[...].astype(F32))
    gain = gain_ref[...]
    first_in = (hat * gain).astype(BF16)
    weight_sum[...] += nn(dqkv[0 : 3 * own, :], first_in)
    back = tn(dqkv[...], w_ref[...].reshape(slots * 3 * lanes, dim))
    gain_sum[...] += jnp.sum(back * hat, axis=0, keepdims=True)
    total = resid_grad_ref[...].astype(F32) + norm_back(back, gain, hat, inv_std)
    swap.send(step_id, block, total.astype(BF16))

    @pl.when(block == 0)
    def _():
        put_rows(last_parts, [weight_sum[...].T, jnp.broadcast_to(gain_sum[...], (GB, dim)).T])
        last.start()
        put_rows(
            conv_parts,
            [
                total[h]
                for slot in range(2)
                for total in (kconv_sum, vconv_sum)
                for h in range(slot * slot_heads, (slot + 1) * slot_heads)
            ],
        )
        convs.start()
        middle_total = middle.total()
        turn(0, middle_turn, middle_total)
        last_total = last.total()
        turn(1, last_turn, last_total)
        conv_total = convs.total()
        turn(2, conv_turn, conv_total)
        for n, (out, ref, total) in enumerate(
            ((middle_out, middle_turn, middle_total), (last_out, last_turn, last_total), (conv_out, conv_turn, conv_total))
        ):
            turned(n, ref).wait()
            cols = out.shape[1]
            split = total.shape[1] - cols
            kept = [total[:, :split]] + ([total[:, 2 * split :]] if cols > split else [])
            out[...] = ref[1].astype(F32) + jnp.concatenate(kept, axis=1)
        swap.finish(block)


def place_rows(lens_ref, longest_here, mine, theirs, natural, out_ref):
    half = mine.shape[0]
    first = longest_first(lens_ref, half // 3)
    chunks = natural.shape[0]

    def taps(block, r):
        rows = pl.ds(pl.multiple_of(block * TB + r * GB, GB), GB)
        return mine[rows, :].astype(F32), theirs[rows, :].astype(F32)

    def outside(block, carry):
        for r in range(3):
            a, b = taps(block, r)
            other = jnp.where(longest_here, b, a)
            for c in range(chunks):
                for base in (0, half):
                    natural[c, pl.ds(base + block * TB + r, GB, stride=3), :] = other[:, c * 128 : (c + 1) * 128]
        return carry

    def inside(block, carry):
        for r in range(3):
            a, b = taps(block, r)
            longest = jnp.where(longest_here, a, b)
            for c in range(chunks):
                natural[c, pl.ds(first + block * TB + r, GB, stride=3), :] = longest[:, c * 128 : (c + 1) * 128]
        return carry

    def written(block, carry):
        rows = pl.ds(pl.multiple_of(block * TB, TB), TB)
        out_ref[rows, :] = jnp.concatenate([natural[c, rows, :] for c in range(chunks)], axis=1).astype(BF16)
        return carry

    lax.fori_loop(0, half // TB, outside, 0)
    lax.fori_loop(0, half // TB, inside, 0)
    lax.fori_loop(0, 2 * half // TB, written, 0)


def last_kernel(
    hd, lens_ref, mixed_ref, mixed_peer, tokens_ref, tokens_peer, middle_ref, last_ref, conv_ref,
    mixed_out, tokens_out, gain1_out, gain2_out, query_out, key_out, value_out, out_out, kconv_out, vconv_out,
    up_out, down_out, natural,
):
    longest_here = lax.rem(lax.axis_index("tensor"), 2) == 0
    place_rows(lens_ref, longest_here, mixed_ref, mixed_peer, natural, mixed_out)
    place_rows(lens_ref, longest_here, tokens_ref, tokens_peer, natural, tokens_out)
    units, own = up_out.shape[1], query_out.shape[1]
    up_out[...] = middle_ref[:, 0:units]
    down_out[...] = middle_ref[:, units : 2 * units].T
    out_out[...] = middle_ref[:, 2 * units : 2 * units + own].T
    gain2_out[...] = middle_ref[:, 2 * units + own :].T[0:1]
    for n, out in enumerate((query_out, key_out, value_out)):
        out[...] = last_ref[:, n * own : (n + 1) * own]
    gain1_out[...] = last_ref[:, 3 * own :].T[0:1]
    for n, out in enumerate((kconv_out, vconv_out)):
        for h in range(out.shape[0]):
            out[h] = conv_ref[:, n * own + h * hd : n * own + (h + 1) * hd]


def whole(shape):
    return pl.BlockSpec(shape, lambda *_: (0,) * len(shape))


def cost(micros):
    return pl.CostEstimate(flops=int(micros * 1e9), bytes_accessed=1 << 20, transcendentals=0)


def params():
    return pltpu.CompilerParams(vmem_limit_bytes=VMEM, dimension_semantics=("arbitrary",))


def halves(lengths, rows):
    longest = jnp.argmax(lengths)
    before = jnp.arange(lengths.shape[0]) < longest
    first = 3 * jnp.sum(jnp.where(before, lengths, 0))
    return longest, first, jnp.arange(rows // 2, dtype=jnp.int32)


def own_rows(array, place, first, longest_here):
    half = place.shape[0]
    inside = lax.dynamic_slice_in_dim(array, first, half, 0)
    others = jnp.where(place < first, array[:half], array[half:])
    return jnp.where(longest_here, inside, others)


def on_device(
    tokens, first_gain, second_gain, query_weight, key_weight, value_weight, out_weight,
    key_conv, value_conv, up_weight, down_weight, pad_mask, item_lengths, cotangent,
):
    dim = tokens.shape[1]
    own_heads, taps, hd = key_conv.shape
    peers = lax.axis_size("tensor")
    heads = own_heads * peers
    width = heads * hd
    own = own_heads * hd
    units = up_weight.shape[1]
    longest_here = lax.rem(lax.axis_index("tensor"), 2) == 0
    longest, first, place = halves(item_lengths[0], tokens.shape[0])
    lens = item_lengths[0]
    pack = (place, first, longest_here)
    rows = tokens.shape[0] // 2
    blocks = rows // TB
    groups = rows // 3
    mask = own_rows(pad_mask, *pack)
    mask = mask.reshape(blocks, GB, 3).transpose(0, 2, 1).reshape(blocks, 1, TB).astype(F32)
    gain1, gain2 = first_gain[None], second_gain[None]

    rows_spec = pl.BlockSpec((TB, dim), lambda b, *_: (b, 0))
    cols_spec = pl.BlockSpec((width, TB), lambda b, *_: (0, b))
    stat_spec = pl.BlockSpec((heads, TB), lambda b, *_: (0, b))
    mask_spec = pl.BlockSpec((1, 1, TB), lambda b, *_: (b, 0, 0))
    anywhere = pl.BlockSpec(memory_space=pl.ANY)
    inside = pl.BlockSpec(memory_space=pltpu.VMEM)
    x, g, q, k, v, ctx, lse, ck, ckt, cv, w_all, conv_all, out_all, up_all, down_all = pl.pallas_call(
        functools.partial(forward_kernel, heads, hd),
        grid_spec=pltpu.PrefetchScalarGridSpec(
            num_scalar_prefetch=1,
            grid=(blocks,),
            in_specs=[inside, inside, whole((1, dim)), mask_spec] + [inside] * 5 + [anywhere] * 3,
            out_specs=[
                rows_spec, rows_spec, cols_spec, cols_spec, cols_spec, cols_spec, stat_spec,
                whole((heads, groups, hd)), whole((width, groups)), whole((heads, groups, hd)),
                anywhere, anywhere, anywhere, anywhere, anywhere,
            ],
            scratch_shapes=[
                pltpu.VMEM((dim // 128, 2 * rows, 128), F32), pltpu.VMEM((dim // 128, 2 * rows, 128), F32),
                pltpu.VMEM((peers, 3 * own, dim), BF16), pltpu.VMEM((peers, 2 * taps, own), BF16),
                pltpu.VMEM((width, groups), BF16),
                pltpu.VMEM((heads, TB), F32), pltpu.VMEM((heads, TB), F32), pltpu.VMEM((width, TB), F32),
                pltpu.SemaphoreType.DMA((2, 2, 2, peers - 1)), pltpu.SemaphoreType.DMA((2, 3, 2, peers - 1)),
                pltpu.SemaphoreType.DMA((5,)),
            ],
        ),
        out_shape=[jax.ShapeDtypeStruct((rows, dim), BF16)] * 2
        + [jax.ShapeDtypeStruct((width, rows), BF16)] * 4
        + [
            jax.ShapeDtypeStruct((heads, rows), F32),
            jax.ShapeDtypeStruct((heads, groups, hd), BF16),
            jax.ShapeDtypeStruct((width, groups), BF16),
            jax.ShapeDtypeStruct((heads, groups, hd), BF16),
            jax.ShapeDtypeStruct((peers, 3 * own, dim), BF16),
            jax.ShapeDtypeStruct((peers, 2 * taps, own), BF16),
            jax.ShapeDtypeStruct((peers, own, dim), BF16),
            jax.ShapeDtypeStruct((peers, dim, units), BF16),
            jax.ShapeDtypeStruct((peers, units, dim), BF16),
        ],
        compiler_params=pltpu.CompilerParams(
            vmem_limit_bytes=VMEM, dimension_semantics=("arbitrary",), collective_id=0, has_side_effects=True
        ),
        cost_estimate=cost(55),
        name="attention_forward",
    )(
        lens, tokens, cotangent, gain1, mask, query_weight, key_weight, value_weight, key_conv, value_conv,
        out_weight, up_weight, down_weight,
    )

    count = lax.axis_size("dp")
    slot_cols = 2 * units + own
    mid_cols = 2 * slot_cols + GB
    mixed, mixed_peer, resid_grad, dctx, delta, middle_grads = pl.pallas_call(
        functools.partial(middle_kernel, heads, hd),
        grid=(blocks,),
        in_specs=[
            rows_spec, rows_spec, whole((1, dim)), cols_spec, whole((width, dim)),
            whole((peers, dim, units)), whole((peers, units, dim)),
        ],
        out_specs=[anywhere, anywhere, rows_spec, cols_spec, stat_spec, whole((count, dim // count, mid_cols))],
        out_shape=[
            jax.ShapeDtypeStruct((rows, dim), BF16),
            jax.ShapeDtypeStruct((rows, dim), BF16),
            jax.ShapeDtypeStruct((rows, dim), BF16),
            jax.ShapeDtypeStruct((width, rows), BF16),
            jax.ShapeDtypeStruct((heads, rows), F32),
            jax.ShapeDtypeStruct((count, dim // count, mid_cols), BF16),
        ],
        scratch_shapes=[
            pltpu.VMEM((2, TB, dim), BF16), pltpu.VMEM((2, units, dim), F32),
            pltpu.VMEM((2, dim, units), F32), pltpu.VMEM((2 * own, dim), F32), pltpu.VMEM((1, dim), F32),
            pltpu.SemaphoreType.DMA((2, blocks)), pltpu.SemaphoreType.DMA((blocks,)),
        ],
        compiler_params=pltpu.CompilerParams(
            vmem_limit_bytes=VMEM, dimension_semantics=("arbitrary",), collective_id=1, has_side_effects=True
        ),
        cost_estimate=cost(55),
        name="feed_forward",
    )(x, g, gain2, ctx, out_all.reshape(width, dim), up_all, down_all)

    back_rows = pl.BlockSpec((TB, dim), lambda b, *_: (blocks - 1 - b, 0))
    back_cols = pl.BlockSpec((width, TB), lambda b, *_: (0, blocks - 1 - b))
    back_stat = pl.BlockSpec((heads, TB), lambda b, *_: (0, blocks - 1 - b))
    back_mask = pl.BlockSpec((1, 1, TB), lambda b, *_: (blocks - 1 - b, 0, 0))
    two = 2 * own_heads
    last_cols = 6 * own + GB
    out_dims = [(dim // count, slot_cols + GB), (dim // count, 3 * own + GB), (taps // count, 2 * own)]
    grad_rows, grad_peer, middle_share, last_share, conv_share = pl.pallas_call(
        functools.partial(backward_kernel, heads, hd, two),
        grid_spec=pltpu.PrefetchScalarGridSpec(
            num_scalar_prefetch=1,
            grid=(blocks,),
            in_specs=[
                back_rows, whole((1, dim)), whole((peers, 3 * own, dim)), whole((peers, 2 * taps, own)), back_mask,
                back_cols, back_cols, back_cols, back_stat,
                back_cols, back_stat, back_rows, whole((heads, groups, hd)), whole((width, groups)),
                whole((heads, groups, hd)), anywhere,
            ],
            out_specs=[anywhere, anywhere] + [whole(d) for d in out_dims],
            scratch_shapes=[
                pltpu.VMEM((2, TB, dim), BF16), pltpu.VMEM((heads, groups, hd), F32),
                pltpu.VMEM((heads, groups, hd), F32), pltpu.VMEM((width, TB), F32),
                pltpu.VMEM((3 * width, TB), BF16), pltpu.VMEM((6 * own, dim), F32),
                pltpu.VMEM((two, taps, hd), F32), pltpu.VMEM((two, taps, hd), F32),
                pltpu.VMEM((1, dim), F32),
                pltpu.VMEM((count, dim // count, mid_cols), BF16),
                pltpu.VMEM((count, dim // count, last_cols), BF16), pltpu.VMEM((count, dim // count, last_cols), BF16),
                pltpu.VMEM((count, taps // count, 4 * own), BF16), pltpu.VMEM((count, taps // count, 4 * own), BF16),
            ]
            + [pltpu.VMEM((2, *d), BF16) for d in out_dims]
            + [
                pltpu.VMEM((dim // count, mid_cols), F32), pltpu.VMEM((dim // count, last_cols), F32),
                pltpu.VMEM((taps // count, 4 * own), F32),
            ]
            + [
                pltpu.SemaphoreType.DMA((2, blocks)), pltpu.SemaphoreType.DMA((blocks,)),
                pltpu.SemaphoreType.DMA((2, count)), pltpu.SemaphoreType.DMA((2, count)),
                pltpu.SemaphoreType.DMA((2, count)), pltpu.SemaphoreType.DMA((2, 3)), pltpu.SemaphoreType.DMA((3,)),
            ],
        ),
        out_shape=[jax.ShapeDtypeStruct((rows, dim), BF16)] * 2 + [jax.ShapeDtypeStruct(d, F32) for d in out_dims],
        compiler_params=pltpu.CompilerParams(
            vmem_limit_bytes=VMEM, dimension_semantics=("arbitrary",), collective_id=2, has_side_effects=True
        ),
        cost_estimate=cost(60),
        name="attention_backward",
    )(lens, x, gain1, w_all, conv_all, mask, q, k, v, lse, dctx, delta, resid_grad, ck, ckt, cv, middle_grads)

    share = dim // count
    shapes = [
        ((2 * rows, dim), BF16), ((2 * rows, dim), BF16), ((1, share), F32), ((1, share), F32),
        ((share, own), F32), ((share, own), F32), ((share, own), F32), ((own, share), F32),
        ((own_heads, taps // count, hd), F32), ((own_heads, taps // count, hd), F32),
        ((share, units), F32), ((units, share), F32),
    ]
    outs = pl.pallas_call(
        functools.partial(last_kernel, hd),
        in_specs=[pl.BlockSpec(memory_space=pltpu.SMEM)] + [inside] * 7,
        out_specs=[inside] * len(shapes),
        out_shape=[jax.ShapeDtypeStruct(d, t) for d, t in shapes],
        scratch_shapes=[pltpu.VMEM((dim // 128, 2 * rows, 128), F32)],
        compiler_params=pltpu.CompilerParams(vmem_limit_bytes=VMEM),
        cost_estimate=cost(15),
        name="in_order",
    )(lens, mixed, mixed_peer, grad_rows, grad_peer, middle_share, last_share, conv_share)
    return (*outs[:2], outs[2].reshape(share), outs[3].reshape(share), *outs[4:])


def solution(mesh):
    in_specs = (
        P("dp", None),
        P(),
        P(),
        P(None, "tensor"),
        P(None, "tensor"),
        P(None, "tensor"),
        P("tensor", None),
        P("tensor", None, None),
        P("tensor", None, None),
        P(None, "tensor"),
        P("tensor", None),
        P("dp"),
        P("dp", None),
        P("dp", None),
    )
    out_specs = (
        P("dp", None),
        P("dp", None),
        P("dp"),
        P("dp"),
        P("dp", "tensor"),
        P("dp", "tensor"),
        P("dp", "tensor"),
        P("tensor", "dp"),
        P("tensor", "dp", None),
        P("tensor", "dp", None),
        P("dp", "tensor"),
        P("tensor", "dp"),
    )
    return jax.shard_map(
        on_device, mesh=mesh, in_specs=in_specs, out_specs=out_specs, check_vma=False
    )
```

```python
import functools
import math

import jax
import jax.numpy as jnp
from jax import lax
from jax.experimental import pallas as pl
from jax.experimental.pallas import tpu as pltpu
from jax.sharding import PartitionSpec as P

F32 = jnp.float32
BF16 = jnp.bfloat16
GB = 128
TB = 3 * GB
NEG = -1e30
LOG2E = 1.0 / math.log(2.0)
VMEM = 60 * 1024 * 1024

ERF_P = 0.43
ERF_C = (
    0.24255178053871013,
    0.24376598744271377,
    0.2089868288055898,
    0.23281685899157548,
    -0.05797941172752005,
    0.3523368029188165,
    -0.2915198548110903,
    0.06904073943922798,
)


def nn(a, b):
    return lax.dot_general(a, b, (((1,), (0,)), ((), ())), preferred_element_type=F32)


def nt(a, b):
    return lax.dot_general(a, b, (((1,), (1,)), ((), ())), preferred_element_type=F32)


def tn(a, b):
    return lax.dot_general(a, b, (((0,), (0,)), ((), ())), preferred_element_type=F32)


def norm_rows(values):
    centred = values - jnp.mean(values, -1, keepdims=True)
    inv_std = lax.rsqrt(jnp.mean(centred * centred, -1, keepdims=True) + 1e-05)
    return centred * inv_std, inv_std


def norm_back(grad_out, gains, normed, inv_std):
    scaled = grad_out * gains
    return inv_std * (
        scaled
        - jnp.mean(scaled, -1, keepdims=True)
        - normed * jnp.mean(scaled * normed, -1, keepdims=True)
    )


def gelu_and_slope(h):
    t = 1.0 / (1.0 + (ERF_P * math.sqrt(0.5)) * jnp.abs(h))
    poly = t * (0.5 * ERF_C[-1]) + 0.5 * ERF_C[-2]
    for c in ERF_C[-3::-1]:
        poly = poly * t + 0.5 * c
    e = jnp.exp2((h * h) * (-0.5 * LOG2E))
    tail = e * (poly * t)
    cdf = jnp.where(h >= 0, 1.0 - tail, tail)
    return h * cdf, cdf + h * (e * (1.0 / math.sqrt(2.0 * math.pi)))


def item_starts(lens_ref, block, longest_here, half):
    places = block * GB + lax.broadcasted_iota(jnp.int32, (1, GB), 1)
    starts = jnp.zeros((1, GB), jnp.int32)
    end = jnp.int32(0)
    for i in range(lens_ref.shape[0] - 1):
        end = end + jnp.where((lens_ref[i] == half) == longest_here, lens_ref[i], 0)
        starts = jnp.where(places >= end, end, starts)
    return places, starts


def longest_first(lens_ref, half):
    first, ahead = jnp.int32(0), jnp.int32(1)
    for i in range(lens_ref.shape[0]):
        ahead = jnp.where(lens_ref[i] == half, 0, ahead)
        first = first + ahead * lens_ref[i]
    return 3 * first


def own_taps(source, block, first, longest_here):
    half = source.shape[1] // 2
    base = block * TB
    parts = []
    for c in range(source.shape[0]):
        for r in range(3):
            inside = source[c, pl.ds(first + base + r, GB, stride=3), :]
            low = source[c, pl.ds(base + r, GB, stride=3), :]
            high = source[c, pl.ds(half + base + r, GB, stride=3), :]
            place = base + r + 3 * lax.broadcasted_iota(jnp.int32, (GB, 1), 0)
            parts.append(jnp.where(longest_here, inside, jnp.where(place < first, low, high)))
    return jnp.concatenate(
        [jnp.concatenate(parts[3 * c : 3 * c + 3], axis=0) for c in range(source.shape[0])], axis=1
    )


def put_bias(bias_ref, places, starts, count):
    for kb in range(count):
        keys = kb * GB + lax.broadcasted_iota(jnp.int32, (GB, GB), 0)
        bias_ref[kb * GB : (kb + 1) * GB, :] = jnp.where((keys >= starts) & (keys < places), 0.0, NEG)


def each_head(heads, hd, work):
    def some(i, carry):
        for n in range(4):
            h = 4 * i + n
            work(h, pl.ds(pl.multiple_of(h * hd, hd), hd), pl.ds(h, 1))
        return carry

    lax.fori_loop(0, heads // 4, some, 0)


def key_rows(kb):
    return pl.ds(pl.multiple_of(kb * GB, GB), GB)


def remote(src, dst, sems, at, device):
    return pltpu.make_async_remote_copy(
        src_ref=src, dst_ref=dst, send_sem=sems.at[(0, *at)], recv_sem=sems.at[(1, *at)],
        device_id=device, device_id_type=pl.DeviceIdType.MESH,
    )


def meet(devices):
    barrier = pltpu.get_barrier_semaphore()
    for device in devices:
        pl.semaphore_signal(barrier, inc=1, device_id=device, device_id_type=pl.DeviceIdType.MESH)
    pl.semaphore_wait(barrier, len(devices))


def put_rows(ref, pieces, at=0):
    count, rows, _ = ref.shape
    for piece in pieces:
        cols = piece.shape[1]
        for d in range(count):
            ref[d, :, at : at + cols] = piece[d * rows : (d + 1) * rows].astype(ref.dtype)
        at += cols


class Swap:
    def __init__(self, staged, mine, theirs, sems, local_sems):
        self.staged, self.mine, self.theirs, self.sems, self.local_sems = staged, mine, theirs, sems, local_sems
        self.device = (lax.axis_index("dp"), lax.axis_index("tensor") ^ 1)
        self.blocks = mine.shape[0] // TB

    def rows(self, block):
        return pl.ds(pl.multiple_of(block * TB, TB), TB)

    def local(self, step, block):
        staged = self.staged.at[lax.rem(step, 2)]
        return pltpu.make_async_copy(staged, self.mine.at[self.rows(block)], self.local_sems.at[step])

    def far(self, step, block):
        staged = self.staged.at[lax.rem(step, 2)]
        return remote(staged, self.theirs.at[self.rows(block)], self.sems, (step,), self.device)

    def settle(self, step, block):
        self.local(step, block).wait()
        self.far(step, block).wait_send()

    def send(self, step, block, values):
        @pl.when(step >= 2)
        def _():
            self.settle(step - 2, block)

        self.staged[lax.rem(step, 2)] = values
        self.local(step, block).start()
        self.far(step, block).start()

    def finish(self, block):
        for step in range(max(self.blocks - 2, 0), self.blocks):
            self.settle(step, block)
        for step in range(self.blocks):
            self.far(step, block).wait_recv()


class Spread:
    def __init__(self, source, landed, total, sems, local_sem):
        self.source, self.landed, self.sums, self.sems, self.local_sem = source, landed, total, sems, local_sem
        self.me, self.peer = lax.axis_index("dp"), lax.axis_index("tensor")
        self.count = lax.axis_size("dp")

    def copy(self, s):
        there = lax.rem(self.me + s, self.count)
        return remote(self.source.at[there], self.landed.at[s], self.sems, (s,), (there, self.peer))

    def own(self):
        return pltpu.make_async_copy(self.source.at[self.me], self.landed.at[0], self.local_sem)

    def start(self):
        self.own().start()

        def step(s, carry):
            self.copy(s).start()
            return carry

        lax.fori_loop(1, self.count, step, 0)

    def total(self):
        self.own().wait()

        def step(s, carry):
            self.copy(s).wait()
            return carry

        lax.fori_loop(1, self.count, step, 0)

        self.sums[...] = self.landed[0].astype(F32)

        def add(s, carry):
            self.sums[...] += self.landed[s].astype(F32)
            return carry

        lax.fori_loop(1, self.count, add, 0)
        return self.sums


class Gather:
    def __init__(self, own, far, sems):
        self.own, self.far, self.sems = own, far, sems
        self.dp, self.tensor = lax.axis_index("dp"), lax.axis_index("tensor")
        self.peers = lax.axis_size("tensor")

    def devices(self):
        return [(self.dp, self.tensor ^ s) for s in range(1, self.peers)] + [
            (self.dp ^ m, self.tensor) for m in (1, 2, 4, 6)
        ]

    def eighth(self, array):
        rows = array.shape[0] // 8
        place = lax.rem(self.dp, 2) * 4 + lax.rem(self.dp, 8) // 2
        return array.at[pl.ds(pl.multiple_of(place * rows, rows), rows)]

    def half(self, array):
        rows = array.shape[0] // 2
        return array.at[pl.ds(pl.multiple_of(lax.rem(self.dp, 2) * rows, rows), rows)]

    def across(self, n, s):
        device = (self.dp, self.tensor ^ s)
        return remote(
            self.eighth(self.own[n]), self.eighth(self.far[n].at[s - 1]), self.sems, (n, 0, s - 1), device
        )

    def around(self, n, s, m):
        part = self.eighth(self.far[n].at[s - 1])
        return remote(part, part, self.sems, (n, m // 2, s - 1), (self.dp ^ m, self.tensor))

    def beside(self, n, s):
        part = self.half(self.far[n].at[s - 1])
        return remote(part, part, self.sems, (n, 4, s - 1), (self.dp ^ 1, self.tensor))

    def each(self):
        return [(n, s) for s in range(self.peers - 1, 0, -1) for n in range(len(self.far))]

    def start(self):
        for n, s in self.each():
            self.across(n, s).start()

    def pass_around(self):
        for n, s in self.each():
            self.across(n, s).wait_recv()
            for m in (6, 4, 2):
                self.around(n, s, m).start()

    def pass_beside(self):
        for n, s in self.each():
            for m in (2, 4, 6):
                self.around(n, s, m).wait_recv()
            self.beside(n, s).start()

    def arrive(self):
        for n, s in self.each():
            self.beside(n, s).wait_recv()

    def finish(self):
        for n, s in self.each():
            self.across(n, s).wait_send()
            for m in (2, 4, 6):
                self.around(n, s, m).wait_send()
            self.beside(n, s).wait_send()


def forward_kernel(
    heads, hd, lens_ref, x_ref, g_ref, gain_ref, pad_ref, query_ref, key_ref, value_ref, kconv_ref, vconv_ref,
    out_ref, up_ref, down_ref,
    x_own, g_own, q_ref, k_ref, v_ref, ctx_ref, lse_ref, ck_ref, ckt_ref, cv_ref, w_all, conv_all,
    out_far, up_far, down_far,
    xs, gs, w_ref, conv_ref, cvt_ref, bias_ref, first_sems, last_sems, local_sems,
):
    block = pl.program_id(0)
    blocks = pl.num_programs(0)
    own_heads, _, taps = kconv_ref.shape
    own = own_heads * hd
    dim = x_ref.shape[1]
    conv_cols = conv_ref.shape[2] // 2
    scale = LOG2E / math.sqrt(hd)
    first_gather = Gather((w_ref.at[0], conv_ref.at[0]), (w_ref.at[1:], conv_ref.at[1:]), first_sems)
    last_gather = Gather((out_ref, up_ref, down_ref), (out_far, up_far, down_far), last_sems)
    keep_copies = [
        pltpu.make_async_copy(w_ref, w_all, local_sems.at[0]), pltpu.make_async_copy(conv_ref, conv_all, local_sems.at[1])
    ]

    @pl.when(block == 0)
    def _():
        for n, src in enumerate((query_ref, key_ref, value_ref)):
            w_ref[0, n * own : (n + 1) * own, :] = src[...].T
        conv_ref[0] = jnp.zeros_like(conv_ref[0])
        for n, src in enumerate((kconv_ref, vconv_ref)):
            for h in range(own_heads):
                conv_ref[0, h * hd : (h + 1) * hd, n * conv_cols : n * conv_cols + taps] = src[h]
        meet(first_gather.devices())
        first_gather.start()
        for src, dst in ((x_ref, xs), (g_ref, gs)):
            for c in range(dim // 128):
                dst[c] = src[:, c * 128 : (c + 1) * 128].astype(F32)
        first_gather.pass_around()
        pads = pad_ref[...].astype(F32).T
        for c in range(pads.shape[1]):
            xs[dim // 128, c * 128 : (c + 1) * 128, :] = jnp.broadcast_to(pads[:, c : c + 1], (128, 128))
        first_gather.pass_beside()
        last_gather.start()
        first_gather.arrive()
        first_gather.finish()
        for copy in keep_copies:
            copy.start()

    half = x_ref.shape[0] // 2
    longest_here = lax.rem(lax.axis_index("tensor"), 2) == 0
    first = longest_first(lens_ref, half // 3)
    x = own_taps(xs, block, first, longest_here)
    mask = x[:, dim:].T[0:1]
    x = x[:, :dim]
    x_own[...] = x.astype(BF16)
    g_own[...] = own_taps(gs, block, first, longest_here).astype(BF16)
    normed, _ = norm_rows(x)
    first_in = (normed * gain_ref[...]).astype(BF16)
    for slot in range(w_ref.shape[0]):
        at = slice(slot * own, (slot + 1) * own)
        part = nt(w_ref[slot], first_in)
        q_ref[at, :] = part[0:own].astype(BF16)
        k_ref[at, :] = (part[own : 2 * own] * mask).astype(BF16)
        v_ref[at, :] = (part[2 * own : 3 * own] * mask).astype(BF16)
    rows = key_rows(block)
    for h in range(heads):
        band = slice(h * hd, (h + 1) * hd)
        slot, i = divmod(h, own_heads)
        for n, src, plain, trans in ((0, k_ref, ck_ref, ckt_ref), (1, v_ref, cv_ref, cvt_ref)):
            grouped = jnp.concatenate([src[band, r * GB : (r + 1) * GB] for r in range(3)], axis=0)
            comp = nn(conv_ref[slot, i * hd : (i + 1) * hd, n * conv_cols : n * conv_cols + taps], grouped)
            trans[band, rows] = comp.astype(BF16)
            plain[h, rows, :] = comp.T.astype(BF16)
    places, starts = item_starts(lens_ref, block, longest_here, half // 3)
    lse_ref[heads:, :] = jnp.broadcast_to(mask, (lse_ref.shape[0] - heads, TB))

    def attend(count):
        keys = slice(0, count * GB)
        put_bias(bias_ref, places, starts, count)

        def head(h, band, one):
            q = q_ref[band, :]
            own_score = jnp.sum(q.astype(F32) * k_ref[band, :].astype(F32), axis=0, keepdims=True) * scale
            s = nn(ck_ref[h, keys, :], q) * scale + jnp.concatenate([bias_ref[keys, :]] * 3, axis=1)
            top = jnp.maximum(own_score, jnp.max(s, axis=0, keepdims=True))
            p = jnp.exp2(s - top)
            own_prob = jnp.exp2(own_score - top)
            total = own_prob + jnp.sum(p, axis=0, keepdims=True)
            mixed = own_prob * v_ref[band, :].astype(F32) + nn(cvt_ref[band, keys], p.astype(BF16))
            ctx_ref[band, :] = (mixed * (1.0 / total)).astype(BF16)
            lse_ref[one, :] = top + jnp.log(total) * LOG2E

        each_head(heads, hd, head)

    for n in range(half // TB):
        pl.when(block == n)(functools.partial(attend, n + 1))

    @pl.when(block == 1)
    def _():
        last_gather.pass_around()

    @pl.when(block == blocks - 2)
    def _():
        last_gather.pass_beside()

    @pl.when(block == blocks - 1)
    def _():
        last_gather.arrive()
        last_gather.finish()
        for copy in keep_copies:
            copy.wait()


def middle_kernel(
    heads, hd, x_ref, g_ref, gain_ref, ctx_ref, out_ref, up_ref, down_ref, out_far, up_far, down_far,
    mixed_ref, mixed_peer, resid_grad_ref, dctx_ref, delta_ref, grads_ref,
    staged, acts, hidden_grads, pre, act_grads, kept_acts, kept_grads, kept_in, kept_g, out_sum, gain_sum,
    sems, local_sems,
):
    block = pl.program_id(0)
    own, two = out_ref.shape[0], out_sum.shape[0]
    units = up_ref.shape[1]
    step = pre.shape[2]
    slots = up_far.shape[0] + 1
    swap = Swap(staged, mixed_ref, mixed_peer, sems, local_sems)

    @pl.when(block == 0)
    def _():
        meet([swap.device])
        out_sum[...] = jnp.zeros_like(out_sum)
        gain_sum[...] = jnp.zeros_like(gain_sum)

    gain = gain_ref[...]
    g_low = g_ref[...]
    resid = x_ref[...].astype(F32) + tn(ctx_ref[0:own, :], out_ref[...]) + tn(ctx_ref[own:, :], out_far[...])
    hat, inv_std = norm_rows(resid)
    second_in = (hat * gain).astype(BF16)
    kept_in[block] = second_in
    kept_g[block] = g_low

    def up(slot, cols=slice(None)):
        return up_ref[:, cols] if slot == 0 else up_far[slot - 1, :, cols]

    def down(slot, rows=slice(None)):
        return down_ref[rows, :] if slot == 0 else down_far[slot - 1, rows, :]

    def products(c):
        slot, at = divmod(c * step, units)
        part = slice(at, at + step)
        pre[c % 2] = nn(second_in, up(slot, part))
        act_grads[c % 2] = nt(g_low, down(slot, part))

    count = slots * units // step
    products(0)
    for c in range(count):
        if c + 1 < count:
            products(c + 1)
        act, slope = gelu_and_slope(pre[c % 2])
        act = act.astype(BF16)
        hidden_grad = (act_grads[c % 2] * slope).astype(BF16)
        part = slice(c * step, (c + 1) * step)
        acts[:, part] = act
        hidden_grads[:, part] = hidden_grad
        if c * step < 2 * units:
            kept_acts[block, :, part] = act
            kept_grads[block, :, part] = hidden_grad
    parts = [slice(slot * units, (slot + 1) * units) for slot in range(slots)]
    ffn = sum(nn(acts[:, part], down(slot)) for slot, part in enumerate(parts))
    swap.send(block, block, (resid + ffn).astype(BF16))
    back = sum(nt(hidden_grads[:, part], up(slot)) for slot, part in enumerate(parts))
    gain_sum[...] += jnp.sum(back * hat, axis=0, keepdims=True)
    resid_grad = g_low.astype(F32) + norm_back(back, gain, hat, inv_std)
    attn_grad = resid_grad.astype(BF16)
    resid_grad_ref[...] = attn_grad
    out_sum[...] += nn(ctx_ref[0:two, :], attn_grad)
    dctx = jnp.concatenate([nt(out_ref[...], attn_grad), nt(out_far[...], attn_grad)], axis=0).astype(BF16)
    dctx_ref[...] = dctx
    dots = dctx.astype(F32) * ctx_ref[...].astype(F32)
    for h in range(heads):
        delta_ref[h : h + 1, :] = jnp.sum(dots[h * hd : (h + 1) * hd], axis=0, keepdims=True)

    @pl.when(block == pl.num_programs(0) - 1)
    def _():
        rows = kept_in.shape[0] * kept_in.shape[1]
        dim = kept_in.shape[2]
        inputs, upstream = kept_in[...].reshape(rows, dim), kept_g[...].reshape(rows, dim)
        at = 0
        for slot in range(2):
            for left, kept in ((inputs, kept_grads), (upstream, kept_acts)):
                for c in range(slot * units, (slot + 1) * units, step):
                    put_rows(grads_ref, [tn(left, kept[:, :, c : c + step].reshape(rows, step))], at)
                    at += step
            put_rows(grads_ref, [out_sum[slot * own : (slot + 1) * own].T], at)
            at += own
        put_rows(grads_ref, [jnp.broadcast_to(gain_sum[...], (GB, dim)).T], at)
        swap.finish(block)


def backward_kernel(
    heads, hd, own_heads, lens_ref, x_ref, gain_ref, w_ref, conv_ref,
    q_ref, k_ref, v_ref, lse_ref, dctx_ref, delta_ref, resid_grad_ref, ck_ref, ckt_ref, cv_ref, middle_ref,
    tokens_ref, tokens_peer, middle_out, last_out, conv_out,
    staged, bias_ref, convs_ref, dck_sum, dcv_sum, dq_sum, dqkv, weight_sum, kconv_sum, vconv_sum, gain_sum,
    middle_in, last_parts, last_in, conv_parts, conv_in,
    middle_turn, last_turn, conv_turn, middle_sum, last_sum, conv_sum,
    swap_sems, swap_local, middle_sems, last_sems, conv_sems, turn_sems, local_sems,
):
    step_id = pl.program_id(0)
    block = pl.num_programs(0) - 1 - step_id
    own = own_heads * hd
    slots, _, dim = w_ref.shape
    taps = convs_ref.shape[2]
    conv_cols = conv_ref.shape[2] // 2
    slot_heads = heads // slots
    lanes = slot_heads * hd
    factor = 1.0 / math.sqrt(hd)
    scale = LOG2E * factor
    swap = Swap(staged, tokens_ref, tokens_peer, swap_sems, swap_local)
    middle = Spread(middle_ref, middle_in, middle_sum, middle_sems, local_sems.at[0])
    last = Spread(last_parts, last_in, last_sum, last_sems, local_sems.at[1])
    convs = Spread(conv_parts, conv_in, conv_sum, conv_sems, local_sems.at[2])

    def turned(n, ref):
        return remote(ref.at[0], ref.at[1], turn_sems, (n,), swap.device)

    def turn(n, ref, total):
        ref[0] = total[:, total.shape[1] - ref.shape[2] :].astype(BF16)
        turned(n, ref).start()

    @pl.when(step_id == 0)
    def _():
        count = lax.axis_size("dp")
        meet([swap.device] + [(lax.rem(lax.axis_index("dp") + s, count), lax.axis_index("tensor")) for s in range(1, count)])
        middle.start()
        for h in range(heads):
            slot, i = divmod(h, slot_heads)
            for n in range(2):
                conv = conv_ref[slot, i * hd : (i + 1) * hd, n * conv_cols : n * conv_cols + taps]
                convs_ref[n, h] = conv.astype(F32).T.astype(BF16)
        dck_sum[...] = jnp.zeros_like(dck_sum)
        dcv_sum[...] = jnp.zeros_like(dcv_sum)
        weight_sum[...] = jnp.zeros_like(weight_sum)
        kconv_sum[...] = jnp.zeros_like(kconv_sum)
        vconv_sum[...] = jnp.zeros_like(vconv_sum)
        gain_sum[...] = jnp.zeros_like(gain_sum)

    longest_here = lax.rem(lax.axis_index("tensor"), 2) == 0
    places, starts = item_starts(lens_ref, block, longest_here, ck_ref.shape[1])

    def attend(count):
        keys = slice(0, count * GB)
        put_bias(bias_ref, places, starts, count)

        def head(h, band, one):
            q, dctx = q_ref[band, :], dctx_ref[band, :]
            s = nn(ck_ref[h, keys, :], q) * scale + jnp.concatenate([bias_ref[keys, :]] * 3, axis=1)
            p = jnp.exp2(s - lse_ref[one, :])
            dp = nn(cv_ref[h, keys, :], dctx)
            ds = (p * (dp - delta_ref[one, :])).astype(BF16)
            dcv_sum[h, keys, :] += nt(p.astype(BF16), dctx)
            dck_sum[h, keys, :] += nt(ds, q)
            dq_sum[band, :] = nn(ckt_ref[band, keys], ds)

        each_head(heads, hd, head)

    for n in range(ck_ref.shape[1] // GB):
        pl.when(block == n)(functools.partial(attend, n + 1))
    mask = lse_ref[heads : heads + 1, :]
    rows = key_rows(block)
    for h in range(heads):
        band = slice(h * hd, (h + 1) * hd)
        one = slice(h, h + 1)
        q, k = q_ref[band, :].astype(F32), k_ref[band, :].astype(F32)
        v, dctx = v_ref[band, :].astype(F32), dctx_ref[band, :].astype(F32)
        own_prob = jnp.exp2(jnp.sum(q * k, axis=0, keepdims=True) * scale - lse_ref[one, :])
        own_dprob = jnp.sum(dctx * v, axis=0, keepdims=True)
        own_dscore = own_prob * (own_dprob - delta_ref[one, :]) * factor
        slot, i = divmod(h, slot_heads)
        base = slot * 3 * lanes + i * hd
        dqkv[base : base + hd, :] = (dq_sum[band, :] * factor + own_dscore * k).astype(BF16)
        dck = (dck_sum[h, rows, :] * factor).astype(BF16)
        dcv = dcv_sum[h, rows, :].astype(BF16)
        for n, src, total, grad, beside in (
            (0, k_ref, kconv_sum, dck, own_dscore * q),
            (1, v_ref, vconv_sum, dcv, own_prob * dctx),
        ):
            spread = nt(convs_ref[n, h], grad)
            spread = jnp.concatenate([spread[r * hd : (r + 1) * hd] for r in range(3)], axis=1)
            at = base + (n + 1) * lanes
            dqkv[at : at + hd, :] = ((spread + beside) * mask).astype(BF16)
            if h < own_heads:
                grouped = jnp.concatenate([src[band, r * GB : (r + 1) * GB] for r in range(3)], axis=0)
                total[h] += nn(grouped, grad)
    hat, inv_std = norm_rows(x_ref[...].astype(F32))
    gain = gain_ref[...]
    first_in = (hat * gain).astype(BF16)
    weight_sum[...] += nn(dqkv[0 : 3 * own, :], first_in)
    back = tn(dqkv[...], w_ref[...].reshape(slots * 3 * lanes, dim))
    gain_sum[...] += jnp.sum(back * hat, axis=0, keepdims=True)
    total = resid_grad_ref[...].astype(F32) + norm_back(back, gain, hat, inv_std)
    swap.send(step_id, block, total.astype(BF16))

    @pl.when(block == 0)
    def _():
        put_rows(last_parts, [weight_sum[...].T, jnp.broadcast_to(gain_sum[...], (GB, dim)).T])
        last.start()
        put_rows(
            conv_parts,
            [
                total[h]
                for slot in range(2)
                for total in (kconv_sum, vconv_sum)
                for h in range(slot * slot_heads, (slot + 1) * slot_heads)
            ],
        )
        convs.start()
        middle_total = middle.total()
        turn(0, middle_turn, middle_total)
        last_total = last.total()
        turn(1, last_turn, last_total)
        conv_total = convs.total()
        turn(2, conv_turn, conv_total)
        for n, (out, ref, total) in enumerate(
            ((middle_out, middle_turn, middle_total), (last_out, last_turn, last_total), (conv_out, conv_turn, conv_total))
        ):
            turned(n, ref).wait()
            cols = out.shape[1]
            split = total.shape[1] - cols
            kept = [total[:, :split]] + ([total[:, 2 * split :]] if cols > split else [])
            out[...] = ref[1].astype(F32) + jnp.concatenate(kept, axis=1)
        swap.finish(block)


def place_rows(lens_ref, longest_here, mine, theirs, natural, out_ref):
    half = mine.shape[0]
    first = longest_first(lens_ref, half // 3)

    def taps(block, r, other):
        rows = pl.ds(pl.multiple_of(block * TB + r * GB, GB), GB)
        a, b = mine[rows, :].astype(F32), theirs[rows, :].astype(F32)
        return jnp.where(longest_here == other, b, a)

    for block in range(half // TB):
        for r in range(3):
            others = taps(block, r, True)
            for base in (0, half):
                natural[pl.ds(base + block * TB + r, GB, stride=3), :] = others
    for block in range(half // TB):
        for r in range(3):
            natural[pl.ds(first + block * TB + r, GB, stride=3), :] = taps(block, r, False)
    out_ref[...] = natural[...].astype(BF16)


def last_kernel(
    hd, lens_ref, mixed_ref, mixed_peer, tokens_ref, tokens_peer, middle_ref, last_ref, conv_ref,
    mixed_out, tokens_out, gain1_out, gain2_out, query_out, key_out, value_out, out_out, kconv_out, vconv_out,
    up_out, down_out, natural_mixed, natural_tokens,
):
    longest_here = lax.rem(lax.axis_index("tensor"), 2) == 0
    place_rows(lens_ref, longest_here, mixed_ref, mixed_peer, natural_mixed, mixed_out)
    place_rows(lens_ref, longest_here, tokens_ref, tokens_peer, natural_tokens, tokens_out)

    @pl.when(pl.program_id(0) == 0)
    def _():
        units, own = up_out.shape[1], query_out.shape[1]
        up_out[...] = middle_ref[:, 0:units]
        down_out[...] = middle_ref[:, units : 2 * units].T
        out_out[...] = middle_ref[:, 2 * units : 2 * units + own].T
        gain2_out[...] = middle_ref[:, 2 * units + own :].T[0:1]
        for n, out in enumerate((query_out, key_out, value_out)):
            out[...] = last_ref[:, n * own : (n + 1) * own]
        gain1_out[...] = last_ref[:, 3 * own :].T[0:1]
        for n, out in enumerate((kconv_out, vconv_out)):
            for h in range(out.shape[0]):
                out[h] = conv_ref[:, n * own + h * hd : n * own + (h + 1) * hd].T


def whole(shape):
    return pl.BlockSpec(shape, lambda *_: (0,) * len(shape))


def cost(micros):
    return pl.CostEstimate(flops=int(micros * 1e9), bytes_accessed=1 << 20, transcendentals=0)


def params():
    return pltpu.CompilerParams(vmem_limit_bytes=VMEM, dimension_semantics=("arbitrary",))


def on_device(
    tokens, first_gain, second_gain, query_weight, key_weight, value_weight, out_weight,
    key_conv, value_conv, up_weight, down_weight, pad_mask, item_lengths, cotangent,
):
    dim = tokens.shape[1]
    own_heads, taps, hd = key_conv.shape
    peers = lax.axis_size("tensor")
    heads = own_heads * peers
    width = heads * hd
    own = own_heads * hd
    units = up_weight.shape[1]
    lens = item_lengths[0]
    rows = tokens.shape[0] // 2
    blocks = rows // TB
    groups = rows // 3
    pads = pad_mask.reshape(-1, 128)
    key_conv, value_conv = key_conv.transpose(0, 2, 1), value_conv.transpose(0, 2, 1)
    conv_cols = -(-taps // 128) * 128
    stats = heads + 8
    gain1, gain2 = first_gain[None], second_gain[None]

    rows_spec = pl.BlockSpec((TB, dim), lambda b, *_: (b, 0))
    cols_spec = pl.BlockSpec((width, TB), lambda b, *_: (0, b))
    stat_spec = pl.BlockSpec((heads, TB), lambda b, *_: (0, b))
    lse_spec = pl.BlockSpec((stats, TB), lambda b, *_: (0, b))
    anywhere = pl.BlockSpec(memory_space=pl.ANY)
    inside = pl.BlockSpec(memory_space=pltpu.VMEM)
    x, g, q, k, v, ctx, lse, ck, ckt, cv, w_all, conv_all, out_far, up_far, down_far = pl.pallas_call(
        functools.partial(forward_kernel, heads, hd),
        grid_spec=pltpu.PrefetchScalarGridSpec(
            num_scalar_prefetch=1,
            grid=(blocks,),
            in_specs=[inside, inside, whole((1, dim))] + [inside] * 6 + [anywhere] * 3,
            out_specs=[
                rows_spec, rows_spec, cols_spec, cols_spec, cols_spec, cols_spec, lse_spec,
                whole((heads, groups, hd)), whole((width, groups)), whole((heads, groups, hd)),
                anywhere, anywhere, anywhere, anywhere, anywhere,
            ],
            scratch_shapes=[
                pltpu.VMEM((dim // 128 + 1, 2 * rows, 128), F32), pltpu.VMEM((dim // 128, 2 * rows, 128), F32),
                pltpu.VMEM((peers, 3 * own, dim), BF16), pltpu.VMEM((peers, own, 2 * conv_cols), BF16),
                pltpu.VMEM((width, groups), BF16), pltpu.VMEM((groups, GB), F32),
                pltpu.SemaphoreType.DMA((2, 2, 5, peers - 1)), pltpu.SemaphoreType.DMA((2, 3, 5, peers - 1)),
                pltpu.SemaphoreType.DMA((2,)),
            ],
        ),
        out_shape=[jax.ShapeDtypeStruct((rows, dim), BF16)] * 2
        + [jax.ShapeDtypeStruct((width, rows), BF16)] * 4
        + [
            jax.ShapeDtypeStruct((stats, rows), F32),
            jax.ShapeDtypeStruct((heads, groups, hd), BF16),
            jax.ShapeDtypeStruct((width, groups), BF16),
            jax.ShapeDtypeStruct((heads, groups, hd), BF16),
            jax.ShapeDtypeStruct((peers, 3 * own, dim), BF16),
            jax.ShapeDtypeStruct((peers, own, 2 * conv_cols), BF16),
            jax.ShapeDtypeStruct((peers - 1, own, dim), BF16),
            jax.ShapeDtypeStruct((peers - 1, dim, units), BF16),
            jax.ShapeDtypeStruct((peers - 1, units, dim), BF16),
        ],
        compiler_params=pltpu.CompilerParams(
            vmem_limit_bytes=VMEM, dimension_semantics=("arbitrary",), collective_id=0, has_side_effects=True
        ),
        cost_estimate=cost(55),
        name="attention_forward",
    )(
        lens, tokens, cotangent, gain1, pads, query_weight, key_weight, value_weight, key_conv, value_conv,
        out_weight, up_weight, down_weight,
    )

    count = lax.axis_size("dp")
    slot_cols = 2 * units + own
    mid_cols = 2 * slot_cols + GB
    step = 256
    mixed, mixed_peer, resid_grad, dctx, delta, middle_grads = pl.pallas_call(
        functools.partial(middle_kernel, heads, hd),
        grid=(blocks,),
        in_specs=[
            rows_spec, rows_spec, whole((1, dim)), cols_spec, whole((own, dim)),
            whole((dim, units)), whole((units, dim)), whole((width - own, dim)),
            whole((peers - 1, dim, units)), whole((peers - 1, units, dim)),
        ],
        out_specs=[anywhere, anywhere, rows_spec, cols_spec, stat_spec, whole((count, dim // count, mid_cols))],
        out_shape=[
            jax.ShapeDtypeStruct((rows, dim), BF16),
            jax.ShapeDtypeStruct((rows, dim), BF16),
            jax.ShapeDtypeStruct((rows, dim), BF16),
            jax.ShapeDtypeStruct((width, rows), BF16),
            jax.ShapeDtypeStruct((heads, rows), F32),
            jax.ShapeDtypeStruct((count, dim // count, mid_cols), BF16),
        ],
        scratch_shapes=[
            pltpu.VMEM((2, TB, dim), BF16), pltpu.VMEM((TB, peers * units), BF16), pltpu.VMEM((TB, peers * units), BF16),
            pltpu.VMEM((2, TB, step), F32), pltpu.VMEM((2, TB, step), F32),
            pltpu.VMEM((blocks, TB, 2 * units), BF16), pltpu.VMEM((blocks, TB, 2 * units), BF16),
            pltpu.VMEM((blocks, TB, dim), BF16), pltpu.VMEM((blocks, TB, dim), BF16),
            pltpu.VMEM((2 * own, dim), F32), pltpu.VMEM((1, dim), F32),
            pltpu.SemaphoreType.DMA((2, blocks)), pltpu.SemaphoreType.DMA((blocks,)),
        ],
        compiler_params=pltpu.CompilerParams(
            vmem_limit_bytes=VMEM, dimension_semantics=("arbitrary",), collective_id=1, has_side_effects=True
        ),
        cost_estimate=cost(55),
        name="feed_forward",
    )(x, g, gain2, ctx, out_weight, up_weight, down_weight, out_far.reshape(width - own, dim), up_far, down_far)

    back_rows = pl.BlockSpec((TB, dim), lambda b, *_: (blocks - 1 - b, 0))
    back_cols = pl.BlockSpec((width, TB), lambda b, *_: (0, blocks - 1 - b))
    back_stat = pl.BlockSpec((heads, TB), lambda b, *_: (0, blocks - 1 - b))
    back_lse = pl.BlockSpec((stats, TB), lambda b, *_: (0, blocks - 1 - b))
    two = 2 * own_heads
    last_cols = 6 * own + GB
    out_dims = [(dim // count, slot_cols + GB), (dim // count, 3 * own + GB), (taps // count, 2 * own)]
    grad_rows, grad_peer, middle_share, last_share, conv_share = pl.pallas_call(
        functools.partial(backward_kernel, heads, hd, two),
        grid_spec=pltpu.PrefetchScalarGridSpec(
            num_scalar_prefetch=1,
            grid=(blocks,),
            in_specs=[
                back_rows, whole((1, dim)), whole((peers, 3 * own, dim)), whole((peers, own, 2 * conv_cols)),
                back_cols, back_cols, back_cols, back_lse,
                back_cols, back_stat, back_rows, whole((heads, groups, hd)), whole((width, groups)),
                whole((heads, groups, hd)), anywhere,
            ],
            out_specs=[anywhere, anywhere] + [whole(d) for d in out_dims],
            scratch_shapes=[
                pltpu.VMEM((2, TB, dim), BF16), pltpu.VMEM((groups, GB), F32),
                pltpu.VMEM((2, heads, taps, hd), BF16), pltpu.VMEM((heads, groups, hd), F32),
                pltpu.VMEM((heads, groups, hd), F32), pltpu.VMEM((width, TB), F32),
                pltpu.VMEM((3 * width, TB), BF16), pltpu.VMEM((6 * own, dim), F32),
                pltpu.VMEM((two, taps, hd), F32), pltpu.VMEM((two, taps, hd), F32),
                pltpu.VMEM((1, dim), F32),
                pltpu.VMEM((count, dim // count, mid_cols), BF16),
                pltpu.VMEM((count, dim // count, last_cols), BF16), pltpu.VMEM((count, dim // count, last_cols), BF16),
                pltpu.VMEM((count, taps // count, 4 * own), BF16), pltpu.VMEM((count, taps // count, 4 * own), BF16),
            ]
            + [pltpu.VMEM((2, *d), BF16) for d in out_dims]
            + [
                pltpu.VMEM((dim // count, mid_cols), F32), pltpu.VMEM((dim // count, last_cols), F32),
                pltpu.VMEM((taps // count, 4 * own), F32),
            ]
            + [
                pltpu.SemaphoreType.DMA((2, blocks)), pltpu.SemaphoreType.DMA((blocks,)),
                pltpu.SemaphoreType.DMA((2, count)), pltpu.SemaphoreType.DMA((2, count)),
                pltpu.SemaphoreType.DMA((2, count)), pltpu.SemaphoreType.DMA((2, 3)), pltpu.SemaphoreType.DMA((3,)),
            ],
        ),
        out_shape=[jax.ShapeDtypeStruct((rows, dim), BF16)] * 2 + [jax.ShapeDtypeStruct(d, F32) for d in out_dims],
        compiler_params=pltpu.CompilerParams(
            vmem_limit_bytes=VMEM, dimension_semantics=("arbitrary",), collective_id=2, has_side_effects=True
        ),
        cost_estimate=cost(60),
        name="attention_backward",
    )(lens, x, gain1, w_all, conv_all, q, k, v, lse, dctx, delta, resid_grad, ck, ckt, cv, middle_grads)

    share = dim // count
    own_conv = (own_heads, hd, taps // count)
    shapes = [
        ((1, share), F32), ((1, share), F32), ((share, own), F32), ((share, own), F32), ((share, own), F32),
        ((own, share), F32), (own_conv, F32), (own_conv, F32), ((share, units), F32), ((units, share), F32),
    ]
    lane_half = pl.BlockSpec((rows, 128), lambda c: (0, c))
    lane_all = pl.BlockSpec((2 * rows, 128), lambda c: (0, c))
    outs = pl.pallas_call(
        functools.partial(last_kernel, hd),
        grid=(dim // 128,),
        in_specs=[pl.BlockSpec(memory_space=pltpu.SMEM)] + [lane_half] * 4 + [whole(d) for d in out_dims],
        out_specs=[lane_all] * 2 + [whole(d) for d, _ in shapes],
        out_shape=[jax.ShapeDtypeStruct((2 * rows, dim), BF16)] * 2 + [jax.ShapeDtypeStruct(d, t) for d, t in shapes],
        scratch_shapes=[pltpu.VMEM((2 * rows, 128), F32)] * 2,
        compiler_params=params(),
        cost_estimate=cost(15),
        name="in_order",
    )(lens, mixed, mixed_peer, grad_rows, grad_peer, middle_share, last_share, conv_share)
    mixed, grad_tokens, gain1, gain2, query, key, value, out, kconv, vconv, up, down = outs
    return (
        mixed, grad_tokens, gain1.reshape(share), gain2.reshape(share), query, key, value, out,
        kconv.transpose(0, 2, 1), vconv.transpose(0, 2, 1), up, down,
    )


def solution(mesh):
    in_specs = (
        P("dp", None),
        P(),
        P(),
        P(None, "tensor"),
        P(None, "tensor"),
        P(None, "tensor"),
        P("tensor", None),
        P("tensor", None, None),
        P("tensor", None, None),
        P(None, "tensor"),
        P("tensor", None),
        P("dp"),
        P("dp", None),
        P("dp", None),
    )
    out_specs = (
        P("dp", None),
        P("dp", None),
        P("dp"),
        P("dp"),
        P("dp", "tensor"),
        P("dp", "tensor"),
        P("dp", "tensor"),
        P("tensor", "dp"),
        P("tensor", "dp", None),
        P("tensor", "dp", None),
        P("dp", "tensor"),
        P("tensor", "dp"),
    )
    return jax.shard_map(
        on_device, mesh=mesh, in_specs=in_specs, out_specs=out_specs, check_vma=False
    )
```

```python
import functools
import math

import jax
import jax.numpy as jnp
from jax import lax
from jax.experimental import pallas as pl
from jax.experimental.pallas import tpu as pltpu
from jax.sharding import PartitionSpec as P

F32 = jnp.float32
BF16 = jnp.bfloat16
GB = 128
TB = 3 * GB
NEG = -1e30
LOG2E = 1.0 / math.log(2.0)
VMEM = 60 * 1024 * 1024

ERF_P = 0.43
ERF_C = (
    0.24255178053871013,
    0.24376598744271377,
    0.2089868288055898,
    0.23281685899157548,
    -0.05797941172752005,
    0.3523368029188165,
    -0.2915198548110903,
    0.06904073943922798,
)


def nn(a, b):
    return lax.dot_general(a, b, (((1,), (0,)), ((), ())), preferred_element_type=F32)


def nt(a, b):
    return lax.dot_general(a, b, (((1,), (1,)), ((), ())), preferred_element_type=F32)


def tn(a, b):
    return lax.dot_general(a, b, (((0,), (0,)), ((), ())), preferred_element_type=F32)


def norm_rows(values):
    centred = values - jnp.mean(values, -1, keepdims=True)
    inv_std = lax.rsqrt(jnp.mean(centred * centred, -1, keepdims=True) + 1e-05)
    return centred * inv_std, inv_std


def norm_back(grad_out, gains, normed, inv_std):
    scaled = grad_out * gains
    return inv_std * (
        scaled
        - jnp.mean(scaled, -1, keepdims=True)
        - normed * jnp.mean(scaled * normed, -1, keepdims=True)
    )


def gelu_and_slope(h):
    t = 1.0 / (1.0 + (ERF_P * math.sqrt(0.5)) * jnp.abs(h))
    poly = t * (0.5 * ERF_C[-1]) + 0.5 * ERF_C[-2]
    for c in ERF_C[-3::-1]:
        poly = poly * t + 0.5 * c
    e = jnp.exp2((h * h) * (-0.5 * LOG2E))
    tail = e * (poly * t)
    cdf = jnp.where(h >= 0, 1.0 - tail, tail)
    return h * cdf, cdf + h * (e * (1.0 / math.sqrt(2.0 * math.pi)))


def item_starts(lens_ref, block, longest_here, half):
    places = block * GB + lax.broadcasted_iota(jnp.int32, (1, GB), 1)
    starts = jnp.zeros((1, GB), jnp.int32)
    end = jnp.int32(0)
    for i in range(lens_ref.shape[0] - 1):
        end = end + jnp.where((lens_ref[i] == half) == longest_here, lens_ref[i], 0)
        starts = jnp.where(places >= end, end, starts)
    return places, starts


def longest_first(lens_ref, half):
    first, ahead = jnp.int32(0), jnp.int32(1)
    for i in range(lens_ref.shape[0]):
        ahead = jnp.where(lens_ref[i] == half, 0, ahead)
        first = first + ahead * lens_ref[i]
    return 3 * first


def own_taps(source, block, first, longest_here):
    half = source.shape[1] // 2
    base = block * TB
    parts = []
    for c in range(source.shape[0]):
        for r in range(3):
            inside = source[c, pl.ds(first + base + r, GB, stride=3), :]
            low = source[c, pl.ds(base + r, GB, stride=3), :]
            high = source[c, pl.ds(half + base + r, GB, stride=3), :]
            place = base + r + 3 * lax.broadcasted_iota(jnp.int32, (GB, 1), 0)
            parts.append(jnp.where(longest_here, inside, jnp.where(place < first, low, high)))
    return jnp.concatenate(
        [jnp.concatenate(parts[3 * c : 3 * c + 3], axis=0) for c in range(source.shape[0])], axis=1
    )


def put_bias(bias_ref, places, starts, count):
    for kb in range(count):
        keys = kb * GB + lax.broadcasted_iota(jnp.int32, (GB, GB), 0)
        bias_ref[kb * GB : (kb + 1) * GB, :] = jnp.where((keys >= starts) & (keys < places), 0.0, NEG)


def each_head(heads, hd, work):
    def some(i, carry):
        for n in range(2):
            h = 2 * i + n
            work(h, pl.ds(pl.multiple_of(h * hd, hd), hd), pl.ds(h, 1))
        return carry

    lax.fori_loop(0, heads // 2, some, 0)


def key_rows(kb):
    return pl.ds(pl.multiple_of(kb * GB, GB), GB)


def remote(src, dst, sems, at, device):
    return pltpu.make_async_remote_copy(
        src_ref=src, dst_ref=dst, send_sem=sems.at[(0, *at)], recv_sem=sems.at[(1, *at)],
        device_id=device, device_id_type=pl.DeviceIdType.MESH,
    )


def meet(devices):
    barrier = pltpu.get_barrier_semaphore()
    for device in devices:
        pl.semaphore_signal(barrier, inc=1, device_id=device, device_id_type=pl.DeviceIdType.MESH)
    pl.semaphore_wait(barrier, len(devices))


def put_rows(ref, pieces, at=0):
    count, rows, _ = ref.shape
    for piece in pieces:
        cols = piece.shape[1]
        for d in range(count):
            ref[d, :, at : at + cols] = piece[d * rows : (d + 1) * rows].astype(ref.dtype)
        at += cols


class Swap:
    def __init__(self, staged, mine, theirs, sems, local_sems):
        self.staged, self.mine, self.theirs, self.sems, self.local_sems = staged, mine, theirs, sems, local_sems
        self.device = (lax.axis_index("dp"), lax.axis_index("tensor") ^ 1)
        self.blocks = mine.shape[0] // TB

    def rows(self, block):
        return pl.ds(pl.multiple_of(block * TB, TB), TB)

    def local(self, step, block):
        staged = self.staged.at[lax.rem(step, 2)]
        return pltpu.make_async_copy(staged, self.mine.at[self.rows(block)], self.local_sems.at[step])

    def far(self, step, block):
        staged = self.staged.at[lax.rem(step, 2)]
        return remote(staged, self.theirs.at[self.rows(block)], self.sems, (step,), self.device)

    def settle(self, step, block):
        self.local(step, block).wait()
        self.far(step, block).wait_send()

    def send(self, step, block, values, far=True):
        @pl.when(step >= 2)
        def _():
            self.settle(step - 2, block)

        self.staged[lax.rem(step, 2)] = values
        self.local(step, block).start()
        if far is True:
            self.far(step, block).start()
        else:
            pl.when(far)(lambda: self.far(step, block).start())

    def finish(self, block, count):
        for step in range(max(self.blocks - 2, 0), self.blocks):
            self.local(step, block).wait()
            if step < count:
                self.far(step, block).wait_send()
        for step in range(count):
            self.far(step, block).wait_recv()


class Spread:
    def __init__(self, source, landed, total, sems, local_sem):
        self.source, self.landed, self.sums, self.sems, self.local_sem = source, landed, total, sems, local_sem
        self.me, self.peer = lax.axis_index("dp"), lax.axis_index("tensor")
        self.count = lax.axis_size("dp")

    def copy(self, s):
        there = lax.rem(self.me + s, self.count)
        return remote(self.source.at[there], self.landed.at[s], self.sems, (s,), (there, self.peer))

    def own(self):
        return pltpu.make_async_copy(self.source.at[self.me], self.landed.at[0], self.local_sem)

    def start(self):
        self.own().start()

        def step(s, carry):
            self.copy(s).start()
            return carry

        lax.fori_loop(1, self.count, step, 0)

    def total(self):
        self.own().wait()

        def step(s, carry):
            self.copy(s).wait()
            return carry

        lax.fori_loop(1, self.count, step, 0)

        self.sums[...] = self.landed[0].astype(F32)

        def add(s, carry):
            self.sums[...] += self.landed[s].astype(F32)
            return carry

        lax.fori_loop(1, self.count, add, 0)
        return self.sums


class Gather:
    def __init__(self, own, far, sems):
        self.own, self.far, self.sems = own, far, sems
        self.dp, self.tensor = lax.axis_index("dp"), lax.axis_index("tensor")
        self.peers = lax.axis_size("tensor")

    def devices(self):
        return [(self.dp, self.tensor ^ s) for s in range(1, self.peers)] + [
            (self.dp ^ m, self.tensor) for m in (1, 2, 4, 6)
        ]

    def eighth(self, array):
        rows = array.shape[0] // 8
        place = lax.rem(self.dp, 2) * 4 + lax.rem(self.dp, 8) // 2
        return array.at[pl.ds(pl.multiple_of(place * rows, rows), rows)]

    def half(self, array):
        rows = array.shape[0] // 2
        return array.at[pl.ds(pl.multiple_of(lax.rem(self.dp, 2) * rows, rows), rows)]

    def across(self, n, s):
        device = (self.dp, self.tensor ^ s)
        return remote(
            self.eighth(self.own[n]), self.eighth(self.far[n].at[s - 1]), self.sems, (n, 0, s - 1), device
        )

    def around(self, n, s, m):
        part = self.eighth(self.far[n].at[s - 1])
        return remote(part, part, self.sems, (n, m // 2, s - 1), (self.dp ^ m, self.tensor))

    def beside(self, n, s):
        part = self.half(self.far[n].at[s - 1])
        return remote(part, part, self.sems, (n, 4, s - 1), (self.dp ^ 1, self.tensor))

    def each(self):
        return [(n, s) for s in range(1, self.peers) for n in range(len(self.far))]

    def start(self):
        for n, s in self.each():
            self.across(n, s).start()

    def pass_around(self):
        for n, s in self.each():
            self.across(n, s).wait_recv()
            for m in (6, 4, 2):
                self.around(n, s, m).start()

    def pass_beside(self):
        for n, s in self.each():
            for m in (2, 4, 6):
                self.around(n, s, m).wait_recv()
            self.beside(n, s).start()

    def arrive(self):
        for n, s in self.each():
            self.beside(n, s).wait_recv()

    def finish(self):
        for n, s in self.each():
            self.across(n, s).wait_send()
            for m in (2, 4, 6):
                self.around(n, s, m).wait_send()
            self.beside(n, s).wait_send()


def forward_kernel(
    heads, hd, lens_ref, x_ref, g_ref, gain_ref, pad_ref, query_ref, key_ref, value_ref, kconv_ref, vconv_ref,
    out_ref, up_ref, down_ref,
    x_own, g_own, q_ref, k_ref, v_ref, ctx_ref, lse_ref, ck_ref, ckt_ref, cv_ref, w_all, conv_all,
    out_far, up_far, down_far,
    xs, gs, first_all, mask_rows, w_ref, conv_ref, cvt_ref, bias_ref, first_sems, last_sems, local_sems,
):
    block = pl.program_id(0)
    blocks = pl.num_programs(0)
    own_heads, _, taps = kconv_ref.shape
    own = own_heads * hd
    dim = x_ref.shape[1]
    conv_cols = conv_ref.shape[2] // 2
    scale = LOG2E / math.sqrt(hd)
    first_gather = Gather((w_ref.at[0], conv_ref.at[0]), (w_ref.at[1:], conv_ref.at[1:]), first_sems)
    last_gather = Gather((out_ref, up_ref, down_ref), (out_far, up_far, down_far), last_sems)
    keep_copies = [
        pltpu.make_async_copy(w_ref, w_all, local_sems.at[0]), pltpu.make_async_copy(conv_ref, conv_all, local_sems.at[1])
    ]

    half = x_ref.shape[0] // 2
    longest_here = lax.rem(lax.axis_index("tensor"), 2) == 0
    first = longest_first(lens_ref, half // 3)

    @pl.when(block == 0)
    def _():
        for n, src in enumerate((query_ref, key_ref, value_ref)):
            w_ref[0, n * own : (n + 1) * own, :] = src[...].T
        conv_ref[0] = jnp.zeros_like(conv_ref[0])
        for n, src in enumerate((kconv_ref, vconv_ref)):
            for h in range(own_heads):
                conv_ref[0, h * hd : (h + 1) * hd, n * conv_cols : n * conv_cols + taps] = src[h]
        meet(first_gather.devices())
        first_gather.start()
        for src, dst in ((x_ref, xs), (g_ref, gs)):
            for c in range(dim // 128):
                dst[c] = src[:, c * 128 : (c + 1) * 128].astype(F32)
        pads = pad_ref[...].astype(F32).T
        for c in range(pads.shape[1]):
            xs[dim // 128, c * 128 : (c + 1) * 128, :] = jnp.broadcast_to(pads[:, c : c + 1], (128, 128))
        first_gather.pass_around()
        last_gather.start()

        def prepare(n, carry):
            x = own_taps(xs, n, first, longest_here)
            mask_rows[n] = jnp.broadcast_to(x[:, dim:].T[0:1], mask_rows.shape[1:])
            x = x[:, :dim]
            normed, _ = norm_rows(x)
            first_all[n] = (normed * gain_ref[...]).astype(BF16)
            rows = pl.ds(pl.multiple_of(n * TB, TB), TB)
            x_own[rows, :] = x.astype(BF16)
            g_own[rows, :] = own_taps(gs, n, first, longest_here).astype(BF16)
            return carry

        lax.fori_loop(0, half // TB // 2, prepare, 0)
        first_gather.pass_beside()
        lax.fori_loop(half // TB // 2, half // TB, prepare, 0)
        first_gather.arrive()
        first_gather.finish()
        for copy in keep_copies:
            copy.start()

    mask = mask_rows[block, 0:1]
    first_in = first_all[block]
    for slot in range(w_ref.shape[0]):
        at = slice(slot * own, (slot + 1) * own)
        part = nt(w_ref[slot], first_in)
        q_ref[at, :] = part[0:own].astype(BF16)
        k_ref[at, :] = (part[own : 2 * own] * mask).astype(BF16)
        v_ref[at, :] = (part[2 * own : 3 * own] * mask).astype(BF16)
    rows = key_rows(block)
    for h in range(heads):
        band = slice(h * hd, (h + 1) * hd)
        slot, i = divmod(h, own_heads)
        for n, src, plain, trans in ((0, k_ref, ck_ref, ckt_ref), (1, v_ref, cv_ref, cvt_ref)):
            grouped = jnp.concatenate([src[band, r * GB : (r + 1) * GB] for r in range(3)], axis=0)
            comp = nn(conv_ref[slot, i * hd : (i + 1) * hd, n * conv_cols : n * conv_cols + taps], grouped)
            trans[band, rows] = comp.astype(BF16)
            plain[h, rows, :] = comp.T.astype(BF16)
    places, starts = item_starts(lens_ref, block, longest_here, half // 3)
    lse_ref[heads:, :] = jnp.broadcast_to(mask, (lse_ref.shape[0] - heads, TB))

    def attend(count):
        keys = slice(0, count * GB)
        put_bias(bias_ref, places, starts, count)

        def head(h, band, one):
            q = q_ref[band, :]
            own_score = jnp.sum(q.astype(F32) * k_ref[band, :].astype(F32), axis=0, keepdims=True) * scale
            s = nn(ck_ref[h, keys, :], q) * scale + jnp.concatenate([bias_ref[keys, :]] * 3, axis=1)
            top = jnp.maximum(own_score, jnp.max(s, axis=0, keepdims=True))
            p = jnp.exp2(s - top)
            own_prob = jnp.exp2(own_score - top)
            total = own_prob + jnp.sum(p, axis=0, keepdims=True)
            mixed = own_prob * v_ref[band, :].astype(F32) + nn(cvt_ref[band, keys], p.astype(BF16))
            ctx_ref[band, :] = (mixed * (1.0 / total)).astype(BF16)
            lse_ref[one, :] = top + jnp.log(total) * LOG2E

        each_head(heads, hd, head)

    @pl.when(block == 1)
    def _():
        last_gather.pass_around()

    for n in range(half // TB):
        pl.when(block == n)(functools.partial(attend, n + 1))

    @pl.when(block == blocks - 2)
    def _():
        last_gather.pass_beside()

    @pl.when(block == blocks - 1)
    def _():
        last_gather.arrive()
        last_gather.finish()
        for copy in keep_copies:
            copy.wait()


def middle_kernel(
    heads, hd, x_ref, g_ref, gain_ref, ctx_ref, out_ref, up_ref, down_ref, out_far, up_far, down_far,
    mixed_ref, mixed_peer, resid_grad_ref, dctx_ref, delta_ref, grads_ref,
    staged, acts, hidden_grads, pre, act_grads, kept_acts, kept_grads, kept_in, kept_g, out_sum, gain_sum,
    sems, local_sems,
):
    block = pl.program_id(0)
    own, two = out_ref.shape[0], out_sum.shape[0]
    units = up_ref.shape[1]
    step = pre.shape[2]
    slots = up_far.shape[0] + 1
    swap = Swap(staged, mixed_ref, mixed_peer, sems, local_sems)

    @pl.when(block == 0)
    def _():
        meet([swap.device])
        out_sum[...] = jnp.zeros_like(out_sum)
        gain_sum[...] = jnp.zeros_like(gain_sum)

    gain = gain_ref[...]
    g_low = g_ref[...]
    resid = x_ref[...].astype(F32) + tn(ctx_ref[0:own, :], out_ref[...]) + tn(ctx_ref[own:, :], out_far[...])
    hat, inv_std = norm_rows(resid)
    second_in = (hat * gain).astype(BF16)
    kept_in[block] = second_in
    kept_g[block] = g_low

    def up(slot, cols=slice(None)):
        return up_ref[:, cols] if slot == 0 else up_far[slot - 1, :, cols]

    def down(slot, rows=slice(None)):
        return down_ref[rows, :] if slot == 0 else down_far[slot - 1, rows, :]

    def products(c):
        slot, at = divmod(c * step, units)
        part = slice(at, at + step)
        pre[c % 2] = nn(second_in, up(slot, part))
        act_grads[c % 2] = nt(g_low, down(slot, part))

    count = slots * units // step
    products(0)
    for c in range(count):
        if c + 1 < count:
            products(c + 1)
        act, slope = gelu_and_slope(pre[c % 2])
        act = act.astype(BF16)
        hidden_grad = (act_grads[c % 2] * slope).astype(BF16)
        part = slice(c * step, (c + 1) * step)
        acts[:, part] = act
        hidden_grads[:, part] = hidden_grad
        if c * step < 2 * units:
            kept_acts[block, :, part] = act
            kept_grads[block, :, part] = hidden_grad
    parts = [slice(slot * units, (slot + 1) * units) for slot in range(slots)]
    ffn = sum(nn(acts[:, part], down(slot)) for slot, part in enumerate(parts))
    swap.send(block, block, (resid + ffn).astype(BF16), block < pl.num_programs(0) - 1)
    back = sum(nt(hidden_grads[:, part], up(slot)) for slot, part in enumerate(parts))
    gain_sum[...] += jnp.sum(back * hat, axis=0, keepdims=True)
    resid_grad = g_low.astype(F32) + norm_back(back, gain, hat, inv_std)
    attn_grad = resid_grad.astype(BF16)
    resid_grad_ref[...] = attn_grad
    out_sum[...] += nn(ctx_ref[0:two, :], attn_grad)
    dctx = jnp.concatenate([nt(out_ref[...], attn_grad), nt(out_far[...], attn_grad)], axis=0).astype(BF16)
    dctx_ref[...] = dctx
    dots = dctx.astype(F32) * ctx_ref[...].astype(F32)
    for h in range(heads):
        delta_ref[h : h + 1, :] = jnp.sum(dots[h * hd : (h + 1) * hd], axis=0, keepdims=True)

    @pl.when(block == pl.num_programs(0) - 1)
    def _():
        rows = kept_in.shape[0] * kept_in.shape[1]
        dim = kept_in.shape[2]
        inputs, upstream = kept_in[...].reshape(rows, dim), kept_g[...].reshape(rows, dim)
        at = 0
        for slot in range(2):
            for left, kept in ((inputs, kept_grads), (upstream, kept_acts)):
                for c in range(slot * units, (slot + 1) * units, step):
                    put_rows(grads_ref, [tn(left, kept[:, :, c : c + step].reshape(rows, step))], at)
                    at += step
            put_rows(grads_ref, [out_sum[slot * own : (slot + 1) * own].T], at)
            at += own
        put_rows(grads_ref, [jnp.broadcast_to(gain_sum[...], (GB, dim)).T], at)
        swap.finish(block, kept_in.shape[0] - 1)


def backward_kernel(
    heads, hd, own_heads, lens_ref, x_ref, gain_ref, w_ref, conv_ref,
    q_ref, k_ref, v_ref, lse_ref, dctx_ref, delta_ref, resid_grad_ref, ck_ref, ckt_ref, cv_ref, middle_ref, mixed_ref,
    tokens_ref, tokens_peer, mixed_last, middle_out, last_out, conv_out,
    staged, bias_ref, convs_ref, dck_sum, dcv_sum, dq_sum, dqkv, weight_sum, kconv_sum, vconv_sum, gain_sum,
    middle_in, last_parts, last_in, conv_parts, conv_in,
    middle_turn, last_turn, conv_turn, middle_sum, last_sum, conv_sum,
    swap_sems, swap_local, middle_sems, last_sems, conv_sems, turn_sems, local_sems,
):
    step_id = pl.program_id(0)
    block = pl.num_programs(0) - 1 - step_id
    own = own_heads * hd
    slots, _, dim = w_ref.shape
    taps = convs_ref.shape[2]
    conv_cols = conv_ref.shape[2] // 2
    slot_heads = heads // slots
    lanes = slot_heads * hd
    factor = 1.0 / math.sqrt(hd)
    scale = LOG2E * factor
    swap = Swap(staged, tokens_ref, tokens_peer, swap_sems, swap_local)
    middle = Spread(middle_ref, middle_in, middle_sum, middle_sems, local_sems.at[0])
    last = Spread(last_parts, last_in, last_sum, last_sems, local_sems.at[1])
    convs = Spread(conv_parts, conv_in, conv_sum, conv_sems, local_sems.at[2])

    def mixed_tail():
        rows = mixed_ref.shape[0]
        return remote(mixed_ref.at[rows - TB : rows], mixed_last, turn_sems, (3,), swap.device)

    def turned(n, ref):
        return remote(ref.at[0], ref.at[1], turn_sems, (n,), swap.device)

    def turn(n, ref, total):
        ref[0] = total[:, total.shape[1] - ref.shape[2] :].astype(BF16)
        turned(n, ref).start()

    @pl.when(step_id == 0)
    def _():
        count = lax.axis_size("dp")
        meet([swap.device] + [(lax.rem(lax.axis_index("dp") + s, count), lax.axis_index("tensor")) for s in range(1, count)])
        mixed_tail().start()
        middle.start()
        for h in range(heads):
            slot, i = divmod(h, slot_heads)
            for n in range(2):
                conv = conv_ref[slot, i * hd : (i + 1) * hd, n * conv_cols : n * conv_cols + taps]
                convs_ref[n, h] = conv.astype(F32).T.astype(BF16)
        dck_sum[...] = jnp.zeros_like(dck_sum)
        dcv_sum[...] = jnp.zeros_like(dcv_sum)
        weight_sum[...] = jnp.zeros_like(weight_sum)
        kconv_sum[...] = jnp.zeros_like(kconv_sum)
        vconv_sum[...] = jnp.zeros_like(vconv_sum)
        gain_sum[...] = jnp.zeros_like(gain_sum)

    longest_here = lax.rem(lax.axis_index("tensor"), 2) == 0
    places, starts = item_starts(lens_ref, block, longest_here, ck_ref.shape[1])

    def attend(count):
        keys = slice(0, count * GB)
        put_bias(bias_ref, places, starts, count)

        def head(h, band, one):
            q, dctx = q_ref[band, :], dctx_ref[band, :]
            s = nn(ck_ref[h, keys, :], q) * scale + jnp.concatenate([bias_ref[keys, :]] * 3, axis=1)
            p = jnp.exp2(s - lse_ref[one, :])
            dp = nn(cv_ref[h, keys, :], dctx)
            ds = (p * (dp - delta_ref[one, :])).astype(BF16)
            dcv_sum[h, keys, :] += nt(p.astype(BF16), dctx)
            dck_sum[h, keys, :] += nt(ds, q)
            dq_sum[band, :] = nn(ckt_ref[band, keys], ds)

        each_head(heads, hd, head)

    for n in range(ck_ref.shape[1] // GB):
        pl.when(block == n)(functools.partial(attend, n + 1))
    mask = lse_ref[heads : heads + 1, :]
    rows = key_rows(block)
    for h in range(heads):
        band = slice(h * hd, (h + 1) * hd)
        one = slice(h, h + 1)
        q, k = q_ref[band, :].astype(F32), k_ref[band, :].astype(F32)
        v, dctx = v_ref[band, :].astype(F32), dctx_ref[band, :].astype(F32)
        own_prob = jnp.exp2(jnp.sum(q * k, axis=0, keepdims=True) * scale - lse_ref[one, :])
        own_dprob = jnp.sum(dctx * v, axis=0, keepdims=True)
        own_dscore = own_prob * (own_dprob - delta_ref[one, :]) * factor
        slot, i = divmod(h, slot_heads)
        base = slot * 3 * lanes + i * hd
        dqkv[base : base + hd, :] = (dq_sum[band, :] * factor + own_dscore * k).astype(BF16)
        dck = (dck_sum[h, rows, :] * factor).astype(BF16)
        dcv = dcv_sum[h, rows, :].astype(BF16)
        for n, src, total, grad, beside in (
            (0, k_ref, kconv_sum, dck, own_dscore * q),
            (1, v_ref, vconv_sum, dcv, own_prob * dctx),
        ):
            spread = nt(convs_ref[n, h], grad)
            spread = jnp.concatenate([spread[r * hd : (r + 1) * hd] for r in range(3)], axis=1)
            at = base + (n + 1) * lanes
            dqkv[at : at + hd, :] = ((spread + beside) * mask).astype(BF16)
            if h < own_heads:
                grouped = jnp.concatenate([src[band, r * GB : (r + 1) * GB] for r in range(3)], axis=0)
                total[h] += nn(grouped, grad)
    hat, inv_std = norm_rows(x_ref[...].astype(F32))
    gain = gain_ref[...]
    first_in = (hat * gain).astype(BF16)
    weight_sum[...] += nn(dqkv[0 : 3 * own, :], first_in)
    back = tn(dqkv[...], w_ref[...].reshape(slots * 3 * lanes, dim))
    gain_sum[...] += jnp.sum(back * hat, axis=0, keepdims=True)
    total = resid_grad_ref[...].astype(F32) + norm_back(back, gain, hat, inv_std)
    swap.send(step_id, block, total.astype(BF16))

    @pl.when(block == 1)
    def _():
        turn(0, middle_turn, middle.total())

    @pl.when(block == 0)
    def _():
        put_rows(last_parts, [weight_sum[...].T, jnp.broadcast_to(gain_sum[...], (GB, dim)).T])
        last.start()
        put_rows(
            conv_parts,
            [
                total[h]
                for slot in range(2)
                for total in (kconv_sum, vconv_sum)
                for h in range(slot * slot_heads, (slot + 1) * slot_heads)
            ],
        )
        convs.start()
        last_total = last.total()
        turn(1, last_turn, last_total)
        conv_total = convs.total()
        turn(2, conv_turn, conv_total)
        for n, (out, ref, total) in enumerate(
            ((middle_out, middle_turn, middle_sum), (last_out, last_turn, last_total), (conv_out, conv_turn, conv_total))
        ):
            turned(n, ref).wait()
            cols = out.shape[1]
            split = total.shape[1] - cols
            kept = [total[:, :split]] + ([total[:, 2 * split :]] if cols > split else [])
            out[...] = ref[1].astype(F32) + jnp.concatenate(kept, axis=1)
        swap.finish(block, swap.blocks)
        mixed_tail().wait()


def place_rows(lens_ref, longest_here, mine, theirs, theirs_last, natural, out_ref):
    half = mine.shape[0]
    first = longest_first(lens_ref, half // 3)

    def taps(block, r, other):
        rows = slice(block * TB + r * GB, block * TB + (r + 1) * GB)
        apart = theirs_last is not None and (block + 1) * TB == half
        a = mine[rows, :].astype(F32)
        b = (theirs_last[r * GB : (r + 1) * GB, :] if apart else theirs[rows, :]).astype(F32)
        return jnp.where(longest_here == other, b, a)

    for block in range(half // TB):
        for r in range(3):
            others = taps(block, r, True)
            for base in (0, half):
                natural[pl.ds(base + block * TB + r, GB, stride=3), :] = others
    for block in range(half // TB):
        for r in range(3):
            natural[pl.ds(first + block * TB + r, GB, stride=3), :] = taps(block, r, False)
    out_ref[...] = natural[...].astype(BF16)


def last_kernel(
    hd, lens_ref, mixed_last, mixed_ref, mixed_peer, tokens_ref, tokens_peer, middle_ref, last_ref, conv_ref,
    mixed_out, tokens_out, gain1_out, gain2_out, query_out, key_out, value_out, out_out, kconv_out, vconv_out,
    up_out, down_out, natural_mixed, natural_tokens,
):
    longest_here = lax.rem(lax.axis_index("tensor"), 2) == 0
    place_rows(lens_ref, longest_here, mixed_ref, mixed_peer, mixed_last, natural_mixed, mixed_out)
    place_rows(lens_ref, longest_here, tokens_ref, tokens_peer, None, natural_tokens, tokens_out)

    @pl.when(pl.program_id(0) == 0)
    def _():
        units, own = up_out.shape[1], query_out.shape[1]
        up_out[...] = middle_ref[:, 0:units]
        down_out[...] = middle_ref[:, units : 2 * units]
        out_out[...] = middle_ref[:, 2 * units : 2 * units + own]
        gain2_out[...] = middle_ref[:, 2 * units + own :].T[0:1]
        for n, out in enumerate((query_out, key_out, value_out)):
            out[...] = last_ref[:, n * own : (n + 1) * own]
        gain1_out[...] = last_ref[:, 3 * own :].T[0:1]
        for n, out in enumerate((kconv_out, vconv_out)):
            for h in range(out.shape[0]):
                out[h] = conv_ref[:, n * own + h * hd : n * own + (h + 1) * hd]


def whole(shape):
    return pl.BlockSpec(shape, lambda *_: (0,) * len(shape))


def cost(micros):
    return pl.CostEstimate(flops=int(micros * 1e9), bytes_accessed=1 << 20, transcendentals=0)


def params():
    return pltpu.CompilerParams(vmem_limit_bytes=VMEM, dimension_semantics=("arbitrary",))


def on_device(
    tokens, first_gain, second_gain, query_weight, key_weight, value_weight, out_weight,
    key_conv, value_conv, up_weight, down_weight, pad_mask, item_lengths, cotangent,
):
    dim = tokens.shape[1]
    own_heads, taps, hd = key_conv.shape
    peers = lax.axis_size("tensor")
    heads = own_heads * peers
    width = heads * hd
    own = own_heads * hd
    units = up_weight.shape[1]
    lens = item_lengths[0]
    rows = tokens.shape[0] // 2
    blocks = rows // TB
    groups = rows // 3
    pads = pad_mask.reshape(-1, 128)
    key_conv, value_conv = key_conv.transpose(0, 2, 1), value_conv.transpose(0, 2, 1)
    conv_cols = -(-taps // 128) * 128
    stats = heads + 8
    gain1, gain2 = first_gain[None], second_gain[None]

    rows_spec = pl.BlockSpec((TB, dim), lambda b, *_: (b, 0))
    cols_spec = pl.BlockSpec((width, TB), lambda b, *_: (0, b))
    stat_spec = pl.BlockSpec((heads, TB), lambda b, *_: (0, b))
    lse_spec = pl.BlockSpec((stats, TB), lambda b, *_: (0, b))
    anywhere = pl.BlockSpec(memory_space=pl.ANY)
    inside = pl.BlockSpec(memory_space=pltpu.VMEM)
    x, g, q, k, v, ctx, lse, ck, ckt, cv, w_all, conv_all, out_far, up_far, down_far = pl.pallas_call(
        functools.partial(forward_kernel, heads, hd),
        grid_spec=pltpu.PrefetchScalarGridSpec(
            num_scalar_prefetch=1,
            grid=(blocks,),
            in_specs=[inside, inside, whole((1, dim))] + [inside] * 6 + [anywhere] * 3,
            out_specs=[
                whole((rows, dim)), whole((rows, dim)), cols_spec, cols_spec, cols_spec, cols_spec, lse_spec,
                whole((heads, groups, hd)), whole((width, groups)), whole((heads, groups, hd)),
                anywhere, anywhere, anywhere, anywhere, anywhere,
            ],
            scratch_shapes=[
                pltpu.VMEM((dim // 128 + 1, 2 * rows, 128), F32), pltpu.VMEM((dim // 128, 2 * rows, 128), F32),
                pltpu.VMEM((blocks, TB, dim), BF16), pltpu.VMEM((blocks, 8, TB), F32),
                pltpu.VMEM((peers, 3 * own, dim), BF16), pltpu.VMEM((peers, own, 2 * conv_cols), BF16),
                pltpu.VMEM((width, groups), BF16), pltpu.VMEM((groups, GB), F32),
                pltpu.SemaphoreType.DMA((2, 2, 5, peers - 1)), pltpu.SemaphoreType.DMA((2, 3, 5, peers - 1)),
                pltpu.SemaphoreType.DMA((2,)),
            ],
        ),
        out_shape=[jax.ShapeDtypeStruct((rows, dim), BF16)] * 2
        + [jax.ShapeDtypeStruct((width, rows), BF16)] * 4
        + [
            jax.ShapeDtypeStruct((stats, rows), F32),
            jax.ShapeDtypeStruct((heads, groups, hd), BF16),
            jax.ShapeDtypeStruct((width, groups), BF16),
            jax.ShapeDtypeStruct((heads, groups, hd), BF16),
            jax.ShapeDtypeStruct((peers, 3 * own, dim), BF16),
            jax.ShapeDtypeStruct((peers, own, 2 * conv_cols), BF16),
            jax.ShapeDtypeStruct((peers - 1, own, dim), BF16),
            jax.ShapeDtypeStruct((peers - 1, dim, units), BF16),
            jax.ShapeDtypeStruct((peers - 1, units, dim), BF16),
        ],
        compiler_params=pltpu.CompilerParams(
            vmem_limit_bytes=VMEM, dimension_semantics=("arbitrary",), collective_id=0, has_side_effects=True
        ),
        cost_estimate=cost(55),
        name="attention_forward",
    )(
        lens, tokens, cotangent, gain1, pads, query_weight, key_weight, value_weight, key_conv, value_conv,
        out_weight, up_weight, down_weight,
    )

    count = lax.axis_size("dp")
    slot_cols = 2 * units + own
    mid_cols = 2 * slot_cols + GB
    step = 256
    mixed, mixed_peer, resid_grad, dctx, delta, middle_grads = pl.pallas_call(
        functools.partial(middle_kernel, heads, hd),
        grid=(blocks,),
        in_specs=[
            rows_spec, rows_spec, whole((1, dim)), cols_spec, whole((own, dim)),
            whole((dim, units)), whole((units, dim)), whole((width - own, dim)),
            whole((peers - 1, dim, units)), whole((peers - 1, units, dim)),
        ],
        out_specs=[anywhere, anywhere, rows_spec, cols_spec, stat_spec, whole((count, dim // count, mid_cols))],
        out_shape=[
            jax.ShapeDtypeStruct((rows, dim), BF16),
            jax.ShapeDtypeStruct((rows, dim), BF16),
            jax.ShapeDtypeStruct((rows, dim), BF16),
            jax.ShapeDtypeStruct((width, rows), BF16),
            jax.ShapeDtypeStruct((heads, rows), F32),
            jax.ShapeDtypeStruct((count, dim // count, mid_cols), BF16),
        ],
        scratch_shapes=[
            pltpu.VMEM((2, TB, dim), BF16), pltpu.VMEM((TB, peers * units), BF16), pltpu.VMEM((TB, peers * units), BF16),
            pltpu.VMEM((2, TB, step), F32), pltpu.VMEM((2, TB, step), F32),
            pltpu.VMEM((blocks, TB, 2 * units), BF16), pltpu.VMEM((blocks, TB, 2 * units), BF16),
            pltpu.VMEM((blocks, TB, dim), BF16), pltpu.VMEM((blocks, TB, dim), BF16),
            pltpu.VMEM((2 * own, dim), F32), pltpu.VMEM((1, dim), F32),
            pltpu.SemaphoreType.DMA((2, blocks)), pltpu.SemaphoreType.DMA((blocks,)),
        ],
        compiler_params=pltpu.CompilerParams(
            vmem_limit_bytes=VMEM, dimension_semantics=("arbitrary",), collective_id=1, has_side_effects=True
        ),
        cost_estimate=cost(55),
        name="feed_forward",
    )(x, g, gain2, ctx, out_weight, up_weight, down_weight, out_far.reshape(width - own, dim), up_far, down_far)

    back_rows = pl.BlockSpec((TB, dim), lambda b, *_: (blocks - 1 - b, 0))
    back_cols = pl.BlockSpec((width, TB), lambda b, *_: (0, blocks - 1 - b))
    back_stat = pl.BlockSpec((heads, TB), lambda b, *_: (0, blocks - 1 - b))
    back_lse = pl.BlockSpec((stats, TB), lambda b, *_: (0, blocks - 1 - b))
    two = 2 * own_heads
    last_cols = 6 * own + GB
    out_dims = [(dim // count, slot_cols + GB), (dim // count, 3 * own + GB), (taps // count, 2 * own)]
    grad_rows, grad_peer, mixed_last, middle_share, last_share, conv_share = pl.pallas_call(
        functools.partial(backward_kernel, heads, hd, two),
        grid_spec=pltpu.PrefetchScalarGridSpec(
            num_scalar_prefetch=1,
            grid=(blocks,),
            in_specs=[
                back_rows, whole((1, dim)), whole((peers, 3 * own, dim)), whole((peers, own, 2 * conv_cols)),
                back_cols, back_cols, back_cols, back_lse,
                back_cols, back_stat, back_rows, whole((heads, groups, hd)), whole((width, groups)),
                whole((heads, groups, hd)), anywhere, anywhere,
            ],
            out_specs=[anywhere] * 3 + [whole(d) for d in out_dims],
            scratch_shapes=[
                pltpu.VMEM((2, TB, dim), BF16), pltpu.VMEM((groups, GB), F32),
                pltpu.VMEM((2, heads, taps, hd), BF16), pltpu.VMEM((heads, groups, hd), F32),
                pltpu.VMEM((heads, groups, hd), F32), pltpu.VMEM((width, TB), F32),
                pltpu.VMEM((3 * width, TB), BF16), pltpu.VMEM((6 * own, dim), F32),
                pltpu.VMEM((two, taps, hd), F32), pltpu.VMEM((two, taps, hd), F32),
                pltpu.VMEM((1, dim), F32),
                pltpu.VMEM((count, dim // count, mid_cols), BF16),
                pltpu.VMEM((count, dim // count, last_cols), BF16), pltpu.VMEM((count, dim // count, last_cols), BF16),
                pltpu.VMEM((count, taps // count, 4 * own), BF16), pltpu.VMEM((count, taps // count, 4 * own), BF16),
            ]
            + [pltpu.VMEM((2, *d), BF16) for d in out_dims]
            + [
                pltpu.VMEM((dim // count, mid_cols), F32), pltpu.VMEM((dim // count, last_cols), F32),
                pltpu.VMEM((taps // count, 4 * own), F32),
            ]
            + [
                pltpu.SemaphoreType.DMA((2, blocks)), pltpu.SemaphoreType.DMA((blocks,)),
                pltpu.SemaphoreType.DMA((2, count)), pltpu.SemaphoreType.DMA((2, count)),
                pltpu.SemaphoreType.DMA((2, count)), pltpu.SemaphoreType.DMA((2, 4)), pltpu.SemaphoreType.DMA((3,)),
            ],
        ),
        out_shape=[jax.ShapeDtypeStruct((rows, dim), BF16)] * 2
        + [jax.ShapeDtypeStruct((TB, dim), BF16)]
        + [jax.ShapeDtypeStruct(d, F32) for d in out_dims],
        compiler_params=pltpu.CompilerParams(
            vmem_limit_bytes=VMEM, dimension_semantics=("arbitrary",), collective_id=2, has_side_effects=True
        ),
        cost_estimate=cost(60),
        name="attention_backward",
    )(lens, x, gain1, w_all, conv_all, q, k, v, lse, dctx, delta, resid_grad, ck, ckt, cv, middle_grads, mixed)

    share = dim // count
    own_conv = (own_heads, taps // count, hd)
    shapes = [
        ((1, share), F32), ((1, share), F32), ((share, own), F32), ((share, own), F32), ((share, own), F32),
        ((share, own), F32), (own_conv, F32), (own_conv, F32), ((share, units), F32), ((share, units), F32),
    ]
    lane_half = pl.BlockSpec((rows, 128), lambda c: (0, c))
    lane_all = pl.BlockSpec((2 * rows, 128), lambda c: (0, c))
    outs = pl.pallas_call(
        functools.partial(last_kernel, hd),
        grid=(dim // 128,),
        in_specs=[pl.BlockSpec(memory_space=pltpu.SMEM), pl.BlockSpec((TB, 128), lambda c: (0, c))]
        + [lane_half] * 4
        + [whole(d) for d in out_dims],
        out_specs=[lane_all] * 2 + [whole(d) for d, _ in shapes],
        out_shape=[jax.ShapeDtypeStruct((2 * rows, dim), BF16)] * 2 + [jax.ShapeDtypeStruct(d, t) for d, t in shapes],
        scratch_shapes=[pltpu.VMEM((2 * rows, 128), F32)] * 2,
        compiler_params=params(),
        cost_estimate=cost(15),
        name="in_order",
    )(lens, mixed_last, mixed, mixed_peer, grad_rows, grad_peer, middle_share, last_share, conv_share)
    mixed, grad_tokens, gain1, gain2, query, key, value, out, kconv, vconv, up, down = outs
    return (
        mixed, grad_tokens, gain1.reshape(share), gain2.reshape(share), query, key, value, out.T,
        kconv, vconv, up, down.T,
    )


def solution(mesh):
    in_specs = (
        P("dp", None),
        P(),
        P(),
        P(None, "tensor"),
        P(None, "tensor"),
        P(None, "tensor"),
        P("tensor", None),
        P("tensor", None, None),
        P("tensor", None, None),
        P(None, "tensor"),
        P("tensor", None),
        P("dp"),
        P("dp", None),
        P("dp", None),
    )
    out_specs = (
        P("dp", None),
        P("dp", None),
        P("dp"),
        P("dp"),
        P("dp", "tensor"),
        P("dp", "tensor"),
        P("dp", "tensor"),
        P("tensor", "dp"),
        P("tensor", "dp", None),
        P("tensor", "dp", None),
        P("dp", "tensor"),
        P("tensor", "dp"),
    )
    return jax.shard_map(
        on_device, mesh=mesh, in_specs=in_specs, out_specs=out_specs, check_vma=False
    )
```

```python
import functools
import math

import jax
import jax.numpy as jnp
from jax import lax
from jax.experimental import pallas as pl
from jax.experimental.pallas import tpu as pltpu
from jax.sharding import PartitionSpec as P

F32 = jnp.float32
BF16 = jnp.bfloat16
GB = 128
TB = 3 * GB
NEG = -1e30
LOG2E = 1.0 / math.log(2.0)
VMEM = 60 * 1024 * 1024

ERF_P = 0.43
ERF_C = (
    0.24255178053871013,
    0.24376598744271377,
    0.2089868288055898,
    0.23281685899157548,
    -0.05797941172752005,
    0.3523368029188165,
    -0.2915198548110903,
    0.06904073943922798,
)


def nn(a, b):
    return lax.dot_general(a, b, (((1,), (0,)), ((), ())), preferred_element_type=F32)


def nt(a, b):
    return lax.dot_general(a, b, (((1,), (1,)), ((), ())), preferred_element_type=F32)


def tn(a, b):
    return lax.dot_general(a, b, (((0,), (0,)), ((), ())), preferred_element_type=F32)


def norm_rows(values):
    centred = values - jnp.mean(values, -1, keepdims=True)
    inv_std = lax.rsqrt(jnp.mean(centred * centred, -1, keepdims=True) + 1e-05)
    return centred * inv_std, inv_std


def norm_back(grad_out, gains, normed, inv_std):
    scaled = grad_out * gains
    return inv_std * (
        scaled
        - jnp.mean(scaled, -1, keepdims=True)
        - normed * jnp.mean(scaled * normed, -1, keepdims=True)
    )


def gelu_and_slope(h):
    t = 1.0 / (1.0 + (ERF_P * math.sqrt(0.5)) * jnp.abs(h))
    poly = t * (0.5 * ERF_C[-1]) + 0.5 * ERF_C[-2]
    for c in ERF_C[-3::-1]:
        poly = poly * t + 0.5 * c
    e = jnp.exp2((h * h) * (-0.5 * LOG2E))
    tail = e * (poly * t)
    cdf = jnp.where(h >= 0, 1.0 - tail, tail)
    return h * cdf, cdf + h * (e * (1.0 / math.sqrt(2.0 * math.pi)))


def item_starts(lens_ref, block, longest_here, half):
    places = block * GB + lax.broadcasted_iota(jnp.int32, (1, GB), 1)
    starts = jnp.zeros((1, GB), jnp.int32)
    end = jnp.int32(0)
    for i in range(lens_ref.shape[0] - 1):
        end = end + jnp.where((lens_ref[i] == half) == longest_here, lens_ref[i], 0)
        starts = jnp.where(places >= end, end, starts)
    return places, starts


def longest_first(lens_ref, half):
    first, ahead = jnp.int32(0), jnp.int32(1)
    for i in range(lens_ref.shape[0]):
        ahead = jnp.where(lens_ref[i] == half, 0, ahead)
        first = first + ahead * lens_ref[i]
    return 3 * first


def own_taps(source, block, first, longest_here):
    half = source.shape[1] // 2
    base = block * TB
    parts = []
    for c in range(source.shape[0]):
        for r in range(3):
            inside = source[c, pl.ds(first + base + r, GB, stride=3), :]
            low = source[c, pl.ds(base + r, GB, stride=3), :]
            high = source[c, pl.ds(half + base + r, GB, stride=3), :]
            place = base + r + 3 * lax.broadcasted_iota(jnp.int32, (GB, 1), 0)
            parts.append(jnp.where(longest_here, inside, jnp.where(place < first, low, high)))
    return jnp.concatenate(
        [jnp.concatenate(parts[3 * c : 3 * c + 3], axis=0) for c in range(source.shape[0])], axis=1
    )


def put_bias(bias_ref, places, starts, count):
    for kb in range(count):
        keys = kb * GB + lax.broadcasted_iota(jnp.int32, (GB, GB), 0)
        bias_ref[kb * GB : (kb + 1) * GB, :] = jnp.where((keys >= starts) & (keys < places), 0.0, NEG)


def each_head(heads, hd, work):
    def some(i, carry):
        for n in range(2):
            h = 2 * i + n
            work(h, pl.ds(pl.multiple_of(h * hd, hd), hd), pl.ds(h, 1))
        return carry

    lax.fori_loop(0, heads // 2, some, 0)


def key_rows(kb):
    return pl.ds(pl.multiple_of(kb * GB, GB), GB)


def remote(src, dst, sems, at, device):
    return pltpu.make_async_remote_copy(
        src_ref=src, dst_ref=dst, send_sem=sems.at[(0, *at)], recv_sem=sems.at[(1, *at)],
        device_id=device, device_id_type=pl.DeviceIdType.MESH,
    )


def meet(devices):
    barrier = pltpu.get_barrier_semaphore()
    for device in devices:
        pl.semaphore_signal(barrier, inc=1, device_id=device, device_id_type=pl.DeviceIdType.MESH)
    pl.semaphore_wait(barrier, len(devices))


def put_rows(ref, pieces, at=0):
    parities, count, rows, _ = ref.shape
    for piece in pieces:
        cols = piece.shape[1]
        for d in range(parities * count):
            ref[d % 2, d // 2, :, at : at + cols] = piece[d * rows : (d + 1) * rows].astype(ref.dtype)
        at += cols


class Swap:
    def __init__(self, staged, mine, theirs, sems, local_sems):
        self.staged, self.mine, self.theirs, self.sems, self.local_sems = staged, mine, theirs, sems, local_sems
        self.device = (lax.axis_index("dp"), lax.axis_index("tensor") ^ 1)
        self.blocks = mine.shape[0] // TB

    def rows(self, block):
        return pl.ds(pl.multiple_of(block * TB, TB), TB)

    def local(self, block):
        return pltpu.make_async_copy(
            self.staged.at[block], self.mine.at[self.rows(block)], self.local_sems.at[block]
        )

    def far(self, block):
        return remote(
            self.staged.at[block], self.theirs.at[self.rows(block)], self.sems, (block,), self.device
        )

    def send(self, block, values):
        self.staged[block] = values
        self.local(block).start()
        self.far(block).start()

    def finish(self):
        for block in range(self.blocks):
            self.local(block).wait()
            self.far(block).wait()


class Spread:
    def __init__(self, source, paired, landed, sums, sems):
        self.source, self.paired, self.landed, self.sums, self.sems = source, paired, landed, sums, sems
        self.me, self.peer = lax.axis_index("dp"), lax.axis_index("tensor")
        self.parity = lax.rem(self.me, 2)
        self.count = lax.axis_size("dp")

    def beside(self):
        return remote(
            self.source.at[1 - self.parity], self.paired, self.sems, (0,), (self.me ^ 1, self.peer)
        )

    def copy(self, s):
        there = lax.rem(self.me + 2 * s, self.count)
        return remote(self.paired.at[there // 2], self.landed.at[s], self.sems, (s,), (there, self.peer))

    def start(self):
        self.beside().start()

    def pass_on(self):
        self.beside().wait()

        def add(n, carry):
            pair = self.paired[n].astype(F32) + self.source[self.parity, n].astype(F32)
            self.paired[n] = pair.astype(BF16)
            return carry

        lax.fori_loop(0, self.count // 2, add, 0)

        def step(s, carry):
            self.copy(s).start()
            return carry

        lax.fori_loop(1, self.count // 2, step, 0)

    def total(self):
        def step(s, carry):
            self.copy(s).wait()
            return carry

        lax.fori_loop(1, self.count // 2, step, 0)
        self.sums[...] = self.paired[self.me // 2].astype(F32)

        def add(s, carry):
            self.sums[...] += self.landed[s].astype(F32)
            return carry

        lax.fori_loop(1, self.count // 2, add, 0)
        return self.sums


class Gather:
    def __init__(self, own, far, sems):
        self.own, self.far, self.sems = own, far, sems
        self.dp, self.tensor = lax.axis_index("dp"), lax.axis_index("tensor")
        self.peers = lax.axis_size("tensor")

    def devices(self):
        return [(self.dp, self.tensor ^ s) for s in range(1, self.peers)] + [
            (self.dp ^ m, self.tensor) for m in (1, 2, 4, 6)
        ]

    def eighth(self, array):
        rows = array.shape[0] // 8
        place = lax.rem(self.dp, 2) * 4 + lax.rem(self.dp, 8) // 2
        return array.at[pl.ds(pl.multiple_of(place * rows, rows), rows)]

    def half(self, array):
        rows = array.shape[0] // 2
        return array.at[pl.ds(pl.multiple_of(lax.rem(self.dp, 2) * rows, rows), rows)]

    def across(self, n, s):
        device = (self.dp, self.tensor ^ s)
        return remote(
            self.eighth(self.own[n]), self.eighth(self.far[n].at[s - 1]), self.sems, (n, 0, s - 1), device
        )

    def around(self, n, s, m):
        part = self.eighth(self.far[n].at[s - 1])
        return remote(part, part, self.sems, (n, m // 2, s - 1), (self.dp ^ m, self.tensor))

    def beside(self, n, s):
        part = self.half(self.far[n].at[s - 1])
        return remote(part, part, self.sems, (n, 4, s - 1), (self.dp ^ 1, self.tensor))

    def each(self, s=None):
        peers = range(1, self.peers) if s is None else (s,)
        return [(n, s) for s in peers for n in range(len(self.far))]

    def start(self):
        for n, s in self.each():
            self.across(n, s).start()

    def pass_around(self, s=None):
        for n, s in self.each(s):
            self.across(n, s).wait_recv()
            for m in (6, 4, 2):
                self.around(n, s, m).start()

    def pass_beside(self, s=None):
        for n, s in self.each(s):
            for m in (2, 4, 6):
                self.around(n, s, m).wait_recv()
            self.beside(n, s).start()

    def arrive(self):
        for n, s in self.each():
            self.beside(n, s).wait_recv()

    def finish(self):
        for n, s in self.each():
            self.across(n, s).wait_send()
            for m in (2, 4, 6):
                self.around(n, s, m).wait_send()
            self.beside(n, s).wait_send()


def attend_forward(
    heads, hd, count, places, starts, bias_ref, ck_ref, cvt_ref, q_ref, k_ref, v_ref, ctx_ref, put_lse
):
    scale = LOG2E / math.sqrt(hd)
    keys = slice(0, count * GB)
    put_bias(bias_ref, places, starts, count)

    def head(h, band, one):
        q = q_ref[band, :]
        own_score = jnp.sum(q.astype(F32) * k_ref[band, :].astype(F32), axis=0, keepdims=True) * scale
        s = nn(ck_ref[h, keys, :], q) * scale + jnp.concatenate([bias_ref[keys, :]] * 3, axis=1)
        top = jnp.maximum(own_score, jnp.max(s, axis=0, keepdims=True))
        p = jnp.exp2(s - top)
        own_prob = jnp.exp2(own_score - top)
        total = own_prob + jnp.sum(p, axis=0, keepdims=True)
        mixed = own_prob * v_ref[band, :].astype(F32) + nn(cvt_ref[band, keys], p.astype(BF16))
        ctx_ref[band, :] = (mixed * (1.0 / total)).astype(BF16)
        put_lse(one, top + jnp.log(total) * LOG2E)

    each_head(heads, hd, head)


def forward_kernel(
    heads, hd, lens_ref, x_ref, g_ref, gain_ref, pad_ref, query_ref, key_ref, value_ref, kconv_ref, vconv_ref,
    out_ref, up_ref, down_ref,
    x_own, g_own, q_ref, k_ref, v_ref, ctx_ref, lse_ref, ck_ref, ckt_ref, cv_ref, cvt_ref, w_all, conv_all,
    out_far, up_far, down_far,
    xs, gs, first_all, mask_rows, w_ref, conv_ref, bias_ref, first_sems, last_sems, local_sems,
):
    block = pl.program_id(0)
    blocks = pl.num_programs(0)
    own_heads, _, taps = kconv_ref.shape
    own = own_heads * hd
    dim = x_ref.shape[1]
    conv_cols = conv_ref.shape[2] // 2
    first_gather = Gather((w_ref.at[0], conv_ref.at[0]), (w_ref.at[1:], conv_ref.at[1:]), first_sems)
    last_gather = Gather((out_ref, up_ref, down_ref), (out_far, up_far, down_far), last_sems)
    keep_copies = [
        pltpu.make_async_copy(w_ref, w_all, local_sems.at[0]), pltpu.make_async_copy(conv_ref, conv_all, local_sems.at[1])
    ]

    half = x_ref.shape[0] // 2
    blocks_there = half // TB
    longest_here = lax.rem(lax.axis_index("tensor"), 2) == 0
    first = longest_first(lens_ref, half // 3)

    @pl.when(block == 0)
    def _():
        for n, src in enumerate((query_ref, key_ref, value_ref)):
            w_ref[0, n * own : (n + 1) * own, :] = src[...].T
        conv_ref[0] = jnp.zeros_like(conv_ref[0])
        for n, src in enumerate((kconv_ref, vconv_ref)):
            for h in range(own_heads):
                conv_ref[0, h * hd : (h + 1) * hd, n * conv_cols : n * conv_cols + taps] = src[h]
        meet(first_gather.devices())
        first_gather.start()
        for src, dst in ((x_ref, xs), (g_ref, gs)):
            for c in range(dim // 128):
                dst[c] = src[:, c * 128 : (c + 1) * 128].astype(F32)
        pads = pad_ref[...].astype(F32).T
        for c in range(pads.shape[1]):
            xs[dim // 128, c * 128 : (c + 1) * 128, :] = jnp.broadcast_to(pads[:, c : c + 1], (128, 128))
        first_gather.pass_around()
        last_gather.start()

        def prepare(n, carry):
            x = own_taps(xs, n, first, longest_here)
            mask_rows[n] = jnp.broadcast_to(x[:, dim:].T[0:1], mask_rows.shape[1:])
            x = x[:, :dim]
            normed, _ = norm_rows(x)
            first_all[n] = (normed * gain_ref[...]).astype(BF16)
            rows = pl.ds(pl.multiple_of(n * TB, TB), TB)
            x_own[rows, :] = x.astype(BF16)
            g_own[rows, :] = own_taps(gs, n, first, longest_here).astype(BF16)
            return carry

        lax.fori_loop(0, half // TB // 2, prepare, 0)
        first_gather.pass_beside()
        lax.fori_loop(half // TB // 2, half // TB, prepare, 0)
        first_gather.arrive()
        first_gather.finish()
        for copy in keep_copies:
            copy.start()

    mask = mask_rows[block, 0:1]
    first_in = first_all[block]
    for slot in range(w_ref.shape[0]):
        at = slice(slot * own, (slot + 1) * own)
        part = nt(w_ref[slot], first_in)
        q_ref[at, :] = part[0:own].astype(BF16)
        k_ref[at, :] = (part[own : 2 * own] * mask).astype(BF16)
        v_ref[at, :] = (part[2 * own : 3 * own] * mask).astype(BF16)
    rows = key_rows(block)
    for h in range(heads):
        band = slice(h * hd, (h + 1) * hd)
        slot, i = divmod(h, own_heads)
        for n, src, plain, trans in ((0, k_ref, ck_ref, ckt_ref), (1, v_ref, cv_ref, cvt_ref)):
            grouped = jnp.concatenate([src[band, r * GB : (r + 1) * GB] for r in range(3)], axis=0)
            comp = nn(conv_ref[slot, i * hd : (i + 1) * hd, n * conv_cols : n * conv_cols + taps], grouped)
            trans[band, rows] = comp.astype(BF16)
            plain[h, rows, :] = comp.T.astype(BF16)
    places, starts = item_starts(lens_ref, block, longest_here, half // 3)
    lse_ref[heads:, :] = jnp.broadcast_to(mask, (lse_ref.shape[0] - heads, TB))

    peers = w_ref.shape[0]
    for s in range(1, peers):
        pl.when(block == s - 1)(functools.partial(last_gather.pass_around, s))
        if s < peers - 1:
            pl.when(block == blocks_there - peers + 1 + s)(functools.partial(last_gather.pass_beside, s))

    @pl.when(block < blocks // 2)
    def _():
        lse_ref[0:heads, :] = jnp.zeros_like(lse_ref[0:heads, :])

    def put_lse(one, values):
        lse_ref[one, :] = values

    for n in range(blocks_there // 2, blocks_there):
        pl.when(block == n)(
            functools.partial(
                attend_forward, heads, hd, n + 1, places, starts, bias_ref, ck_ref, cvt_ref, q_ref, k_ref, v_ref,
                ctx_ref, put_lse,
            )
        )

    @pl.when(block == blocks - 1)
    def _():
        last_gather.pass_beside(w_ref.shape[0] - 1)

    @pl.when(block == blocks - 1)
    def _():
        last_gather.arrive()
        last_gather.finish()
        for copy in keep_copies:
            copy.wait()


def feed_forward(
    heads, hd, block, swap, x_ref, g_ref, gain_ref, ctx_ref, out_ref, up_ref, down_ref,
    out_far, up_far, down_far, resid_all, dctx_all, delta_all, grads_ref,
    acts, hidden_grads, pre, act_grads, ff_sum, out_sum, gain_sum,
):
    own, two = out_ref.shape[0], out_sum.shape[0]
    units = up_ref.shape[1]
    step = pre.shape[2]
    slots = up_far.shape[0] + 1
    gain = gain_ref[...]
    g_low = g_ref[...]
    resid = x_ref[...].astype(F32) + tn(ctx_ref[0:own, :], out_ref[...]) + tn(ctx_ref[own:, :], out_far[...])
    hat, inv_std = norm_rows(resid)
    second_in = (hat * gain).astype(BF16)

    def up(slot, cols=slice(None)):
        return up_ref[:, cols] if slot == 0 else up_far[slot - 1, :, cols]

    def down(slot, rows=slice(None)):
        return down_ref[rows, :] if slot == 0 else down_far[slot - 1, rows, :]

    def products(c):
        slot, at = divmod(c * step, units)
        part = slice(at, at + step)
        pre[c % 2] = nn(second_in, up(slot, part))
        act_grads[c % 2] = nt(g_low, down(slot, part))

    count = slots * units // step
    products(0)
    for c in range(count):
        if c + 1 < count:
            products(c + 1)
        act, slope = gelu_and_slope(pre[c % 2])
        act = act.astype(BF16)
        hidden_grad = (act_grads[c % 2] * slope).astype(BF16)
        part = slice(c * step, (c + 1) * step)
        acts[:, part] = act
        hidden_grads[:, part] = hidden_grad
        slot, at = divmod(c * step, units)
        if slot < 2:
            ff_sum[slot, 0, :, at : at + step] += tn(second_in, hidden_grad)
            ff_sum[slot, 1, :, at : at + step] += tn(g_low, act)
    parts = [slice(slot * units, (slot + 1) * units) for slot in range(slots)]
    ffn = sum(nn(acts[:, part], down(slot)) for slot, part in enumerate(parts))
    swap.send(block, (resid + ffn).astype(BF16))
    back = sum(nt(hidden_grads[:, part], up(slot)) for slot, part in enumerate(parts))
    gain_sum[...] += jnp.sum(back * hat, axis=0, keepdims=True)
    resid_grad = g_low.astype(F32) + norm_back(back, gain, hat, inv_std)
    attn_grad = resid_grad.astype(BF16)
    resid_all[block] = attn_grad
    out_sum[...] += nn(ctx_ref[0:two, :], attn_grad)
    dctx = jnp.concatenate([nt(out_ref[...], attn_grad), nt(out_far[...], attn_grad)], axis=0).astype(BF16)
    dctx_all[block] = dctx
    dots = dctx.astype(F32) * ctx_ref[...].astype(F32)
    for h in range(heads):
        delta_all[block, h : h + 1, :] = jnp.sum(dots[h * hd : (h + 1) * hd], axis=0, keepdims=True)

    @pl.when(block == 0)
    def _():
        pieces = []
        for slot in range(2):
            pieces += [ff_sum[slot, 0], ff_sum[slot, 1], out_sum[slot * own : (slot + 1) * own].T]
        put_rows(grads_ref, pieces + [jnp.broadcast_to(gain_sum[...], (GB, gain.shape[1])).T])


def attention_back(
    heads, hd, own_heads, lens_ref, block, swap, x_ref, gain_ref, w_ref, q_ref, k_ref, v_ref, stats_ref,
    lse_all, dctx_all, delta_all, resid_all, ck_ref, ckt_ref, cv_ref,
    bias_ref, convs_ref, dck_sum, dcv_sum, dq_sum, dqkv, weight_sum, kconv_sum, vconv_sum, gain_sum,
):
    own = own_heads * hd
    slots, _, dim = w_ref.shape
    slot_heads = heads // slots
    lanes = slot_heads * hd
    factor = 1.0 / math.sqrt(hd)
    scale = LOG2E * factor
    longest_here = lax.rem(lax.axis_index("tensor"), 2) == 0
    places, starts = item_starts(lens_ref, block, longest_here, ck_ref.shape[1])

    def attend(count):
        keys = slice(0, count * GB)
        put_bias(bias_ref, places, starts, count)

        def head(h, band, one):
            q, dctx = q_ref[band, :], dctx_all[block, band, :]
            s = nn(ck_ref[h, keys, :], q) * scale + jnp.concatenate([bias_ref[keys, :]] * 3, axis=1)
            p = jnp.exp2(s - lse_all[block, one, :])
            dp = nn(cv_ref[h, keys, :], dctx)
            ds = (p * (dp - delta_all[block, one, :])).astype(BF16)
            dcv_sum[h, keys, :] += nt(p.astype(BF16), dctx)
            dck_sum[h, keys, :] += nt(ds, q)
            dq_sum[band, :] = nn(ckt_ref[band, keys], ds)

        each_head(heads, hd, head)

    for n in range(ck_ref.shape[1] // GB):
        pl.when(block == n)(functools.partial(attend, n + 1))
    mask = stats_ref[heads : heads + 1, :]
    rows = key_rows(block)
    for h in range(heads):
        band = slice(h * hd, (h + 1) * hd)
        one = slice(h, h + 1)
        q, k = q_ref[band, :].astype(F32), k_ref[band, :].astype(F32)
        v, dctx = v_ref[band, :].astype(F32), dctx_all[block, band, :].astype(F32)
        own_prob = jnp.exp2(jnp.sum(q * k, axis=0, keepdims=True) * scale - lse_all[block, one, :])
        own_dprob = jnp.sum(dctx * v, axis=0, keepdims=True)
        own_dscore = own_prob * (own_dprob - delta_all[block, one, :]) * factor
        slot, i = divmod(h, slot_heads)
        base = slot * 3 * lanes + i * hd
        dqkv[base : base + hd, :] = (dq_sum[band, :] * factor + own_dscore * k).astype(BF16)
        dck = (dck_sum[h, rows, :] * factor).astype(BF16)
        dcv = dcv_sum[h, rows, :].astype(BF16)
        for n, src, total, grad, beside in (
            (0, k_ref, kconv_sum, dck, own_dscore * q),
            (1, v_ref, vconv_sum, dcv, own_prob * dctx),
        ):
            spread = nt(convs_ref[n, h], grad)
            spread = jnp.concatenate([spread[r * hd : (r + 1) * hd] for r in range(3)], axis=1)
            at = base + (n + 1) * lanes
            dqkv[at : at + hd, :] = ((spread + beside) * mask).astype(BF16)
            if h < own_heads:
                grouped = jnp.concatenate([src[band, r * GB : (r + 1) * GB] for r in range(3)], axis=0)
                total[h] += nn(grouped, grad)
    hat, inv_std = norm_rows(x_ref[...].astype(F32))
    gain = gain_ref[...]
    first_in = (hat * gain).astype(BF16)
    weight_sum[...] += nn(dqkv[0 : 3 * own, :], first_in)
    back = tn(dqkv[...], w_ref[...].reshape(slots * 3 * lanes, dim))
    gain_sum[...] += jnp.sum(back * hat, axis=0, keepdims=True)
    total = resid_all[block].astype(F32) + norm_back(back, gain, hat, inv_std)
    swap.send(block, total.astype(BF16))


def schedule(step, blocks):
    late = (step + 3) // (2 * blocks)
    started = (step + 2 * blocks - 1) // (2 * blocks)
    last = (step + 4) // (2 * blocks)
    forward = started * (1 - last) * (blocks - 1 - (step + 1) // 2)
    forward = forward + (1 - started) * (blocks - 1)
    backward = started * ((1 - late) * (blocks - step // 2) + late * (2 * blocks - 1 - step))
    backward = backward + (1 - started) * (blocks - 1)
    backward = jnp.minimum(backward, blocks - 1)
    is_forward = (1 - started) + started * (1 - late) * ((step % 2) * (1 - last) + last * (1 - late))
    return forward, backward, is_forward


def later_kernel(
    heads, hd, own_heads, lens_ref,
    x_ref, g_ref, gain2_ref, ctx_ref, out_ref, up_ref, down_ref, out_far, up_far, down_far,
    q_front, k_front, v_front,
    x_back, gain1_ref, q_ref, k_ref, v_ref, lse_ref, w_hbm, conv_hbm, ck_hbm, ckt_hbm, cv_hbm, cvt_hbm,
    mixed_ref, mixed_peer, tokens_ref, tokens_peer, middle_out, last_out, conv_out,
    w_ref, conv_ref, ck_ref, ckt_ref, cv_ref, cvt_ref,
    mixed_staged, acts, hidden_grads, pre, act_grads, ff_sum, out_sum, gain2_sum,
    ctx_block, lse_all, dctx_all, resid_all, delta_all,
    bias_ref, convs_ref, dck_sum, dcv_sum, dq_sum, dqkv, weight_sum, kconv_sum, vconv_sum, gain1_sum,
    middle_parts, middle_pair, middle_in, last_parts, last_pair, last_in, conv_parts, conv_pair, conv_in,
    middle_turn, last_turn, conv_turn, middle_sum, last_sum, conv_sum,
    mixed_sems, mixed_local, swap_sems, swap_local, middle_sems, last_sems, conv_sems, turn_sems, load_sems,
):
    step_id = pl.program_id(0)
    blocks = dctx_all.shape[0]
    forward_block, backward_block, is_forward = schedule(step_id, blocks)
    mixed_swap = Swap(mixed_staged, mixed_ref, mixed_peer, mixed_sems, mixed_local)
    swap = Swap(resid_all, tokens_ref, tokens_peer, swap_sems, swap_local)
    middle = Spread(middle_parts, middle_pair, middle_in, middle_sum, middle_sems)
    last = Spread(last_parts, last_pair, last_in, last_sum, last_sems)
    convs = Spread(conv_parts, conv_pair, conv_in, conv_sum, conv_sems)
    slots, _, dim = w_ref.shape
    taps = convs_ref.shape[2]
    conv_cols = conv_ref.shape[2] // 2
    slot_heads = heads // slots

    loads = [
        pltpu.make_async_copy(src, dst, load_sems.at[n])
        for n, (src, dst) in enumerate(
            (
                (w_hbm, w_ref), (conv_hbm, conv_ref), (ck_hbm, ck_ref), (ckt_hbm, ckt_ref), (cv_hbm, cv_ref),
                (cvt_hbm, cvt_ref),
            )
        )
    ]

    @pl.when(step_id == 0)
    def _():
        for load in loads:
            load.start()
        count = lax.axis_size("dp")
        me, peer = lax.axis_index("dp"), lax.axis_index("tensor")
        meet([swap.device, (me ^ 1, peer)] + [(lax.rem(me + 2 * s, count), peer) for s in range(1, count // 2)])
        for ref in (
            ff_sum, out_sum, gain2_sum, dck_sum, dcv_sum, weight_sum, kconv_sum, vconv_sum, gain1_sum,
        ):
            ref[...] = jnp.zeros_like(ref)

    @pl.when(step_id == 2)
    def _():
        for load in loads:
            load.wait()
        for h in range(heads):
            slot, i = divmod(h, slot_heads)
            for n in range(2):
                conv = conv_ref[slot, i * hd : (i + 1) * hd, n * conv_cols : n * conv_cols + taps]
                convs_ref[n, h] = conv.astype(F32).T.astype(BF16)

    longest_here = lax.rem(lax.axis_index("tensor"), 2) == 0

    @pl.when(is_forward == 1)
    def _():
        places, starts = item_starts(lens_ref, forward_block, longest_here, ck_ref.shape[1])

        def put_lse(one, values):
            lse_all[forward_block, one, :] = values

        @pl.when(forward_block >= blocks // 2)
        def _():
            ctx_block[...] = ctx_ref[...]

        for n in range(blocks // 2):
            pl.when(forward_block == n)(
                functools.partial(
                    attend_forward, heads, hd, n + 1, places, starts, bias_ref, ck_ref, cvt_ref, q_front, k_front,
                    v_front, ctx_block, put_lse,
                )
            )
        feed_forward(
            heads, hd, forward_block, mixed_swap, x_ref, g_ref, gain2_ref, ctx_block, out_ref, up_ref, down_ref,
            out_far, up_far, down_far, resid_all, dctx_all, delta_all, middle_parts,
            acts, hidden_grads, pre, act_grads, ff_sum, out_sum, gain2_sum,
        )

        @pl.when(forward_block == 0)
        def _():
            middle.start()

    @pl.when(is_forward == 0)
    def _():
        @pl.when(backward_block >= blocks // 2)
        def _():
            lse_all[backward_block] = lse_ref[0:heads, :]

        attention_back(
            heads, hd, own_heads, lens_ref, backward_block, swap, x_back, gain1_ref, w_ref, q_ref, k_ref, v_ref, lse_ref,
            lse_all, dctx_all, delta_all, resid_all, ck_ref, ckt_ref, cv_ref,
            bias_ref, convs_ref, dck_sum, dcv_sum, dq_sum, dqkv, weight_sum, kconv_sum, vconv_sum, gain1_sum,
        )

    @pl.when((is_forward == 0) & (backward_block == blocks // 2 - 1))
    def _():
        middle.pass_on()

    def turned(n, ref):
        return remote(ref.at[0], ref.at[1], turn_sems, (n,), swap.device)

    def turn(n, ref, total):
        ref[0] = total[:, total.shape[1] - ref.shape[2] :].astype(BF16)
        turned(n, ref).start()

    @pl.when(step_id == 2 * blocks - 1)
    def _():
        put_rows(last_parts, [weight_sum[...].T, jnp.broadcast_to(gain1_sum[...], (GB, dim)).T])
        last.start()
        put_rows(
            conv_parts,
            [
                total[h]
                for slot in range(2)
                for total in (kconv_sum, vconv_sum)
                for h in range(slot * slot_heads, (slot + 1) * slot_heads)
            ],
        )
        convs.start()
        last.pass_on()
        convs.pass_on()
        sums = ((middle_out, middle_turn, middle), (last_out, last_turn, last), (conv_out, conv_turn, convs))
        for n, (_, ref, spread) in enumerate(sums):
            turn(n, ref, spread.total())
        for n, (out, ref, spread) in enumerate(sums):
            turned(n, ref).wait()
            total, cols = spread.sums, out.shape[1]
            split = total.shape[1] - cols
            kept = [total[:, :split]] + ([total[:, 2 * split :]] if cols > split else [])
            out[...] = ref[1].astype(F32) + jnp.concatenate(kept, axis=1)
        mixed_swap.finish()
        swap.finish()


def place_rows(lens_ref, longest_here, mine, theirs, natural, out_ref):
    half = mine.shape[0]
    first = longest_first(lens_ref, half // 3)

    def taps(block, r, other):
        rows = slice(block * TB + r * GB, block * TB + (r + 1) * GB)
        a, b = mine[rows, :].astype(F32), theirs[rows, :].astype(F32)
        return jnp.where(longest_here == other, b, a)

    for block in range(half // TB):
        for r in range(3):
            others = taps(block, r, True)
            for base in (0, half):
                natural[pl.ds(base + block * TB + r, GB, stride=3), :] = others
    for block in range(half // TB):
        for r in range(3):
            natural[pl.ds(first + block * TB + r, GB, stride=3), :] = taps(block, r, False)
    out_ref[...] = natural[...].astype(BF16)


def last_kernel(
    hd, lens_ref, mixed_ref, mixed_peer, tokens_ref, tokens_peer, middle_ref, last_ref, conv_ref,
    mixed_out, tokens_out, gain1_out, gain2_out, query_out, key_out, value_out, out_out, kconv_out, vconv_out,
    up_out, down_out, natural_mixed, natural_tokens,
):
    longest_here = lax.rem(lax.axis_index("tensor"), 2) == 0
    place_rows(lens_ref, longest_here, mixed_ref, mixed_peer, natural_mixed, mixed_out)
    place_rows(lens_ref, longest_here, tokens_ref, tokens_peer, natural_tokens, tokens_out)

    @pl.when(pl.program_id(0) == 0)
    def _():
        units, own = up_out.shape[1], query_out.shape[1]
        up_out[...] = middle_ref[:, 0:units]
        down_out[...] = middle_ref[:, units : 2 * units]
        out_out[...] = middle_ref[:, 2 * units : 2 * units + own]
        gain2_out[...] = middle_ref[:, 2 * units + own :].T[0:1]
        for n, out in enumerate((query_out, key_out, value_out)):
            out[...] = last_ref[:, n * own : (n + 1) * own]
        gain1_out[...] = last_ref[:, 3 * own :].T[0:1]
        for n, out in enumerate((kconv_out, vconv_out)):
            for h in range(out.shape[0]):
                out[h] = conv_ref[:, n * own + h * hd : n * own + (h + 1) * hd]


def whole(shape):
    return pl.BlockSpec(shape, lambda *_: (0,) * len(shape))


def cost(micros):
    return pl.CostEstimate(flops=int(micros * 1e9), bytes_accessed=1 << 20, transcendentals=0)


def params():
    return pltpu.CompilerParams(vmem_limit_bytes=VMEM, dimension_semantics=("arbitrary",))


def on_device(
    tokens, first_gain, second_gain, query_weight, key_weight, value_weight, out_weight,
    key_conv, value_conv, up_weight, down_weight, pad_mask, item_lengths, cotangent,
):
    dim = tokens.shape[1]
    own_heads, taps, hd = key_conv.shape
    peers = lax.axis_size("tensor")
    heads = own_heads * peers
    width = heads * hd
    own = own_heads * hd
    units = up_weight.shape[1]
    lens = item_lengths[0]
    rows = tokens.shape[0] // 2
    blocks = rows // TB
    groups = rows // 3
    pads = pad_mask.reshape(-1, 128)
    key_conv, value_conv = key_conv.transpose(0, 2, 1), value_conv.transpose(0, 2, 1)
    conv_cols = -(-taps // 128) * 128
    stats = heads + 8
    gain1, gain2 = first_gain[None], second_gain[None]

    rows_spec = pl.BlockSpec((TB, dim), lambda b, *_: (b, 0))
    cols_spec = pl.BlockSpec((width, TB), lambda b, *_: (0, b))
    stat_spec = pl.BlockSpec((heads, TB), lambda b, *_: (0, b))
    lse_spec = pl.BlockSpec((stats, TB), lambda b, *_: (0, b))
    early = blocks // 2
    late_cols = pl.BlockSpec((width, TB), lambda b, *_: (0, jnp.maximum(b - early, 0)))
    anywhere = pl.BlockSpec(memory_space=pl.ANY)
    inside = pl.BlockSpec(memory_space=pltpu.VMEM)
    x, g, q, k, v, ctx, lse, ck, ckt, cv, cvt, w_all, conv_all, out_far, up_far, down_far = pl.pallas_call(
        functools.partial(forward_kernel, heads, hd),
        grid_spec=pltpu.PrefetchScalarGridSpec(
            num_scalar_prefetch=1,
            grid=(blocks,),
            in_specs=[inside, inside, whole((1, dim))] + [inside] * 6 + [anywhere] * 3,
            out_specs=[
                whole((rows, dim)), whole((rows, dim)), cols_spec, cols_spec, cols_spec, late_cols, lse_spec,
                whole((heads, groups, hd)), whole((width, groups)), whole((heads, groups, hd)), whole((width, groups)),
                anywhere, anywhere, anywhere, anywhere, anywhere,
            ],
            scratch_shapes=[
                pltpu.VMEM((dim // 128 + 1, 2 * rows, 128), F32), pltpu.VMEM((dim // 128, 2 * rows, 128), F32),
                pltpu.VMEM((blocks, TB, dim), BF16), pltpu.VMEM((blocks, 8, TB), F32),
                pltpu.VMEM((peers, 3 * own, dim), BF16), pltpu.VMEM((peers, own, 2 * conv_cols), BF16),
                pltpu.VMEM((groups, GB), F32),
                pltpu.SemaphoreType.DMA((2, 2, 5, peers - 1)), pltpu.SemaphoreType.DMA((2, 3, 5, peers - 1)),
                pltpu.SemaphoreType.DMA((2,)),
            ],
        ),
        out_shape=[jax.ShapeDtypeStruct((rows, dim), BF16)] * 2
        + [jax.ShapeDtypeStruct((width, rows), BF16)] * 3
        + [jax.ShapeDtypeStruct((width, (blocks - early) * TB), BF16)]
        + [
            jax.ShapeDtypeStruct((stats, rows), F32),
            jax.ShapeDtypeStruct((heads, groups, hd), BF16),
            jax.ShapeDtypeStruct((width, groups), BF16),
            jax.ShapeDtypeStruct((heads, groups, hd), BF16),
            jax.ShapeDtypeStruct((width, groups), BF16),
            jax.ShapeDtypeStruct((peers, 3 * own, dim), BF16),
            jax.ShapeDtypeStruct((peers, own, 2 * conv_cols), BF16),
            jax.ShapeDtypeStruct((peers - 1, own, dim), BF16),
            jax.ShapeDtypeStruct((peers - 1, dim, units), BF16),
            jax.ShapeDtypeStruct((peers - 1, units, dim), BF16),
        ],
        compiler_params=pltpu.CompilerParams(
            vmem_limit_bytes=VMEM, dimension_semantics=("arbitrary",), collective_id=0, has_side_effects=True
        ),
        cost_estimate=cost(55),
        name="attention_forward",
    )(
        lens, tokens, cotangent, gain1, pads, query_weight, key_weight, value_weight, key_conv, value_conv,
        out_weight, up_weight, down_weight,
    )

    count = lax.axis_size("dp")
    slot_cols = 2 * units + own
    mid_cols = 2 * slot_cols + GB
    last_cols = 6 * own + GB
    two = 2 * own_heads
    step = 256

    def forward_at(n):
        return schedule(n, blocks)[0]

    def backward_at(n):
        return schedule(n, blocks)[1]

    def left_at(n):
        return jnp.minimum(forward_at(n), early - 1)

    left_cols = pl.BlockSpec((width, TB), lambda n, *_: (0, left_at(n)))
    front_rows = pl.BlockSpec((TB, dim), lambda n, *_: (forward_at(n), 0))
    front_cols = pl.BlockSpec((width, TB), lambda n, *_: (0, jnp.maximum(forward_at(n) - early, 0)))
    back_rows = pl.BlockSpec((TB, dim), lambda n, *_: (backward_at(n), 0))
    back_cols = pl.BlockSpec((width, TB), lambda n, *_: (0, backward_at(n)))
    back_lse = pl.BlockSpec((stats, TB), lambda n, *_: (0, backward_at(n)))
    out_dims = [(dim // count, slot_cols + GB), (dim // count, 3 * own + GB), (taps // count, 2 * own)]
    swap_sems = [pltpu.SemaphoreType.DMA((2, blocks)), pltpu.SemaphoreType.DMA((blocks,))]
    spread_sems = pltpu.SemaphoreType.DMA((2, count // 2))
    split = [(dim // count, mid_cols), (dim // count, last_cols), (taps // count, 4 * own)]
    mixed, mixed_peer, grad_rows, grad_peer, middle_share, last_share, conv_share = pl.pallas_call(
        functools.partial(later_kernel, heads, hd, two),
        grid_spec=pltpu.PrefetchScalarGridSpec(
            num_scalar_prefetch=1,
            grid=(2 * blocks,),
            in_specs=[front_rows, front_rows, inside, front_cols]
            + [inside] * 6
            + [left_cols] * 3
            + [back_rows, inside, back_cols, back_cols, back_cols, back_lse]
            + [anywhere] * 6,
            out_specs=[anywhere] * 4 + [whole(d) for d in out_dims],
            scratch_shapes=[
                pltpu.VMEM((peers, 3 * own, dim), BF16), pltpu.VMEM((peers, own, 2 * conv_cols), BF16),
                pltpu.VMEM((heads, groups, hd), BF16), pltpu.VMEM((width, groups), BF16),
                pltpu.VMEM((heads, groups, hd), BF16), pltpu.VMEM((width, groups), BF16),
                pltpu.VMEM((blocks, TB, dim), BF16),
                pltpu.VMEM((TB, peers * units), BF16), pltpu.VMEM((TB, peers * units), BF16),
                pltpu.VMEM((2, TB, step), F32), pltpu.VMEM((2, TB, step), F32),
                pltpu.VMEM((2, 2, dim, units), F32), pltpu.VMEM((2 * own, dim), F32), pltpu.VMEM((1, dim), F32),
                pltpu.VMEM((width, TB), BF16), pltpu.VMEM((blocks, heads, TB), F32),
                pltpu.VMEM((blocks, width, TB), BF16), pltpu.VMEM((blocks, TB, dim), BF16),
                pltpu.VMEM((blocks, heads, TB), F32),
                pltpu.VMEM((groups, GB), F32),
                pltpu.VMEM((2, heads, taps, hd), BF16), pltpu.VMEM((heads, groups, hd), F32),
                pltpu.VMEM((heads, groups, hd), F32), pltpu.VMEM((width, TB), F32),
                pltpu.VMEM((3 * width, TB), BF16), pltpu.VMEM((6 * own, dim), F32),
                pltpu.VMEM((two, taps, hd), F32), pltpu.VMEM((two, taps, hd), F32),
                pltpu.VMEM((1, dim), F32),
            ]
            + [pltpu.VMEM((*lead, *d), BF16) for d in split for lead in ((2, count // 2), (count // 2,), (count // 2,))]
            + [pltpu.VMEM((2, *d), BF16) for d in out_dims]
            + [pltpu.VMEM(d, F32) for d in split]
            + swap_sems * 2
            + [spread_sems] * 3
            + [pltpu.SemaphoreType.DMA((2, 3)), pltpu.SemaphoreType.DMA((6,))],
        ),
        out_shape=[jax.ShapeDtypeStruct((rows, dim), BF16)] * 4 + [jax.ShapeDtypeStruct(d, F32) for d in out_dims],
        compiler_params=pltpu.CompilerParams(
            vmem_limit_bytes=VMEM, dimension_semantics=("arbitrary",), collective_id=1, has_side_effects=True
        ),
        cost_estimate=cost(110),
        name="feed_forward_and_backward",
    )(
        lens, x, g, gain2, ctx, out_weight, up_weight, down_weight, out_far.reshape(width - own, dim), up_far, down_far,
        q, k, v, x, gain1, q, k, v, lse, w_all, conv_all, ck, ckt, cv, cvt,
    )

    share = dim // count
    own_conv = (own_heads, taps // count, hd)
    shapes = [
        ((1, share), F32), ((1, share), F32), ((share, own), F32), ((share, own), F32), ((share, own), F32),
        ((share, own), F32), (own_conv, F32), (own_conv, F32), ((share, units), F32), ((share, units), F32),
    ]
    lane_half = pl.BlockSpec((rows, 128), lambda c: (0, c))
    lane_all = pl.BlockSpec((2 * rows, 128), lambda c: (0, c))
    outs = pl.pallas_call(
        functools.partial(last_kernel, hd),
        grid=(dim // 128,),
        in_specs=[pl.BlockSpec(memory_space=pltpu.SMEM)] + [lane_half] * 4 + [whole(d) for d in out_dims],
        out_specs=[lane_all] * 2 + [whole(d) for d, _ in shapes],
        out_shape=[jax.ShapeDtypeStruct((2 * rows, dim), BF16)] * 2 + [jax.ShapeDtypeStruct(d, t) for d, t in shapes],
        scratch_shapes=[pltpu.VMEM((2 * rows, 128), F32)] * 2,
        compiler_params=params(),
        cost_estimate=cost(15),
        name="in_order",
    )(lens, mixed, mixed_peer, grad_rows, grad_peer, middle_share, last_share, conv_share)
    mixed, grad_tokens, gain1, gain2, query, key, value, out, kconv, vconv, up, down = outs
    return (
        mixed, grad_tokens, gain1.reshape(share), gain2.reshape(share), query, key, value, out.T,
        kconv, vconv, up, down.T,
    )


def solution(mesh):
    in_specs = (
        P("dp", None),
        P(),
        P(),
        P(None, "tensor"),
        P(None, "tensor"),
        P(None, "tensor"),
        P("tensor", None),
        P("tensor", None, None),
        P("tensor", None, None),
        P(None, "tensor"),
        P("tensor", None),
        P("dp"),
        P("dp", None),
        P("dp", None),
    )
    out_specs = (
        P("dp", None),
        P("dp", None),
        P("dp"),
        P("dp"),
        P("dp", "tensor"),
        P("dp", "tensor"),
        P("dp", "tensor"),
        P("tensor", "dp"),
        P("tensor", "dp", None),
        P("tensor", "dp", None),
        P("dp", "tensor"),
        P("tensor", "dp"),
    )
    return jax.shard_map(
        on_device, mesh=mesh, in_specs=in_specs, out_specs=out_specs, check_vma=False
    )
```

```python
import functools
import math

import jax
import jax.numpy as jnp
from jax import lax
from jax.experimental import pallas as pl
from jax.experimental.pallas import tpu as pltpu
from jax.sharding import PartitionSpec as P

F32 = jnp.float32
BF16 = jnp.bfloat16
GB = 128
TB = 3 * GB
NEG = -1e30
LOG2E = 1.0 / math.log(2.0)
VMEM = 60 * 1024 * 1024

ERF_P = 0.43
ERF_C = (
    0.24255178053871013,
    0.24376598744271377,
    0.2089868288055898,
    0.23281685899157548,
    -0.05797941172752005,
    0.3523368029188165,
    -0.2915198548110903,
    0.06904073943922798,
)


def nn(a, b):
    return lax.dot_general(a, b, (((1,), (0,)), ((), ())), preferred_element_type=F32)


def nt(a, b):
    return lax.dot_general(a, b, (((1,), (1,)), ((), ())), preferred_element_type=F32)


def tn(a, b):
    return lax.dot_general(a, b, (((0,), (0,)), ((), ())), preferred_element_type=F32)


def norm_rows(values):
    centred = values - jnp.mean(values, -1, keepdims=True)
    inv_std = lax.rsqrt(jnp.mean(centred * centred, -1, keepdims=True) + 1e-05)
    return centred * inv_std, inv_std


def norm_back(grad_out, gains, normed, inv_std):
    scaled = grad_out * gains
    return inv_std * (
        scaled
        - jnp.mean(scaled, -1, keepdims=True)
        - normed * jnp.mean(scaled * normed, -1, keepdims=True)
    )


def gelu_and_slope(h):
    t = 1.0 / (1.0 + (ERF_P * math.sqrt(0.5)) * jnp.abs(h))
    poly = t * (0.5 * ERF_C[-1]) + 0.5 * ERF_C[-2]
    for c in ERF_C[-3::-1]:
        poly = poly * t + 0.5 * c
    e = jnp.exp2((h * h) * (-0.5 * LOG2E))
    tail = e * (poly * t)
    cdf = jnp.where(h >= 0, 1.0 - tail, tail)
    return h * cdf, cdf + h * (e * (1.0 / math.sqrt(2.0 * math.pi)))


def item_starts(lens_ref, block, longest_here, half):
    places = block * GB + lax.broadcasted_iota(jnp.int32, (1, GB), 1)
    starts = jnp.zeros((1, GB), jnp.int32)
    end = jnp.int32(0)
    for i in range(lens_ref.shape[0] - 1):
        end = end + jnp.where((lens_ref[i] == half) == longest_here, lens_ref[i], 0)
        starts = jnp.where(places >= end, end, starts)
    return places, starts


def longest_first(lens_ref, half):
    first, ahead = jnp.int32(0), jnp.int32(1)
    for i in range(lens_ref.shape[0]):
        ahead = jnp.where(lens_ref[i] == half, 0, ahead)
        first = first + ahead * lens_ref[i]
    return 3 * first


def own_taps(source, block, first, longest_here):
    half = source.shape[1] // 2
    base = block * TB
    parts = []
    for c in range(source.shape[0]):
        for r in range(3):
            inside = source[c, pl.ds(first + base + r, GB, stride=3), :]
            low = source[c, pl.ds(base + r, GB, stride=3), :]
            high = source[c, pl.ds(half + base + r, GB, stride=3), :]
            place = base + r + 3 * lax.broadcasted_iota(jnp.int32, (GB, 1), 0)
            parts.append(jnp.where(longest_here, inside, jnp.where(place < first, low, high)))
    return jnp.concatenate(
        [jnp.concatenate(parts[3 * c : 3 * c + 3], axis=0) for c in range(source.shape[0])], axis=1
    )


def put_bias(bias_ref, places, starts, count):
    for kb in range(count):
        keys = kb * GB + lax.broadcasted_iota(jnp.int32, (GB, GB), 0)
        bias_ref[kb * GB : (kb + 1) * GB, :] = jnp.where((keys >= starts) & (keys < places), 0.0, NEG)


def each_head(heads, hd, work):
    def some(i, carry):
        for n in range(2):
            h = 2 * i + n
            work(h, pl.ds(pl.multiple_of(h * hd, hd), hd), pl.ds(h, 1))
        return carry

    lax.fori_loop(0, heads // 2, some, 0)


def key_rows(kb):
    return pl.ds(pl.multiple_of(kb * GB, GB), GB)


def remote(src, dst, sems, at, device):
    return pltpu.make_async_remote_copy(
        src_ref=src, dst_ref=dst, send_sem=sems.at[(0, *at)], recv_sem=sems.at[(1, *at)],
        device_id=device, device_id_type=pl.DeviceIdType.MESH,
    )


def greet(devices):
    barrier = pltpu.get_barrier_semaphore()
    for device in devices:
        pl.semaphore_signal(barrier, inc=1, device_id=device, device_id_type=pl.DeviceIdType.MESH)


def greeted(devices):
    pl.semaphore_wait(pltpu.get_barrier_semaphore(), len(devices))


def put_rows(ref, pieces, at=0):
    parities, count, rows, _ = ref.shape
    for piece in pieces:
        cols = piece.shape[1]
        for d in range(parities * count):
            ref[d % 2, d // 2, :, at : at + cols] = piece[d * rows : (d + 1) * rows].astype(ref.dtype)
        at += cols


class Swap:
    def __init__(self, staged, mine, theirs, sems, local_sems):
        self.staged, self.mine, self.theirs, self.sems, self.local_sems = staged, mine, theirs, sems, local_sems
        self.device = (lax.axis_index("dp"), lax.axis_index("tensor") ^ 1)
        self.blocks = mine.shape[0] // TB

    def rows(self, block):
        return pl.ds(pl.multiple_of(block * TB, TB), TB)

    def local(self, block):
        return pltpu.make_async_copy(
            self.staged.at[block], self.mine.at[self.rows(block)], self.local_sems.at[block]
        )

    def far(self, block):
        return remote(
            self.staged.at[block], self.theirs.at[self.rows(block)], self.sems, (block,), self.device
        )

    def send(self, block, values):
        self.staged[block] = values
        self.local(block).start()
        self.far(block).start()

    def finish(self):
        for block in range(self.blocks):
            self.local(block).wait()
            self.far(block).wait()


class Spread:
    def __init__(self, source, paired, landed, sums, sems):
        self.source, self.paired, self.landed, self.sums, self.sems = source, paired, landed, sums, sems
        self.me, self.peer = lax.axis_index("dp"), lax.axis_index("tensor")
        self.parity = lax.rem(self.me, 2)
        self.count = lax.axis_size("dp")

    def beside(self):
        return remote(
            self.source.at[1 - self.parity], self.paired, self.sems, (0,), (self.me ^ 1, self.peer)
        )

    def copy(self, s):
        there = lax.rem(self.me + 2 * s, self.count)
        return remote(self.paired.at[there // 2], self.landed.at[s], self.sems, (s,), (there, self.peer))

    def start(self):
        self.beside().start()

    def pass_on(self):
        self.beside().wait()

        def add(n, carry):
            pair = self.paired[n].astype(F32) + self.source[self.parity, n].astype(F32)
            self.paired[n] = pair.astype(BF16)
            return carry

        lax.fori_loop(0, self.count // 2, add, 0)

        def step(s, carry):
            self.copy(s).start()
            return carry

        lax.fori_loop(1, self.count // 2, step, 0)

    def total(self):
        def step(s, carry):
            self.copy(s).wait()
            return carry

        lax.fori_loop(1, self.count // 2, step, 0)
        self.sums[...] = self.paired[self.me // 2].astype(F32)

        def add(s, carry):
            self.sums[...] += self.landed[s].astype(F32)
            return carry

        lax.fori_loop(1, self.count // 2, add, 0)
        return self.sums


class Gather:
    def __init__(self, own, far, sems):
        self.own, self.far, self.sems = own, far, sems
        self.dp, self.tensor = lax.axis_index("dp"), lax.axis_index("tensor")
        self.peers = lax.axis_size("tensor")

    def devices(self):
        return [(self.dp, self.tensor ^ s) for s in range(1, self.peers)] + [
            (self.dp ^ m, self.tensor) for m in (1, 2, 4, 6)
        ]

    def eighth(self, array):
        rows = array.shape[0] // 8
        place = lax.rem(self.dp, 2) * 4 + lax.rem(self.dp, 8) // 2
        return array.at[pl.ds(pl.multiple_of(place * rows, rows), rows)]

    def half(self, array):
        rows = array.shape[0] // 2
        return array.at[pl.ds(pl.multiple_of(lax.rem(self.dp, 2) * rows, rows), rows)]

    def across(self, n, s):
        device = (self.dp, self.tensor ^ s)
        return remote(
            self.eighth(self.own[n]), self.eighth(self.far[n].at[s - 1]), self.sems, (n, 0, s - 1), device
        )

    def around(self, n, s, m):
        part = self.eighth(self.far[n].at[s - 1])
        return remote(part, part, self.sems, (n, m // 2, s - 1), (self.dp ^ m, self.tensor))

    def beside(self, n, s):
        part = self.half(self.far[n].at[s - 1])
        return remote(part, part, self.sems, (n, 4, s - 1), (self.dp ^ 1, self.tensor))

    def each(self, s=None):
        peers = range(1, self.peers) if s is None else (s,)
        return [(n, s) for s in peers for n in range(len(self.far))]

    def start(self):
        for n, s in self.each():
            self.across(n, s).start()

    def pass_around(self, s=None):
        for n, s in self.each(s):
            self.across(n, s).wait_recv()
            for m in (6, 4, 2):
                self.around(n, s, m).start()

    def pass_beside(self, s=None):
        for n, s in self.each(s):
            for m in (2, 4, 6):
                self.around(n, s, m).wait_recv()
            self.beside(n, s).start()

    def arrive(self):
        for n, s in self.each():
            self.beside(n, s).wait_recv()

    def finish(self):
        for n, s in self.each():
            self.across(n, s).wait_send()
            for m in (2, 4, 6):
                self.around(n, s, m).wait_send()
            self.beside(n, s).wait_send()


def attend_forward(
    heads, hd, count, places, starts, bias_ref, ck_ref, cvt_ref, q_ref, k_ref, v_ref, ctx_ref, put_lse
):
    scale = LOG2E / math.sqrt(hd)
    keys = slice(0, count * GB)
    put_bias(bias_ref, places, starts, count)

    def head(h, band, one):
        q = q_ref[band, :]
        own_score = jnp.sum(q.astype(F32) * k_ref[band, :].astype(F32), axis=0, keepdims=True) * scale
        s = nn(ck_ref[h, keys, :], q) * scale + jnp.concatenate([bias_ref[keys, :]] * 3, axis=1)
        top = jnp.maximum(own_score, jnp.max(s, axis=0, keepdims=True))
        p = jnp.exp2(s - top)
        own_prob = jnp.exp2(own_score - top)
        total = own_prob + jnp.sum(p, axis=0, keepdims=True)
        mixed = own_prob * v_ref[band, :].astype(F32) + nn(cvt_ref[band, keys], p.astype(BF16))
        ctx_ref[band, :] = (mixed * (1.0 / total)).astype(BF16)
        put_lse(one, top + jnp.log(total) * LOG2E)

    each_head(heads, hd, head)


def forward_kernel(
    heads, hd, lens_ref, x_ref, g_ref, gain_ref, pad_ref, query_ref, key_ref, value_ref, kconv_ref, vconv_ref,
    out_ref, up_ref, down_ref,
    q_ref, k_ref, v_ref, ctx_ref, lse_ref, x_all, g_all, ck_all, ckt_all, cv_all, cvt_all, w_all, conv_all,
    out_far, up_far, down_far,
    xs, gs, x_own, g_own, ck_ref, ckt_ref, cv_ref, cvt_ref, first_all, mask_rows, w_ref, conv_ref, bias_ref, first_sems, last_sems, local_sems,
):
    block = pl.program_id(0)
    blocks = pl.num_programs(0)
    own_heads, _, taps = kconv_ref.shape
    own = own_heads * hd
    dim = x_ref.shape[1]
    conv_cols = conv_ref.shape[2] // 2
    first_gather = Gather((w_ref.at[0], conv_ref.at[0]), (w_ref.at[1:], conv_ref.at[1:]), first_sems)
    last_gather = Gather((out_ref, up_ref, down_ref), (out_far, up_far, down_far), last_sems)
    kept = ((w_ref, w_all), (conv_ref, conv_all), (x_own, x_all), (g_own, g_all))
    kept += ((ck_ref, ck_all), (ckt_ref, ckt_all), (cv_ref, cv_all), (cvt_ref, cvt_all))
    keep_copies = [pltpu.make_async_copy(src, dst, local_sems.at[n]) for n, (src, dst) in enumerate(kept)]
    half = x_ref.shape[0] // 2
    blocks_there = half // TB
    longest_here = lax.rem(lax.axis_index("tensor"), 2) == 0
    first = longest_first(lens_ref, half // 3)

    @pl.when(block == 0)
    def _():
        greet(first_gather.devices())
        for n, src in enumerate((query_ref, key_ref, value_ref)):
            w_ref[0, n * own : (n + 1) * own, :] = src[...].T
        conv_ref[0] = jnp.zeros_like(conv_ref[0])
        for n, src in enumerate((kconv_ref, vconv_ref)):
            for h in range(own_heads):
                conv_ref[0, h * hd : (h + 1) * hd, n * conv_cols : n * conv_cols + taps] = src[h]
        greeted(first_gather.devices())
        first_gather.start()
        for src, dst in ((x_ref, xs), (g_ref, gs)):
            for c in range(dim // 128):
                dst[c] = src[:, c * 128 : (c + 1) * 128].astype(F32)
        pads = pad_ref[...].astype(F32).T
        for c in range(pads.shape[1]):
            xs[dim // 128, c * 128 : (c + 1) * 128, :] = jnp.broadcast_to(pads[:, c : c + 1], (128, 128))
        first_gather.pass_around()
        last_gather.start()

        def prepare(n, carry):
            x = own_taps(xs, n, first, longest_here)
            mask_rows[n] = jnp.broadcast_to(x[:, dim:].T[0:1], mask_rows.shape[1:])
            x = x[:, :dim]
            normed, _ = norm_rows(x)
            first_all[n] = (normed * gain_ref[...]).astype(BF16)
            rows = pl.ds(pl.multiple_of(n * TB, TB), TB)
            x_own[rows, :] = x.astype(BF16)
            g_own[rows, :] = own_taps(gs, n, first, longest_here).astype(BF16)
            return carry

        lax.fori_loop(0, half // TB // 2, prepare, 0)
        first_gather.pass_beside()
        lax.fori_loop(half // TB // 2, half // TB, prepare, 0)
        first_gather.arrive()
        first_gather.finish()
        for copy in keep_copies[:4]:
            copy.start()

    mask = mask_rows[block, 0:1]
    first_in = first_all[block]
    for slot in range(w_ref.shape[0]):
        at = slice(slot * own, (slot + 1) * own)
        part = nt(w_ref[slot], first_in)
        q_ref[at, :] = part[0:own].astype(BF16)
        k_ref[at, :] = (part[own : 2 * own] * mask).astype(BF16)
        v_ref[at, :] = (part[2 * own : 3 * own] * mask).astype(BF16)
    rows = key_rows(block)
    for h in range(heads):
        band = slice(h * hd, (h + 1) * hd)
        slot, i = divmod(h, own_heads)
        for n, src, plain, trans in ((0, k_ref, ck_ref, ckt_ref), (1, v_ref, cv_ref, cvt_ref)):
            grouped = jnp.concatenate([src[band, r * GB : (r + 1) * GB] for r in range(3)], axis=0)
            comp = nn(conv_ref[slot, i * hd : (i + 1) * hd, n * conv_cols : n * conv_cols + taps], grouped)
            trans[band, rows] = comp.astype(BF16)
            plain[h, rows, :] = comp.T.astype(BF16)
    places, starts = item_starts(lens_ref, block, longest_here, half // 3)
    lse_ref[heads:, :] = jnp.broadcast_to(mask, (lse_ref.shape[0] - heads, TB))

    @pl.when(block == blocks - 1)
    def _():
        for copy in keep_copies[4:]:
            copy.start()

    peers = w_ref.shape[0]
    for s in range(1, peers):
        pl.when(block == s - 1)(functools.partial(last_gather.pass_around, s))
        if s < peers - 1:
            pl.when(block == blocks_there - peers + 1 + s)(functools.partial(last_gather.pass_beside, s))

    @pl.when(block < blocks // 2)
    def _():
        lse_ref[0:heads, :] = jnp.zeros_like(lse_ref[0:heads, :])

    def put_lse(one, values):
        lse_ref[one, :] = values

    for n in range(blocks_there // 2, blocks_there):
        pl.when(block == n)(
            functools.partial(
                attend_forward, heads, hd, n + 1, places, starts, bias_ref, ck_ref, cvt_ref, q_ref, k_ref, v_ref,
                ctx_ref, put_lse,
            )
        )

    @pl.when(block == blocks - 1)
    def _():
        last_gather.pass_beside(w_ref.shape[0] - 1)

    @pl.when(block == blocks - 1)
    def _():
        last_gather.arrive()
        last_gather.finish()
        for copy in keep_copies:
            copy.wait()


def feed_forward(
    heads, hd, block, swap, x_ref, g_ref, gain_ref, ctx_ref, out_ref, up_ref, down_ref,
    out_far, up_far, down_far, resid_all, dctx_all, delta_all, grads_ref,
    acts, hidden_grads, pre, act_grads, ff_sum, out_sum, gain_sum,
):
    own, two = out_ref.shape[0], out_sum.shape[0]
    units = up_ref.shape[1]
    step = pre.shape[2]
    slots = up_far.shape[0] + 1
    gain = gain_ref[...]
    g_low = g_ref[...]
    resid = x_ref[...].astype(F32) + tn(ctx_ref[0:own, :], out_ref[...]) + tn(ctx_ref[own:, :], out_far[...])
    hat, inv_std = norm_rows(resid)
    second_in = (hat * gain).astype(BF16)

    def up(slot, cols=slice(None)):
        return up_ref[:, cols] if slot == 0 else up_far[slot - 1, :, cols]

    def down(slot, rows=slice(None)):
        return down_ref[rows, :] if slot == 0 else down_far[slot - 1, rows, :]

    def products(c):
        slot, at = divmod(c * step, units)
        part = slice(at, at + step)
        pre[c % 2] = nn(second_in, up(slot, part))
        act_grads[c % 2] = nt(g_low, down(slot, part))

    count = slots * units // step
    products(0)
    for c in range(count):
        if c + 1 < count:
            products(c + 1)
        act, slope = gelu_and_slope(pre[c % 2])
        act = act.astype(BF16)
        hidden_grad = (act_grads[c % 2] * slope).astype(BF16)
        part = slice(c * step, (c + 1) * step)
        acts[:, part] = act
        hidden_grads[:, part] = hidden_grad
        slot, at = divmod(c * step, units)
        if slot < 2:
            ff_sum[slot, 0, :, at : at + step] += tn(second_in, hidden_grad)
            ff_sum[slot, 1, :, at : at + step] += tn(g_low, act)
    parts = [slice(slot * units, (slot + 1) * units) for slot in range(slots)]
    ffn = sum(nn(acts[:, part], down(slot)) for slot, part in enumerate(parts))
    swap.send(block, (resid + ffn).astype(BF16))
    back = sum(nt(hidden_grads[:, part], up(slot)) for slot, part in enumerate(parts))
    gain_sum[...] += jnp.sum(back * hat, axis=0, keepdims=True)
    resid_grad = g_low.astype(F32) + norm_back(back, gain, hat, inv_std)
    attn_grad = resid_grad.astype(BF16)
    resid_all[block] = attn_grad
    out_sum[...] += nn(ctx_ref[0:two, :], attn_grad)
    dctx = jnp.concatenate([nt(out_ref[...], attn_grad), nt(out_far[...], attn_grad)], axis=0).astype(BF16)
    dctx_all[block] = dctx
    dots = dctx.astype(F32) * ctx_ref[...].astype(F32)
    for h in range(heads):
        delta_all[block, h : h + 1, :] = jnp.sum(dots[h * hd : (h + 1) * hd], axis=0, keepdims=True)

    @pl.when(block == 0)
    def _():
        pieces = []
        for slot in range(2):
            pieces += [ff_sum[slot, 0], ff_sum[slot, 1], out_sum[slot * own : (slot + 1) * own].T]
        put_rows(grads_ref, pieces + [jnp.broadcast_to(gain_sum[...], (GB, gain.shape[1])).T])


def attention_back(
    heads, hd, own_heads, lens_ref, block, swap, x_ref, gain_ref, w_ref, q_ref, k_ref, v_ref, stats_ref,
    lse_all, dctx_all, delta_all, resid_all, ck_ref, ckt_ref, cv_ref,
    bias_ref, convs_ref, dck_sum, dcv_sum, dq_sum, dqkv, weight_sum, kconv_sum, vconv_sum, gain_sum,
):
    own = own_heads * hd
    slots, _, dim = w_ref.shape
    slot_heads = heads // slots
    lanes = slot_heads * hd
    factor = 1.0 / math.sqrt(hd)
    scale = LOG2E * factor
    longest_here = lax.rem(lax.axis_index("tensor"), 2) == 0
    places, starts = item_starts(lens_ref, block, longest_here, ck_ref.shape[1])

    def attend(count):
        keys = slice(0, count * GB)
        put_bias(bias_ref, places, starts, count)

        def head(h, band, one):
            q, dctx = q_ref[band, :], dctx_all[block, band, :]
            s = nn(ck_ref[h, keys, :], q) * scale + jnp.concatenate([bias_ref[keys, :]] * 3, axis=1)
            p = jnp.exp2(s - lse_all[block, one, :])
            dp = nn(cv_ref[h, keys, :], dctx)
            ds = (p * (dp - delta_all[block, one, :])).astype(BF16)
            dcv_sum[h, keys, :] += nt(p.astype(BF16), dctx)
            dck_sum[h, keys, :] += nt(ds, q)
            dq_sum[band, :] = nn(ckt_ref[band, keys], ds)

        each_head(heads, hd, head)

    for n in range(ck_ref.shape[1] // GB):
        pl.when(block == n)(functools.partial(attend, n + 1))
    mask = stats_ref[heads : heads + 1, :]
    rows = key_rows(block)
    for h in range(heads):
        band = slice(h * hd, (h + 1) * hd)
        one = slice(h, h + 1)
        q, k = q_ref[band, :].astype(F32), k_ref[band, :].astype(F32)
        v, dctx = v_ref[band, :].astype(F32), dctx_all[block, band, :].astype(F32)
        own_prob = jnp.exp2(jnp.sum(q * k, axis=0, keepdims=True) * scale - lse_all[block, one, :])
        own_dprob = jnp.sum(dctx * v, axis=0, keepdims=True)
        own_dscore = own_prob * (own_dprob - delta_all[block, one, :]) * factor
        slot, i = divmod(h, slot_heads)
        base = slot * 3 * lanes + i * hd
        dqkv[base : base + hd, :] = (dq_sum[band, :] * factor + own_dscore * k).astype(BF16)
        dck = (dck_sum[h, rows, :] * factor).astype(BF16)
        dcv = dcv_sum[h, rows, :].astype(BF16)
        for n, src, total, grad, beside in (
            (0, k_ref, kconv_sum, dck, own_dscore * q),
            (1, v_ref, vconv_sum, dcv, own_prob * dctx),
        ):
            spread = nt(convs_ref[n, h], grad)
            spread = jnp.concatenate([spread[r * hd : (r + 1) * hd] for r in range(3)], axis=1)
            at = base + (n + 1) * lanes
            dqkv[at : at + hd, :] = ((spread + beside) * mask).astype(BF16)
            if h < own_heads:
                grouped = jnp.concatenate([src[band, r * GB : (r + 1) * GB] for r in range(3)], axis=0)
                total[h] += nn(grouped, grad)
    hat, inv_std = norm_rows(x_ref[...].astype(F32))
    gain = gain_ref[...]
    first_in = (hat * gain).astype(BF16)
    weight_sum[...] += nn(dqkv[0 : 3 * own, :], first_in)
    back = tn(dqkv[...], w_ref[...].reshape(slots * 3 * lanes, dim))
    gain_sum[...] += jnp.sum(back * hat, axis=0, keepdims=True)
    total = resid_all[block].astype(F32) + norm_back(back, gain, hat, inv_std)
    swap.send(block, total.astype(BF16))


def schedule(step, blocks):
    late = (step + 3) // (2 * blocks)
    started = (step + 2 * blocks - 1) // (2 * blocks)
    last = (step + 4) // (2 * blocks)
    forward = started * (1 - last) * (blocks - 1 - (step + 1) // 2)
    forward = forward + (1 - started) * (blocks - 1)
    backward = started * ((1 - late) * (blocks - step // 2) + late * (2 * blocks - 1 - step))
    backward = backward + (1 - started) * (blocks - 1)
    backward = jnp.minimum(backward, blocks - 1)
    is_forward = (1 - started) + started * (1 - late) * ((step % 2) * (1 - last) + last * (1 - late))
    return forward, backward, is_forward


def later_kernel(
    heads, hd, own_heads, lens_ref,
    x_ref, g_ref, gain2_ref, ctx_ref, out_ref, up_ref, down_ref, out_far, up_hbm, down_hbm,
    q_front, k_front, v_front,
    x_back, gain1_ref, q_ref, k_ref, v_ref, lse_ref, w_hbm, conv_hbm, ck_hbm, ckt_hbm, cv_hbm, cvt_hbm,
    mixed_ref, mixed_peer, tokens_ref, tokens_peer, middle_out, last_out, conv_out,
    up_far, down_far, w_ref, conv_ref, ck_ref, ckt_ref, cv_ref, cvt_ref,
    mixed_staged, acts, hidden_grads, pre, act_grads, ff_sum, out_sum, gain2_sum,
    ctx_block, lse_all, dctx_all, resid_all, delta_all,
    bias_ref, convs_ref, dck_sum, dcv_sum, dq_sum, dqkv, weight_sum, kconv_sum, vconv_sum, gain1_sum,
    middle_parts, middle_pair, middle_in, last_parts, last_pair, last_in, conv_parts, conv_pair, conv_in,
    middle_turn, last_turn, conv_turn, middle_sum, last_sum, conv_sum,
    mixed_sems, mixed_local, swap_sems, swap_local, middle_sems, last_sems, conv_sems, turn_sems, load_sems,
):
    step_id = pl.program_id(0)
    blocks = dctx_all.shape[0]
    forward_block, backward_block, is_forward = schedule(step_id, blocks)
    mixed_swap = Swap(mixed_staged, mixed_ref, mixed_peer, mixed_sems, mixed_local)
    swap = Swap(resid_all, tokens_ref, tokens_peer, swap_sems, swap_local)
    middle = Spread(middle_parts, middle_pair, middle_in, middle_sum, middle_sems)
    last = Spread(last_parts, last_pair, last_in, last_sum, last_sems)
    convs = Spread(conv_parts, conv_pair, conv_in, conv_sum, conv_sems)
    slots, _, dim = w_ref.shape
    taps = convs_ref.shape[2]
    conv_cols = conv_ref.shape[2] // 2
    slot_heads = heads // slots

    loads = [
        pltpu.make_async_copy(src, dst, load_sems.at[n])
        for n, (src, dst) in enumerate(
            (
                (up_hbm, up_far), (down_hbm, down_far), (w_hbm, w_ref), (conv_hbm, conv_ref), (ck_hbm, ck_ref), (ckt_hbm, ckt_ref), (cv_hbm, cv_ref),
                (cvt_hbm, cvt_ref),
            )
        )
    ]

    @pl.when(step_id == 0)
    def _():
        for load in loads:
            load.start()
        count = lax.axis_size("dp")
        me, peer = lax.axis_index("dp"), lax.axis_index("tensor")
        devices = [swap.device, (me ^ 1, peer)] + [(lax.rem(me + 2 * s, count), peer) for s in range(1, count // 2)]
        greet(devices)
        for ref in (ff_sum, out_sum, gain2_sum):
            ref[...] = jnp.zeros_like(ref)
        for load in loads[:2]:
            load.wait()
        greeted(devices)

    @pl.when(step_id == 2)
    def _():
        for load in loads[2:]:
            load.wait()
        for ref in (dck_sum, dcv_sum, weight_sum, kconv_sum, vconv_sum, gain1_sum):
            ref[...] = jnp.zeros_like(ref)
        for h in range(heads):
            slot, i = divmod(h, slot_heads)
            for n in range(2):
                conv = conv_ref[slot, i * hd : (i + 1) * hd, n * conv_cols : n * conv_cols + taps]
                convs_ref[n, h] = conv.astype(F32).T.astype(BF16)

    longest_here = lax.rem(lax.axis_index("tensor"), 2) == 0

    @pl.when(is_forward == 1)
    def _():
        places, starts = item_starts(lens_ref, forward_block, longest_here, ck_ref.shape[1])

        def put_lse(one, values):
            lse_all[forward_block, one, :] = values

        @pl.when(forward_block >= blocks // 2)
        def _():
            ctx_block[...] = ctx_ref[...]

        for n in range(blocks // 2):
            pl.when(forward_block == n)(
                functools.partial(
                    attend_forward, heads, hd, n + 1, places, starts, bias_ref, ck_ref, cvt_ref, q_front, k_front,
                    v_front, ctx_block, put_lse,
                )
            )
        feed_forward(
            heads, hd, forward_block, mixed_swap, x_ref, g_ref, gain2_ref, ctx_block, out_ref, up_ref, down_ref,
            out_far, up_far, down_far, resid_all, dctx_all, delta_all, middle_parts,
            acts, hidden_grads, pre, act_grads, ff_sum, out_sum, gain2_sum,
        )

        @pl.when(forward_block == 0)
        def _():
            middle.start()

    @pl.when(is_forward == 0)
    def _():
        @pl.when(backward_block >= blocks // 2)
        def _():
            lse_all[backward_block] = lse_ref[0:heads, :]

        attention_back(
            heads, hd, own_heads, lens_ref, backward_block, swap, x_back, gain1_ref, w_ref, q_ref, k_ref, v_ref, lse_ref,
            lse_all, dctx_all, delta_all, resid_all, ck_ref, ckt_ref, cv_ref,
            bias_ref, convs_ref, dck_sum, dcv_sum, dq_sum, dqkv, weight_sum, kconv_sum, vconv_sum, gain1_sum,
        )

    @pl.when((is_forward == 0) & (backward_block == blocks // 2 - 1))
    def _():
        middle.pass_on()

    def turned(n, ref):
        return remote(ref.at[0], ref.at[1], turn_sems, (n,), swap.device)

    def turn(n, ref, total):
        ref[0] = total[:, total.shape[1] - ref.shape[2] :].astype(BF16)
        turned(n, ref).start()

    @pl.when(step_id == 2 * blocks - 1)
    def _():
        put_rows(last_parts, [weight_sum[...].T, jnp.broadcast_to(gain1_sum[...], (GB, dim)).T])
        last.start()
        put_rows(
            conv_parts,
            [
                total[h]
                for slot in range(2)
                for total in (kconv_sum, vconv_sum)
                for h in range(slot * slot_heads, (slot + 1) * slot_heads)
            ],
        )
        convs.start()
        last.pass_on()
        convs.pass_on()
        sums = ((middle_out, middle_turn, middle), (last_out, last_turn, last), (conv_out, conv_turn, convs))
        for n, (_, ref, spread) in enumerate(sums):
            turn(n, ref, spread.total())
        for n, (out, ref, spread) in enumerate(sums):
            turned(n, ref).wait()
            total, cols = spread.sums, out.shape[1]
            split = total.shape[1] - cols
            kept = [total[:, :split]] + ([total[:, 2 * split :]] if cols > split else [])
            out[...] = ref[1].astype(F32) + jnp.concatenate(kept, axis=1)
        mixed_swap.finish()
        swap.finish()


def place_rows(lens_ref, longest_here, mine, theirs, natural, out_ref):
    half = mine.shape[0]
    first = longest_first(lens_ref, half // 3)

    def taps(block, r, other):
        rows = slice(block * TB + r * GB, block * TB + (r + 1) * GB)
        a, b = mine[rows, :].astype(F32), theirs[rows, :].astype(F32)
        return jnp.where(longest_here == other, b, a)

    parts = natural.shape[0]
    for block in range(half // TB):
        for r in range(3):
            others = taps(block, r, True)
            for c in range(parts):
                for base in (0, half):
                    natural[c, pl.ds(base + block * TB + r, GB, stride=3), :] = others[:, c * 128 : (c + 1) * 128]
    for block in range(half // TB):
        for r in range(3):
            longest = taps(block, r, False)
            for c in range(parts):
                natural[c, pl.ds(first + block * TB + r, GB, stride=3), :] = longest[:, c * 128 : (c + 1) * 128]
    for c in range(parts):
        out_ref[:, c * 128 : (c + 1) * 128] = natural[c].astype(BF16)


def last_kernel(
    hd, lens_ref, mixed_ref, mixed_peer, tokens_ref, tokens_peer, middle_ref, last_ref, conv_ref,
    mixed_out, tokens_out, gain1_out, gain2_out, query_out, key_out, value_out, out_out, kconv_out, vconv_out,
    up_out, down_out, natural_mixed, natural_tokens,
):
    longest_here = lax.rem(lax.axis_index("tensor"), 2) == 0
    place_rows(lens_ref, longest_here, mixed_ref, mixed_peer, natural_mixed, mixed_out)
    place_rows(lens_ref, longest_here, tokens_ref, tokens_peer, natural_tokens, tokens_out)

    @pl.when(pl.program_id(0) == 0)
    def _():
        units, own = up_out.shape[1], query_out.shape[1]
        up_out[...] = middle_ref[:, 0:units]
        down_out[...] = middle_ref[:, units : 2 * units]
        out_out[...] = middle_ref[:, 2 * units : 2 * units + own]
        gain2_out[...] = middle_ref[:, 2 * units + own :].T[0:1]
        for n, out in enumerate((query_out, key_out, value_out)):
            out[...] = last_ref[:, n * own : (n + 1) * own]
        gain1_out[...] = last_ref[:, 3 * own :].T[0:1]
        for n, out in enumerate((kconv_out, vconv_out)):
            for h in range(out.shape[0]):
                out[h] = conv_ref[:, n * own + h * hd : n * own + (h + 1) * hd]


def whole(shape):
    return pl.BlockSpec(shape, lambda *_: (0,) * len(shape))


def cost(micros):
    return pl.CostEstimate(flops=int(micros * 1e9), bytes_accessed=1 << 20, transcendentals=0)


def params():
    return pltpu.CompilerParams(vmem_limit_bytes=VMEM, dimension_semantics=("arbitrary",))


def on_device(
    tokens, first_gain, second_gain, query_weight, key_weight, value_weight, out_weight,
    key_conv, value_conv, up_weight, down_weight, pad_mask, item_lengths, cotangent,
):
    dim = tokens.shape[1]
    own_heads, taps, hd = key_conv.shape
    peers = lax.axis_size("tensor")
    heads = own_heads * peers
    width = heads * hd
    own = own_heads * hd
    units = up_weight.shape[1]
    lens = item_lengths[0]
    rows = tokens.shape[0] // 2
    blocks = rows // TB
    groups = rows // 3
    pads = pad_mask.reshape(-1, 128)
    key_conv, value_conv = key_conv.transpose(0, 2, 1), value_conv.transpose(0, 2, 1)
    conv_cols = -(-taps // 128) * 128
    stats = heads + 8
    gain1, gain2 = first_gain[None], second_gain[None]

    rows_spec = pl.BlockSpec((TB, dim), lambda b, *_: (b, 0))
    cols_spec = pl.BlockSpec((width, TB), lambda b, *_: (0, b))
    stat_spec = pl.BlockSpec((heads, TB), lambda b, *_: (0, b))
    lse_spec = pl.BlockSpec((stats, TB), lambda b, *_: (0, b))
    early = blocks // 2
    late_cols = pl.BlockSpec((width, TB), lambda b, *_: (0, jnp.maximum(b - early, 0)))
    anywhere = pl.BlockSpec(memory_space=pl.ANY)
    inside = pl.BlockSpec(memory_space=pltpu.VMEM)
    q, k, v, ctx, lse, x, g, ck, ckt, cv, cvt, w_all, conv_all, out_far, up_far, down_far = pl.pallas_call(
        functools.partial(forward_kernel, heads, hd),
        grid_spec=pltpu.PrefetchScalarGridSpec(
            num_scalar_prefetch=1,
            grid=(blocks,),
            in_specs=[inside, inside, whole((1, dim))] + [inside] * 6 + [anywhere] * 3,
            out_specs=[
                cols_spec, cols_spec, cols_spec, late_cols, lse_spec,
            ]
            + [anywhere] * 11,
            scratch_shapes=[
                pltpu.VMEM((dim // 128 + 1, 2 * rows, 128), F32), pltpu.VMEM((dim // 128, 2 * rows, 128), F32),
                pltpu.VMEM((rows, dim), BF16), pltpu.VMEM((rows, dim), BF16),
                pltpu.VMEM((heads, groups, hd), BF16), pltpu.VMEM((width, groups), BF16),
                pltpu.VMEM((heads, groups, hd), BF16), pltpu.VMEM((width, groups), BF16),
                pltpu.VMEM((blocks, TB, dim), BF16), pltpu.VMEM((blocks, 8, TB), F32),
                pltpu.VMEM((peers, 3 * own, dim), BF16), pltpu.VMEM((peers, own, 2 * conv_cols), BF16),
                pltpu.VMEM((groups, GB), F32),
                pltpu.SemaphoreType.DMA((2, 2, 5, peers - 1)), pltpu.SemaphoreType.DMA((2, 3, 5, peers - 1)),
                pltpu.SemaphoreType.DMA((8,)),
            ],
        ),
        out_shape=[jax.ShapeDtypeStruct((width, rows), BF16)] * 3
        + [
            jax.ShapeDtypeStruct((width, (blocks - early) * TB), BF16),
            jax.ShapeDtypeStruct((stats, rows), F32),
            jax.ShapeDtypeStruct((rows, dim), BF16),
            jax.ShapeDtypeStruct((rows, dim), BF16),
            jax.ShapeDtypeStruct((heads, groups, hd), BF16),
            jax.ShapeDtypeStruct((width, groups), BF16),
            jax.ShapeDtypeStruct((heads, groups, hd), BF16),
            jax.ShapeDtypeStruct((width, groups), BF16),
            jax.ShapeDtypeStruct((peers, 3 * own, dim), BF16),
            jax.ShapeDtypeStruct((peers, own, 2 * conv_cols), BF16),
            jax.ShapeDtypeStruct((peers - 1, own, dim), BF16),
            jax.ShapeDtypeStruct((peers - 1, dim, units), BF16),
            jax.ShapeDtypeStruct((peers - 1, units, dim), BF16),
        ],
        compiler_params=pltpu.CompilerParams(
            vmem_limit_bytes=VMEM, dimension_semantics=("arbitrary",), collective_id=0, has_side_effects=True
        ),
        cost_estimate=cost(55),
        name="attention_forward",
    )(
        lens, tokens, cotangent, gain1, pads, query_weight, key_weight, value_weight, key_conv, value_conv,
        out_weight, up_weight, down_weight,
    )

    count = lax.axis_size("dp")
    slot_cols = 2 * units + own
    mid_cols = 2 * slot_cols + GB
    last_cols = 6 * own + GB
    two = 2 * own_heads
    step = 256

    def forward_at(n):
        return schedule(n, blocks)[0]

    def backward_at(n):
        return schedule(n, blocks)[1]

    def left_at(n):
        return jnp.minimum(forward_at(n), early - 1)

    left_cols = pl.BlockSpec((width, TB), lambda n, *_: (0, left_at(n)))
    front_rows = pl.BlockSpec((TB, dim), lambda n, *_: (forward_at(n), 0))
    front_cols = pl.BlockSpec((width, TB), lambda n, *_: (0, jnp.maximum(forward_at(n) - early, 0)))
    back_rows = pl.BlockSpec((TB, dim), lambda n, *_: (backward_at(n), 0))
    back_cols = pl.BlockSpec((width, TB), lambda n, *_: (0, backward_at(n)))
    back_lse = pl.BlockSpec((stats, TB), lambda n, *_: (0, backward_at(n)))
    out_dims = [(dim // count, slot_cols + GB), (dim // count, 3 * own + GB), (taps // count, 2 * own)]
    swap_sems = [pltpu.SemaphoreType.DMA((2, blocks)), pltpu.SemaphoreType.DMA((blocks,))]
    spread_sems = pltpu.SemaphoreType.DMA((2, count // 2))
    split = [(dim // count, mid_cols), (dim // count, last_cols), (taps // count, 4 * own)]
    mixed, mixed_peer, grad_rows, grad_peer, middle_share, last_share, conv_share = pl.pallas_call(
        functools.partial(later_kernel, heads, hd, two),
        grid_spec=pltpu.PrefetchScalarGridSpec(
            num_scalar_prefetch=1,
            grid=(2 * blocks,),
            in_specs=[front_rows, front_rows, inside, front_cols]
            + [inside] * 4
            + [anywhere] * 2
            + [left_cols] * 3
            + [back_rows, inside, back_cols, back_cols, back_cols, back_lse]
            + [anywhere] * 6,
            out_specs=[anywhere] * 4 + [whole(d) for d in out_dims],
            scratch_shapes=[
                pltpu.VMEM((peers - 1, dim, units), BF16), pltpu.VMEM((peers - 1, units, dim), BF16),
                pltpu.VMEM((peers, 3 * own, dim), BF16), pltpu.VMEM((peers, own, 2 * conv_cols), BF16),
                pltpu.VMEM((heads, groups, hd), BF16), pltpu.VMEM((width, groups), BF16),
                pltpu.VMEM((heads, groups, hd), BF16), pltpu.VMEM((width, groups), BF16),
                pltpu.VMEM((blocks, TB, dim), BF16),
                pltpu.VMEM((TB, peers * units), BF16), pltpu.VMEM((TB, peers * units), BF16),
                pltpu.VMEM((2, TB, step), F32), pltpu.VMEM((2, TB, step), F32),
                pltpu.VMEM((2, 2, dim, units), F32), pltpu.VMEM((2 * own, dim), F32), pltpu.VMEM((1, dim), F32),
                pltpu.VMEM((width, TB), BF16), pltpu.VMEM((blocks, heads, TB), F32),
                pltpu.VMEM((blocks, width, TB), BF16), pltpu.VMEM((blocks, TB, dim), BF16),
                pltpu.VMEM((blocks, heads, TB), F32),
                pltpu.VMEM((groups, GB), F32),
                pltpu.VMEM((2, heads, taps, hd), BF16), pltpu.VMEM((heads, groups, hd), F32),
                pltpu.VMEM((heads, groups, hd), F32), pltpu.VMEM((width, TB), F32),
                pltpu.VMEM((3 * width, TB), BF16), pltpu.VMEM((6 * own, dim), F32),
                pltpu.VMEM((two, taps, hd), F32), pltpu.VMEM((two, taps, hd), F32),
                pltpu.VMEM((1, dim), F32),
            ]
            + [pltpu.VMEM((*lead, *d), BF16) for d in split for lead in ((2, count // 2), (count // 2,), (count // 2,))]
            + [pltpu.VMEM((2, *d), BF16) for d in out_dims]
            + [pltpu.VMEM(d, F32) for d in split]
            + swap_sems * 2
            + [spread_sems] * 3
            + [pltpu.SemaphoreType.DMA((2, 3)), pltpu.SemaphoreType.DMA((8,))],
        ),
        out_shape=[jax.ShapeDtypeStruct((rows, dim), BF16)] * 4 + [jax.ShapeDtypeStruct(d, F32) for d in out_dims],
        compiler_params=pltpu.CompilerParams(
            vmem_limit_bytes=VMEM, dimension_semantics=("arbitrary",), collective_id=1, has_side_effects=True
        ),
        cost_estimate=cost(110),
        name="feed_forward_and_backward",
    )(
        lens, x, g, gain2, ctx, out_weight, up_weight, down_weight, out_far.reshape(width - own, dim), up_far, down_far,
        q, k, v, x, gain1, q, k, v, lse, w_all, conv_all, ck, ckt, cv, cvt,
    )

    share = dim // count
    own_conv = (own_heads, taps // count, hd)
    shapes = [
        ((1, share), F32), ((1, share), F32), ((share, own), F32), ((share, own), F32), ((share, own), F32),
        ((share, own), F32), (own_conv, F32), (own_conv, F32), ((share, units), F32), ((share, units), F32),
    ]
    lanes = 256
    lane_half = pl.BlockSpec((rows, lanes), lambda c: (0, c))
    lane_all = pl.BlockSpec((2 * rows, lanes), lambda c: (0, c))
    outs = pl.pallas_call(
        functools.partial(last_kernel, hd),
        grid=(dim // lanes,),
        in_specs=[pl.BlockSpec(memory_space=pltpu.SMEM)] + [lane_half] * 4 + [whole(d) for d in out_dims],
        out_specs=[lane_all] * 2 + [whole(d) for d, _ in shapes],
        out_shape=[jax.ShapeDtypeStruct((2 * rows, dim), BF16)] * 2 + [jax.ShapeDtypeStruct(d, t) for d, t in shapes],
        scratch_shapes=[pltpu.VMEM((lanes // 128, 2 * rows, 128), F32)] * 2,
        compiler_params=params(),
        cost_estimate=cost(15),
        name="in_order",
    )(lens, mixed, mixed_peer, grad_rows, grad_peer, middle_share, last_share, conv_share)
    mixed, grad_tokens, gain1, gain2, query, key, value, out, kconv, vconv, up, down = outs
    return (
        mixed, grad_tokens, gain1.reshape(share), gain2.reshape(share), query, key, value, out.T,
        kconv, vconv, up, down.T,
    )


def solution(mesh):
    in_specs = (
        P("dp", None),
        P(),
        P(),
        P(None, "tensor"),
        P(None, "tensor"),
        P(None, "tensor"),
        P("tensor", None),
        P("tensor", None, None),
        P("tensor", None, None),
        P(None, "tensor"),
        P("tensor", None),
        P("dp"),
        P("dp", None),
        P("dp", None),
    )
    out_specs = (
        P("dp", None),
        P("dp", None),
        P("dp"),
        P("dp"),
        P("dp", "tensor"),
        P("dp", "tensor"),
        P("dp", "tensor"),
        P("tensor", "dp"),
        P("tensor", "dp", None),
        P("tensor", "dp", None),
        P("dp", "tensor"),
        P("tensor", "dp"),
    )
    return jax.shard_map(
        on_device, mesh=mesh, in_specs=in_specs, out_specs=out_specs, check_vma=False
    )
```

```python
import functools
import math

import jax
import jax.numpy as jnp
from jax import lax
from jax.experimental import pallas as pl
from jax.experimental.pallas import tpu as pltpu
from jax.sharding import PartitionSpec as P

F32 = jnp.float32
BF16 = jnp.bfloat16
GB = 128
TB = 3 * GB
NEG = -1e30
LOG2E = 1.0 / math.log(2.0)
VMEM = 60 * 1024 * 1024

ERF_P = 0.43
ERF_C = (
    0.24255178053871013,
    0.24376598744271377,
    0.2089868288055898,
    0.23281685899157548,
    -0.05797941172752005,
    0.3523368029188165,
    -0.2915198548110903,
    0.06904073943922798,
)


def nn(a, b):
    return lax.dot_general(a, b, (((1,), (0,)), ((), ())), preferred_element_type=F32)


def nt(a, b):
    return lax.dot_general(a, b, (((1,), (1,)), ((), ())), preferred_element_type=F32)


def tn(a, b):
    return lax.dot_general(a, b, (((0,), (0,)), ((), ())), preferred_element_type=F32)


def norm_rows(values):
    centred = values - jnp.mean(values, -1, keepdims=True)
    inv_std = lax.rsqrt(jnp.mean(centred * centred, -1, keepdims=True) + 1e-05)
    return centred * inv_std, inv_std


def norm_back(grad_out, gains, normed, inv_std):
    scaled = grad_out * gains
    return inv_std * (
        scaled
        - jnp.mean(scaled, -1, keepdims=True)
        - normed * jnp.mean(scaled * normed, -1, keepdims=True)
    )


def gelu_and_slope(h):
    t = 1.0 / (1.0 + (ERF_P * math.sqrt(0.5)) * jnp.abs(h))
    poly = t * (0.5 * ERF_C[-1]) + 0.5 * ERF_C[-2]
    for c in ERF_C[-3::-1]:
        poly = poly * t + 0.5 * c
    e = jnp.exp2((h * h) * (-0.5 * LOG2E))
    tail = e * (poly * t)
    cdf = jnp.where(h >= 0, 1.0 - tail, tail)
    return h * cdf, cdf + h * (e * (1.0 / math.sqrt(2.0 * math.pi)))


def item_starts(lens_ref, block, longest_here, half):
    places = block * GB + lax.broadcasted_iota(jnp.int32, (1, GB), 1)
    starts = jnp.zeros((1, GB), jnp.int32)
    end = jnp.int32(0)
    for i in range(lens_ref.shape[0] - 1):
        end = end + jnp.where((lens_ref[i] == half) == longest_here, lens_ref[i], 0)
        starts = jnp.where(places >= end, end, starts)
    return places, starts


def longest_first(lens_ref, half):
    first, ahead = jnp.int32(0), jnp.int32(1)
    for i in range(lens_ref.shape[0]):
        ahead = jnp.where(lens_ref[i] == half, 0, ahead)
        first = first + ahead * lens_ref[i]
    return 3 * first


def own_taps(source, half, block, first, longest_here):
    base = block * TB
    parts = []
    for c in range(source.shape[0]):
        for r in range(3):
            inside = source[c, pl.ds(first + base + r, GB, stride=3), :]
            low = source[c, pl.ds(base + r, GB, stride=3), :]
            high = source[c, pl.ds(half + base + r, GB, stride=3), :]
            place = base + r + 3 * lax.broadcasted_iota(jnp.int32, (GB, 1), 0)
            parts.append(jnp.where(longest_here, inside, jnp.where(place < first, low, high)))
    return jnp.concatenate(
        [jnp.concatenate(parts[3 * c : 3 * c + 3], axis=0) for c in range(source.shape[0])], axis=1
    )


def put_bias(bias_ref, places, starts, count):
    for kb in range(count):
        keys = kb * GB + lax.broadcasted_iota(jnp.int32, (GB, GB), 0)
        bias_ref[kb * GB : (kb + 1) * GB, :] = jnp.where((keys >= starts) & (keys < places), 0.0, NEG)


def each_head(heads, hd, work):
    def some(i, carry):
        for n in range(2):
            h = 2 * i + n
            work(h, pl.ds(pl.multiple_of(h * hd, hd), hd), pl.ds(h, 1))
        return carry

    lax.fori_loop(0, heads // 2, some, 0)


def key_rows(kb):
    return pl.ds(pl.multiple_of(kb * GB, GB), GB)


def remote(src, dst, sems, at, device):
    return pltpu.make_async_remote_copy(
        src_ref=src, dst_ref=dst, send_sem=sems.at[(0, *at)], recv_sem=sems.at[(1, *at)],
        device_id=device, device_id_type=pl.DeviceIdType.MESH,
    )


def greet(devices):
    barrier = pltpu.get_barrier_semaphore()
    for device in devices:
        pl.semaphore_signal(barrier, inc=1, device_id=device, device_id_type=pl.DeviceIdType.MESH)


def greeted(devices):
    pl.semaphore_wait(pltpu.get_barrier_semaphore(), len(devices))


def put_rows(ref, pieces, at=0):
    parities, count, rows, _ = ref.shape
    for piece in pieces:
        cols = piece.shape[1]
        for d in range(parities * count):
            ref[d % 2, d // 2, :, at : at + cols] = piece[d * rows : (d + 1) * rows].astype(ref.dtype)
        at += cols


class Swap:
    def __init__(self, staged, mine, theirs, sems, local_sems):
        self.staged, self.mine, self.theirs, self.sems, self.local_sems = staged, mine, theirs, sems, local_sems
        self.device = (lax.axis_index("dp"), lax.axis_index("tensor") ^ 1)
        self.blocks = mine.shape[0] // TB

    def rows(self, block):
        return pl.ds(pl.multiple_of(block * TB, TB), TB)

    def local(self, block):
        return pltpu.make_async_copy(
            self.staged.at[block], self.mine.at[self.rows(block)], self.local_sems.at[block]
        )

    def far(self, block):
        return remote(
            self.staged.at[block], self.theirs.at[self.rows(block)], self.sems, (block,), self.device
        )

    def send(self, block, values):
        self.staged[block] = values
        self.local(block).start()
        self.far(block).start()

    def finish(self):
        for block in range(self.blocks):
            self.local(block).wait()
            self.far(block).wait()


class Spread:
    def __init__(self, source, paired, landed, sums, sems):
        self.source, self.paired, self.landed, self.sums, self.sems = source, paired, landed, sums, sems
        self.me, self.peer = lax.axis_index("dp"), lax.axis_index("tensor")
        self.parity = lax.rem(self.me, 2)
        self.count = lax.axis_size("dp")

    def beside(self):
        return remote(
            self.source.at[1 - self.parity], self.paired, self.sems, (0,), (self.me ^ 1, self.peer)
        )

    def copy(self, s):
        there = lax.rem(self.me + 2 * s, self.count)
        return remote(self.paired.at[there // 2], self.landed.at[s], self.sems, (s,), (there, self.peer))

    def start(self):
        self.beside().start()

    def pass_on(self):
        self.beside().wait()

        def add(n, carry):
            pair = self.paired[n].astype(F32) + self.source[self.parity, n].astype(F32)
            self.paired[n] = pair.astype(BF16)
            return carry

        lax.fori_loop(0, self.count // 2, add, 0)

        def step(s, carry):
            self.copy(s).start()
            return carry

        lax.fori_loop(1, self.count // 2, step, 0)

    def total(self):
        def step(s, carry):
            self.copy(s).wait()
            return carry

        lax.fori_loop(1, self.count // 2, step, 0)
        self.sums[...] = self.paired[self.me // 2].astype(F32)

        def add(s, carry):
            self.sums[...] += self.landed[s].astype(F32)
            return carry

        lax.fori_loop(1, self.count // 2, add, 0)
        return self.sums


class Gather:
    def __init__(self, own, far, sems):
        self.own, self.far, self.sems = own, far, sems
        self.dp, self.tensor = lax.axis_index("dp"), lax.axis_index("tensor")
        self.peers = lax.axis_size("tensor")

    def devices(self):
        return [(self.dp, self.tensor ^ s) for s in range(1, self.peers)] + [
            (self.dp ^ m, self.tensor) for m in (1, 2, 4, 6)
        ]

    def eighth(self, array):
        rows = array.shape[0] // 8
        place = lax.rem(self.dp, 2) * 4 + lax.rem(self.dp, 8) // 2
        return array.at[pl.ds(pl.multiple_of(place * rows, rows), rows)]

    def half(self, array):
        rows = array.shape[0] // 2
        return array.at[pl.ds(pl.multiple_of(lax.rem(self.dp, 2) * rows, rows), rows)]

    def across(self, n, s):
        device = (self.dp, self.tensor ^ s)
        return remote(
            self.eighth(self.own[n]), self.eighth(self.far[n].at[s - 1]), self.sems, (n, 0, s - 1), device
        )

    def around(self, n, s, m):
        part = self.eighth(self.far[n].at[s - 1])
        return remote(part, part, self.sems, (n, m // 2, s - 1), (self.dp ^ m, self.tensor))

    def beside(self, n, s):
        part = self.half(self.far[n].at[s - 1])
        return remote(part, part, self.sems, (n, 4, s - 1), (self.dp ^ 1, self.tensor))

    def each(self, s=None):
        peers = range(1, self.peers) if s is None else (s,)
        return [(n, s) for s in peers for n in range(len(self.far))]

    def start(self):
        for n, s in self.each():
            self.across(n, s).start()

    def pass_around(self, s=None):
        for n, s in self.each(s):
            self.across(n, s).wait_recv()
            for m in (6, 4, 2):
                self.around(n, s, m).start()

    def pass_beside(self, s=None):
        for n, s in self.each(s):
            for m in (2, 4, 6):
                self.around(n, s, m).wait_recv()
            self.beside(n, s).start()

    def arrive(self):
        for n, s in self.each():
            self.beside(n, s).wait_recv()

    def finish(self):
        for n, s in self.each():
            self.across(n, s).wait_send()
            for m in (2, 4, 6):
                self.around(n, s, m).wait_send()
            self.beside(n, s).wait_send()


def attend_forward(
    heads, hd, count, places, starts, bias_ref, ck_ref, cvt_ref, q_ref, k_ref, v_ref, ctx_ref, put_lse
):
    scale = LOG2E / math.sqrt(hd)
    keys = slice(0, count * GB)
    put_bias(bias_ref, places, starts, count)

    def head(h, band, one):
        q = q_ref[band, :]
        own_score = jnp.sum(q.astype(F32) * k_ref[band, :].astype(F32), axis=0, keepdims=True) * scale
        s = nn(ck_ref[h, keys, :], q) * scale + jnp.concatenate([bias_ref[keys, :]] * 3, axis=1)
        top = jnp.maximum(own_score, jnp.max(s, axis=0, keepdims=True))
        p = jnp.exp2(s - top)
        own_prob = jnp.exp2(own_score - top)
        total = own_prob + jnp.sum(p, axis=0, keepdims=True)
        mixed = own_prob * v_ref[band, :].astype(F32) + nn(cvt_ref[band, keys], p.astype(BF16))
        ctx_ref[band, :] = (mixed * (1.0 / total)).astype(BF16)
        put_lse(one, top + jnp.log(total) * LOG2E)

    each_head(heads, hd, head)


def forward_kernel(
    heads, hd, lens_ref, x_ref, g_ref, gain_ref, pad_ref, query_ref, key_ref, value_ref, kconv_ref, vconv_ref,
    out_ref, up_ref, down_ref,
    q_ref, k_ref, v_ref, ctx_ref, lse_ref, x_all, g_all, ck_all, ckt_all, cv_all, cvt_all, w_all, conv_all,
    out_far, up_far, down_far,
    xs, gs, x_own, g_own, ck_ref, ckt_ref, cv_ref, cvt_ref, first_all, mask_rows, w_ref, conv_ref, bias_ref, first_sems, last_sems, local_sems,
):
    block = pl.program_id(0)
    blocks = pl.num_programs(0)
    own_heads, _, taps = kconv_ref.shape
    own = own_heads * hd
    dim = x_ref.shape[1]
    conv_cols = conv_ref.shape[2] // 2
    first_gather = Gather((w_ref.at[0], conv_ref.at[0]), (w_ref.at[1:], conv_ref.at[1:]), first_sems)
    last_gather = Gather((out_ref, up_ref, down_ref), (out_far, up_far, down_far), last_sems)
    kept = ((w_ref, w_all), (conv_ref, conv_all), (x_own, x_all), (g_own, g_all))
    kept += ((ck_ref, ck_all), (ckt_ref, ckt_all), (cv_ref, cv_all), (cvt_ref, cvt_all))
    keep_copies = [pltpu.make_async_copy(src, dst, local_sems.at[n]) for n, (src, dst) in enumerate(kept)]
    half = x_ref.shape[0] // 2
    blocks_there = half // TB
    longest_here = lax.rem(lax.axis_index("tensor"), 2) == 0
    first = longest_first(lens_ref, half // 3)

    @pl.when(block == 0)
    def _():
        greet(first_gather.devices())
        for n, src in enumerate((query_ref, key_ref, value_ref)):
            w_ref[0, n * own : (n + 1) * own, :] = src[...].T
        conv_ref[0] = jnp.zeros_like(conv_ref[0])
        for n, src in enumerate((kconv_ref, vconv_ref)):
            for h in range(own_heads):
                conv_ref[0, h * hd : (h + 1) * hd, n * conv_cols : n * conv_cols + taps] = src[h]
        greeted(first_gather.devices())
        first_gather.start()
        for src, dst in ((x_ref, xs), (g_ref, gs)):
            for c in range(dim // 128):
                dst[c, 0 : 2 * half, :] = src[:, c * 128 : (c + 1) * 128].astype(F32)
        pads = pad_ref[...].astype(F32).T
        for c in range(pads.shape[1]):
            xs[dim // 128, c * 128 : (c + 1) * 128, :] = jnp.broadcast_to(pads[:, c : c + 1], (128, 128))
        first_gather.pass_around()
        last_gather.start()

        def prepare(n, carry):
            x = own_taps(xs, half, n, first, longest_here)
            mask_rows[n] = jnp.broadcast_to(x[:, dim:].T[0:1], mask_rows.shape[1:])
            x = x[:, :dim]
            normed, _ = norm_rows(x)
            first_all[n] = (normed * gain_ref[...]).astype(BF16)
            rows = pl.ds(pl.multiple_of(n * TB, TB), TB)
            x_own[rows, :] = x.astype(BF16)
            g_own[rows, :] = own_taps(gs, half, n, first, longest_here).astype(BF16)
            return carry

        lax.fori_loop(0, half // TB // 2, prepare, 0)
        first_gather.pass_beside()
        lax.fori_loop(half // TB // 2, half // TB, prepare, 0)
        first_gather.arrive()
        first_gather.finish()
        for copy in keep_copies[:4]:
            copy.start()

    mask = mask_rows[block, 0:1]
    first_in = first_all[block]
    for slot in range(w_ref.shape[0]):
        at = slice(slot * own, (slot + 1) * own)
        part = nt(w_ref[slot], first_in)
        q_ref[at, :] = part[0:own].astype(BF16)
        k_ref[at, :] = (part[own : 2 * own] * mask).astype(BF16)
        v_ref[at, :] = (part[2 * own : 3 * own] * mask).astype(BF16)
    rows = key_rows(block)
    for h in range(heads):
        band = slice(h * hd, (h + 1) * hd)
        slot, i = divmod(h, own_heads)
        for n, src, plain, trans in ((0, k_ref, ck_ref, ckt_ref), (1, v_ref, cv_ref, cvt_ref)):
            grouped = jnp.concatenate([src[band, r * GB : (r + 1) * GB] for r in range(3)], axis=0)
            comp = nn(conv_ref[slot, i * hd : (i + 1) * hd, n * conv_cols : n * conv_cols + taps], grouped)
            trans[band, rows] = comp.astype(BF16)
            plain[h, rows, :] = comp.T.astype(BF16)
    places, starts = item_starts(lens_ref, block, longest_here, half // 3)
    lse_ref[heads:, :] = jnp.broadcast_to(mask, (lse_ref.shape[0] - heads, TB))

    @pl.when(block == blocks - 1)
    def _():
        for copy in keep_copies[4:]:
            copy.start()

    peers = w_ref.shape[0]
    for s in range(1, peers):
        pl.when(block == s - 1)(functools.partial(last_gather.pass_around, s))
        if s < peers - 1:
            pl.when(block == blocks_there - peers + 1 + s)(functools.partial(last_gather.pass_beside, s))

    @pl.when(block < blocks // 2)
    def _():
        lse_ref[0:heads, :] = jnp.zeros_like(lse_ref[0:heads, :])

    def put_lse(one, values):
        lse_ref[one, :] = values

    for n in range(blocks_there // 2, blocks_there):
        pl.when(block == n)(
            functools.partial(
                attend_forward, heads, hd, n + 1, places, starts, bias_ref, ck_ref, cvt_ref, q_ref, k_ref, v_ref,
                ctx_ref, put_lse,
            )
        )

    @pl.when(block == blocks - 1)
    def _():
        last_gather.pass_beside(w_ref.shape[0] - 1)

    @pl.when(block == blocks - 1)
    def _():
        last_gather.arrive()
        last_gather.finish()
        for copy in keep_copies:
            copy.wait()


def feed_forward(
    heads, hd, block, swap, x_ref, g_ref, gain_ref, ctx_ref, out_ref, up_ref, down_ref,
    out_far, up_far, down_far, resid_all, dctx_all, delta_all, grads_ref,
    acts, hidden_grads, pre, act_grads, ff_sum, out_sum, gain_sum,
):
    own, two = out_ref.shape[0], out_sum.shape[0]
    units = up_ref.shape[1]
    step = pre.shape[2]
    slots = up_far.shape[0] + 1
    gain = gain_ref[...]
    g_low = g_ref[...]
    resid = x_ref[...].astype(F32) + tn(ctx_ref[0:own, :], out_ref[...]) + tn(ctx_ref[own:, :], out_far[...])
    hat, inv_std = norm_rows(resid)
    second_in = (hat * gain).astype(BF16)

    def up(slot, cols=slice(None)):
        return up_ref[:, cols] if slot == 0 else up_far[slot - 1, :, cols]

    def down(slot, rows=slice(None)):
        return down_ref[rows, :] if slot == 0 else down_far[slot - 1, rows, :]

    def products(c):
        slot, at = divmod(c * step, units)
        part = slice(at, at + step)
        pre[c % 2] = nn(second_in, up(slot, part))
        act_grads[c % 2] = nt(g_low, down(slot, part))

    count = slots * units // step
    products(0)
    for c in range(count):
        if c + 1 < count:
            products(c + 1)
        act, slope = gelu_and_slope(pre[c % 2])
        act = act.astype(BF16)
        hidden_grad = (act_grads[c % 2] * slope).astype(BF16)
        part = slice(c * step, (c + 1) * step)
        acts[:, part] = act
        hidden_grads[:, part] = hidden_grad
        slot, at = divmod(c * step, units)
        if slot < 2:
            ff_sum[slot, 0, :, at : at + step] += tn(second_in, hidden_grad)
            ff_sum[slot, 1, :, at : at + step] += tn(g_low, act)
    parts = [slice(slot * units, (slot + 1) * units) for slot in range(slots)]
    ffn = sum(nn(acts[:, part], down(slot)) for slot, part in enumerate(parts))
    swap.send(block, (resid + ffn).astype(BF16))
    back = sum(nt(hidden_grads[:, part], up(slot)) for slot, part in enumerate(parts))
    gain_sum[...] += jnp.sum(back * hat, axis=0, keepdims=True)
    resid_grad = g_low.astype(F32) + norm_back(back, gain, hat, inv_std)
    attn_grad = resid_grad.astype(BF16)
    resid_all[block] = attn_grad
    out_sum[...] += nn(ctx_ref[0:two, :], attn_grad)
    dctx = jnp.concatenate([nt(out_ref[...], attn_grad), nt(out_far[...], attn_grad)], axis=0).astype(BF16)
    dctx_all[block] = dctx
    dots = dctx.astype(F32) * ctx_ref[...].astype(F32)
    for h in range(heads):
        delta_all[block, h : h + 1, :] = jnp.sum(dots[h * hd : (h + 1) * hd], axis=0, keepdims=True)

    @pl.when(block == 0)
    def _():
        pieces = []
        for slot in range(2):
            pieces += [ff_sum[slot, 0], ff_sum[slot, 1], out_sum[slot * own : (slot + 1) * own].T]
        put_rows(grads_ref, pieces + [jnp.broadcast_to(gain_sum[...], (GB, gain.shape[1])).T])


def attention_back(
    heads, hd, own_heads, lens_ref, block, swap, x_ref, gain_ref, w_ref, q_ref, k_ref, v_ref, stats_ref,
    lse_all, dctx_all, delta_all, resid_all, ck_ref, ckt_ref, cv_ref,
    bias_ref, convs_ref, dck_sum, dcv_sum, dq_sum, dqkv, weight_sum, kconv_sum, vconv_sum, gain_sum,
):
    own = own_heads * hd
    slots, _, dim = w_ref.shape
    slot_heads = heads // slots
    lanes = slot_heads * hd
    factor = 1.0 / math.sqrt(hd)
    scale = LOG2E * factor
    longest_here = lax.rem(lax.axis_index("tensor"), 2) == 0
    places, starts = item_starts(lens_ref, block, longest_here, ck_ref.shape[1])

    def attend(count):
        keys = slice(0, count * GB)
        put_bias(bias_ref, places, starts, count)

        def head(h, band, one):
            q, dctx = q_ref[band, :], dctx_all[block, band, :]
            s = nn(ck_ref[h, keys, :], q) * scale + jnp.concatenate([bias_ref[keys, :]] * 3, axis=1)
            p = jnp.exp2(s - lse_all[block, one, :])
            dp = nn(cv_ref[h, keys, :], dctx)
            ds = (p * (dp - delta_all[block, one, :])).astype(BF16)
            dcv_sum[h, keys, :] += nt(p.astype(BF16), dctx)
            dck_sum[h, keys, :] += nt(ds, q)
            dq_sum[band, :] = nn(ckt_ref[band, keys], ds)

        each_head(heads, hd, head)

    for n in range(ck_ref.shape[1] // GB):
        pl.when(block == n)(functools.partial(attend, n + 1))
    mask = stats_ref[heads : heads + 1, :]
    rows = key_rows(block)
    for h in range(heads):
        band = slice(h * hd, (h + 1) * hd)
        one = slice(h, h + 1)
        q, k = q_ref[band, :].astype(F32), k_ref[band, :].astype(F32)
        v, dctx = v_ref[band, :].astype(F32), dctx_all[block, band, :].astype(F32)
        own_prob = jnp.exp2(jnp.sum(q * k, axis=0, keepdims=True) * scale - lse_all[block, one, :])
        own_dprob = jnp.sum(dctx * v, axis=0, keepdims=True)
        own_dscore = own_prob * (own_dprob - delta_all[block, one, :]) * factor
        slot, i = divmod(h, slot_heads)
        base = slot * 3 * lanes + i * hd
        dqkv[base : base + hd, :] = (dq_sum[band, :] * factor + own_dscore * k).astype(BF16)
        dck = (dck_sum[h, rows, :] * factor).astype(BF16)
        dcv = dcv_sum[h, rows, :].astype(BF16)
        for n, src, total, grad, beside in (
            (0, k_ref, kconv_sum, dck, own_dscore * q),
            (1, v_ref, vconv_sum, dcv, own_prob * dctx),
        ):
            spread = nt(convs_ref[n, h], grad)
            spread = jnp.concatenate([spread[r * hd : (r + 1) * hd] for r in range(3)], axis=1)
            at = base + (n + 1) * lanes
            dqkv[at : at + hd, :] = ((spread + beside) * mask).astype(BF16)
            if h < own_heads:
                grouped = jnp.concatenate([src[band, r * GB : (r + 1) * GB] for r in range(3)], axis=0)
                total[h] += nn(grouped, grad)
    hat, inv_std = norm_rows(x_ref[...].astype(F32))
    gain = gain_ref[...]
    first_in = (hat * gain).astype(BF16)
    weight_sum[...] += nn(dqkv[0 : 3 * own, :], first_in)
    back = tn(dqkv[...], w_ref[...].reshape(slots * 3 * lanes, dim))
    gain_sum[...] += jnp.sum(back * hat, axis=0, keepdims=True)
    total = resid_all[block].astype(F32) + norm_back(back, gain, hat, inv_std)
    swap.send(block, total.astype(BF16))


def schedule(step, blocks):
    late = (step + 3) // (2 * blocks)
    started = (step + 2 * blocks - 1) // (2 * blocks)
    last = (step + 4) // (2 * blocks)
    forward = started * (1 - last) * (blocks - 1 - (step + 1) // 2)
    forward = forward + (1 - started) * (blocks - 1)
    backward = started * ((1 - late) * (blocks - step // 2) + late * (2 * blocks - 1 - step))
    backward = backward + (1 - started) * (blocks - 1)
    backward = jnp.minimum(backward, blocks - 1)
    is_forward = (1 - started) + started * (1 - late) * ((step % 2) * (1 - last) + last * (1 - late))
    return forward, backward, is_forward


def later_kernel(
    heads, hd, own_heads, lens_ref,
    x_ref, g_ref, gain2_ref, ctx_ref, out_ref, up_ref, down_ref, out_far, up_hbm, down_hbm,
    q_front, k_front, v_front,
    x_back, gain1_ref, q_ref, k_ref, v_ref, lse_ref, w_hbm, conv_hbm, ck_hbm, ckt_hbm, cv_hbm, cvt_hbm,
    mixed_ref, mixed_peer, tokens_ref, tokens_peer, middle_out, last_out, conv_out,
    up_far, down_far, w_ref, conv_ref, ck_ref, ckt_ref, cv_ref, cvt_ref,
    mixed_staged, acts, hidden_grads, pre, act_grads, ff_sum, out_sum, gain2_sum,
    ctx_block, lse_all, dctx_all, resid_all, delta_all,
    bias_ref, convs_ref, dck_sum, dcv_sum, dq_sum, dqkv, weight_sum, kconv_sum, vconv_sum, gain1_sum,
    middle_parts, middle_pair, middle_in, last_parts, last_pair, last_in, conv_parts, conv_pair, conv_in,
    middle_turn, last_turn, conv_turn, middle_sum, last_sum, conv_sum,
    mixed_sems, mixed_local, swap_sems, swap_local, middle_sems, last_sems, conv_sems, turn_sems, load_sems,
):
    step_id = pl.program_id(0)
    blocks = dctx_all.shape[0]
    forward_block, backward_block, is_forward = schedule(step_id, blocks)
    mixed_swap = Swap(mixed_staged, mixed_ref, mixed_peer, mixed_sems, mixed_local)
    swap = Swap(resid_all, tokens_ref, tokens_peer, swap_sems, swap_local)
    middle = Spread(middle_parts, middle_pair, middle_in, middle_sum, middle_sems)
    last = Spread(last_parts, last_pair, last_in, last_sum, last_sems)
    convs = Spread(conv_parts, conv_pair, conv_in, conv_sum, conv_sems)
    slots, _, dim = w_ref.shape
    taps = convs_ref.shape[2]
    conv_cols = conv_ref.shape[2] // 2
    slot_heads = heads // slots

    loads = [
        pltpu.make_async_copy(src, dst, load_sems.at[n])
        for n, (src, dst) in enumerate(
            (
                (up_hbm, up_far), (down_hbm, down_far), (w_hbm, w_ref), (conv_hbm, conv_ref), (ck_hbm, ck_ref), (ckt_hbm, ckt_ref), (cv_hbm, cv_ref),
                (cvt_hbm, cvt_ref),
            )
        )
    ]

    @pl.when(step_id == 0)
    def _():
        for load in loads:
            load.start()
        count = lax.axis_size("dp")
        me, peer = lax.axis_index("dp"), lax.axis_index("tensor")
        devices = [swap.device, (me ^ 1, peer)] + [(lax.rem(me + 2 * s, count), peer) for s in range(1, count // 2)]
        greet(devices)
        for ref in (ff_sum, out_sum, gain2_sum):
            ref[...] = jnp.zeros_like(ref)
        for load in loads[:2]:
            load.wait()
        greeted(devices)

    @pl.when(step_id == 2)
    def _():
        for load in loads[2:]:
            load.wait()
        for ref in (dck_sum, dcv_sum, weight_sum, kconv_sum, vconv_sum, gain1_sum):
            ref[...] = jnp.zeros_like(ref)
        for h in range(heads):
            slot, i = divmod(h, slot_heads)
            for n in range(2):
                conv = conv_ref[slot, i * hd : (i + 1) * hd, n * conv_cols : n * conv_cols + taps]
                convs_ref[n, h] = conv.astype(F32).T.astype(BF16)

    longest_here = lax.rem(lax.axis_index("tensor"), 2) == 0

    @pl.when(is_forward == 1)
    def _():
        places, starts = item_starts(lens_ref, forward_block, longest_here, ck_ref.shape[1])

        def put_lse(one, values):
            lse_all[forward_block, one, :] = values

        @pl.when(forward_block >= blocks // 2)
        def _():
            ctx_block[...] = ctx_ref[...]

        for n in range(blocks // 2):
            pl.when(forward_block == n)(
                functools.partial(
                    attend_forward, heads, hd, n + 1, places, starts, bias_ref, ck_ref, cvt_ref, q_front, k_front,
                    v_front, ctx_block, put_lse,
                )
            )
        feed_forward(
            heads, hd, forward_block, mixed_swap, x_ref, g_ref, gain2_ref, ctx_block, out_ref, up_ref, down_ref,
            out_far, up_far, down_far, resid_all, dctx_all, delta_all, middle_parts,
            acts, hidden_grads, pre, act_grads, ff_sum, out_sum, gain2_sum,
        )

        @pl.when(forward_block == 0)
        def _():
            middle.start()

    @pl.when(is_forward == 0)
    def _():
        @pl.when(backward_block >= blocks // 2)
        def _():
            lse_all[backward_block] = lse_ref[0:heads, :]

        attention_back(
            heads, hd, own_heads, lens_ref, backward_block, swap, x_back, gain1_ref, w_ref, q_ref, k_ref, v_ref, lse_ref,
            lse_all, dctx_all, delta_all, resid_all, ck_ref, ckt_ref, cv_ref,
            bias_ref, convs_ref, dck_sum, dcv_sum, dq_sum, dqkv, weight_sum, kconv_sum, vconv_sum, gain1_sum,
        )

    @pl.when((is_forward == 0) & (backward_block == blocks // 2 - 1))
    def _():
        middle.pass_on()

    def turned(n, ref):
        return remote(ref.at[0], ref.at[1], turn_sems, (n,), swap.device)

    def turn(n, ref, total):
        ref[0] = total[:, total.shape[1] - ref.shape[2] :].astype(BF16)
        turned(n, ref).start()

    @pl.when(step_id == 2 * blocks - 1)
    def _():
        put_rows(last_parts, [weight_sum[...].T, jnp.broadcast_to(gain1_sum[...], (GB, dim)).T])
        last.start()
        put_rows(
            conv_parts,
            [
                total[h]
                for slot in range(2)
                for total in (kconv_sum, vconv_sum)
                for h in range(slot * slot_heads, (slot + 1) * slot_heads)
            ],
        )
        convs.start()
        turn(0, middle_turn, middle.total())
        last.pass_on()
        convs.pass_on()
        sums = ((middle_out, middle_turn, middle), (last_out, last_turn, last), (conv_out, conv_turn, convs))
        for n, (_, ref, spread) in enumerate(sums):
            if n > 0:
                turn(n, ref, spread.total())
        for n, (out, ref, spread) in enumerate(sums):
            turned(n, ref).wait()
            total, cols = spread.sums, out.shape[1]
            split = total.shape[1] - cols
            kept = [total[:, :split]] + ([total[:, 2 * split :]] if cols > split else [])
            out[...] = ref[1].astype(F32) + jnp.concatenate(kept, axis=1)
        mixed_swap.finish()
        swap.finish()


def place_rows(lens_ref, longest_here, mine, theirs, natural, out_ref):
    half = mine.shape[0]
    first = longest_first(lens_ref, half // 3)

    def taps(block, r, other):
        rows = slice(block * TB + r * GB, block * TB + (r + 1) * GB)
        a, b = mine[rows, :].astype(F32), theirs[rows, :].astype(F32)
        return jnp.where(longest_here == other, b, a)

    parts = natural.shape[0]
    for block in range(half // TB):
        for r in range(3):
            others = taps(block, r, True)
            for c in range(parts):
                for base in (0, half):
                    natural[c, pl.ds(base + block * TB + r, GB, stride=3), :] = others[:, c * 128 : (c + 1) * 128]
    for block in range(half // TB):
        for r in range(3):
            longest = taps(block, r, False)
            for c in range(parts):
                natural[c, pl.ds(first + block * TB + r, GB, stride=3), :] = longest[:, c * 128 : (c + 1) * 128]
    for c in range(parts):
        out_ref[:, c * 128 : (c + 1) * 128] = natural[c, 0 : 2 * half, :].astype(BF16)


def last_kernel(
    hd, lens_ref, mixed_ref, mixed_peer, tokens_ref, tokens_peer, middle_ref, last_ref, conv_ref,
    mixed_out, tokens_out, gain1_out, gain2_out, query_out, key_out, value_out, out_out, kconv_out, vconv_out,
    up_out, down_out, natural_mixed, natural_tokens,
):
    longest_here = lax.rem(lax.axis_index("tensor"), 2) == 0
    place_rows(lens_ref, longest_here, mixed_ref, mixed_peer, natural_mixed, mixed_out)
    place_rows(lens_ref, longest_here, tokens_ref, tokens_peer, natural_tokens, tokens_out)

    @pl.when(pl.program_id(0) == 0)
    def _():
        units, own = up_out.shape[1], query_out.shape[1]
        up_out[...] = middle_ref[:, 0:units]
        down_out[...] = middle_ref[:, units : 2 * units]
        out_out[...] = middle_ref[:, 2 * units : 2 * units + own]
        gain2_out[...] = middle_ref[:, 2 * units + own :].T[0:1]
        for n, out in enumerate((query_out, key_out, value_out)):
            out[...] = last_ref[:, n * own : (n + 1) * own]
        gain1_out[...] = last_ref[:, 3 * own :].T[0:1]
        for n, out in enumerate((kconv_out, vconv_out)):
            for h in range(out.shape[0]):
                out[h] = conv_ref[:, n * own + h * hd : n * own + (h + 1) * hd]


def whole(shape):
    return pl.BlockSpec(shape, lambda *_: (0,) * len(shape))


def cost(micros):
    return pl.CostEstimate(flops=int(micros * 1e9), bytes_accessed=1 << 20, transcendentals=0)


def params():
    return pltpu.CompilerParams(vmem_limit_bytes=VMEM, dimension_semantics=("arbitrary",))


def on_device(
    tokens, first_gain, second_gain, query_weight, key_weight, value_weight, out_weight,
    key_conv, value_conv, up_weight, down_weight, pad_mask, item_lengths, cotangent,
):
    dim = tokens.shape[1]
    own_heads, taps, hd = key_conv.shape
    peers = lax.axis_size("tensor")
    heads = own_heads * peers
    width = heads * hd
    own = own_heads * hd
    units = up_weight.shape[1]
    lens = item_lengths[0]
    rows = tokens.shape[0] // 2
    blocks = rows // TB
    groups = rows // 3
    pads = pad_mask.reshape(-1, 128)
    key_conv, value_conv = key_conv.transpose(0, 2, 1), value_conv.transpose(0, 2, 1)
    conv_cols = -(-taps // 128) * 128
    stats = heads + 8
    gain1, gain2 = first_gain[None], second_gain[None]

    rows_spec = pl.BlockSpec((TB, dim), lambda b, *_: (b, 0))
    cols_spec = pl.BlockSpec((width, TB), lambda b, *_: (0, b))
    stat_spec = pl.BlockSpec((heads, TB), lambda b, *_: (0, b))
    lse_spec = pl.BlockSpec((stats, TB), lambda b, *_: (0, b))
    early = blocks // 2
    late_cols = pl.BlockSpec((width, TB), lambda b, *_: (0, jnp.maximum(b - early, 0)))
    anywhere = pl.BlockSpec(memory_space=pl.ANY)
    inside = pl.BlockSpec(memory_space=pltpu.VMEM)
    q, k, v, ctx, lse, x, g, ck, ckt, cv, cvt, w_all, conv_all, out_far, up_far, down_far = pl.pallas_call(
        functools.partial(forward_kernel, heads, hd),
        grid_spec=pltpu.PrefetchScalarGridSpec(
            num_scalar_prefetch=1,
            grid=(blocks,),
            in_specs=[inside, inside, whole((1, dim))] + [inside] * 6 + [anywhere] * 3,
            out_specs=[
                cols_spec, cols_spec, cols_spec, late_cols, lse_spec,
            ]
            + [anywhere] * 11,
            scratch_shapes=[
                pltpu.VMEM((dim // 128 + 1, 2 * rows + 8, 128), F32), pltpu.VMEM((dim // 128, 2 * rows + 8, 128), F32),
                pltpu.VMEM((rows, dim), BF16), pltpu.VMEM((rows, dim), BF16),
                pltpu.VMEM((heads, groups, hd), BF16), pltpu.VMEM((width, groups), BF16),
                pltpu.VMEM((heads, groups, hd), BF16), pltpu.VMEM((width, groups), BF16),
                pltpu.VMEM((blocks, TB, dim), BF16), pltpu.VMEM((blocks, 8, TB), F32),
                pltpu.VMEM((peers, 3 * own, dim), BF16), pltpu.VMEM((peers, own, 2 * conv_cols), BF16),
                pltpu.VMEM((groups, GB), F32),
                pltpu.SemaphoreType.DMA((2, 2, 5, peers - 1)), pltpu.SemaphoreType.DMA((2, 3, 5, peers - 1)),
                pltpu.SemaphoreType.DMA((8,)),
            ],
        ),
        out_shape=[jax.ShapeDtypeStruct((width, rows), BF16)] * 3
        + [
            jax.ShapeDtypeStruct((width, (blocks - early) * TB), BF16),
            jax.ShapeDtypeStruct((stats, rows), F32),
            jax.ShapeDtypeStruct((rows, dim), BF16),
            jax.ShapeDtypeStruct((rows, dim), BF16),
            jax.ShapeDtypeStruct((heads, groups, hd), BF16),
            jax.ShapeDtypeStruct((width, groups), BF16),
            jax.ShapeDtypeStruct((heads, groups, hd), BF16),
            jax.ShapeDtypeStruct((width, groups), BF16),
            jax.ShapeDtypeStruct((peers, 3 * own, dim), BF16),
            jax.ShapeDtypeStruct((peers, own, 2 * conv_cols), BF16),
            jax.ShapeDtypeStruct((peers - 1, own, dim), BF16),
            jax.ShapeDtypeStruct((peers - 1, dim, units), BF16),
            jax.ShapeDtypeStruct((peers - 1, units, dim), BF16),
        ],
        compiler_params=pltpu.CompilerParams(
            vmem_limit_bytes=VMEM, dimension_semantics=("arbitrary",), collective_id=0, has_side_effects=True
        ),
        cost_estimate=cost(55),
        name="attention_forward",
    )(
        lens, tokens, cotangent, gain1, pads, query_weight, key_weight, value_weight, key_conv, value_conv,
        out_weight, up_weight, down_weight,
    )

    count = lax.axis_size("dp")
    slot_cols = 2 * units + own
    mid_cols = 2 * slot_cols + GB
    last_cols = 6 * own + GB
    two = 2 * own_heads
    step = 256

    def forward_at(n):
        return schedule(n, blocks)[0]

    def backward_at(n):
        return schedule(n, blocks)[1]

    def left_at(n):
        return jnp.minimum(forward_at(n), early - 1)

    left_cols = pl.BlockSpec((width, TB), lambda n, *_: (0, left_at(n)))
    front_rows = pl.BlockSpec((TB, dim), lambda n, *_: (forward_at(n), 0))
    front_cols = pl.BlockSpec((width, TB), lambda n, *_: (0, jnp.maximum(forward_at(n) - early, 0)))
    back_rows = pl.BlockSpec((TB, dim), lambda n, *_: (backward_at(n), 0))
    back_cols = pl.BlockSpec((width, TB), lambda n, *_: (0, backward_at(n)))
    back_lse = pl.BlockSpec((stats, TB), lambda n, *_: (0, backward_at(n)))
    out_dims = [(dim // count, slot_cols + GB), (dim // count, 3 * own + GB), (taps // count, 2 * own)]
    swap_sems = [pltpu.SemaphoreType.DMA((2, blocks)), pltpu.SemaphoreType.DMA((blocks,))]
    spread_sems = pltpu.SemaphoreType.DMA((2, count // 2))
    split = [(dim // count, mid_cols), (dim // count, last_cols), (taps // count, 4 * own)]
    mixed, mixed_peer, grad_rows, grad_peer, middle_share, last_share, conv_share = pl.pallas_call(
        functools.partial(later_kernel, heads, hd, two),
        grid_spec=pltpu.PrefetchScalarGridSpec(
            num_scalar_prefetch=1,
            grid=(2 * blocks,),
            in_specs=[front_rows, front_rows, inside, front_cols]
            + [inside] * 4
            + [anywhere] * 2
            + [left_cols] * 3
            + [back_rows, inside, back_cols, back_cols, back_cols, back_lse]
            + [anywhere] * 6,
            out_specs=[anywhere] * 4 + [whole(d) for d in out_dims],
            scratch_shapes=[
                pltpu.VMEM((peers - 1, dim, units), BF16), pltpu.VMEM((peers - 1, units, dim), BF16),
                pltpu.VMEM((peers, 3 * own, dim), BF16), pltpu.VMEM((peers, own, 2 * conv_cols), BF16),
                pltpu.VMEM((heads, groups, hd), BF16), pltpu.VMEM((width, groups), BF16),
                pltpu.VMEM((heads, groups, hd), BF16), pltpu.VMEM((width, groups), BF16),
                pltpu.VMEM((blocks, TB, dim), BF16),
                pltpu.VMEM((TB, peers * units), BF16), pltpu.VMEM((TB, peers * units), BF16),
                pltpu.VMEM((2, TB, step), F32), pltpu.VMEM((2, TB, step), F32),
                pltpu.VMEM((2, 2, dim, units), F32), pltpu.VMEM((2 * own, dim), F32), pltpu.VMEM((1, dim), F32),
                pltpu.VMEM((width, TB), BF16), pltpu.VMEM((blocks, heads, TB), F32),
                pltpu.VMEM((blocks, width, TB), BF16), pltpu.VMEM((blocks, TB, dim), BF16),
                pltpu.VMEM((blocks, heads, TB), F32),
                pltpu.VMEM((groups, GB), F32),
                pltpu.VMEM((2, heads, taps, hd), BF16), pltpu.VMEM((heads, groups, hd), F32),
                pltpu.VMEM((heads, groups, hd), F32), pltpu.VMEM((width, TB), F32),
                pltpu.VMEM((3 * width, TB), BF16), pltpu.VMEM((6 * own, dim), F32),
                pltpu.VMEM((two, taps, hd), F32), pltpu.VMEM((two, taps, hd), F32),
                pltpu.VMEM((1, dim), F32),
            ]
            + [pltpu.VMEM((*lead, *d), BF16) for d in split for lead in ((2, count // 2), (count // 2,), (count // 2,))]
            + [pltpu.VMEM((2, *d), BF16) for d in out_dims]
            + [pltpu.VMEM(d, F32) for d in split]
            + swap_sems * 2
            + [spread_sems] * 3
            + [pltpu.SemaphoreType.DMA((2, 3)), pltpu.SemaphoreType.DMA((8,))],
        ),
        out_shape=[jax.ShapeDtypeStruct((rows, dim), BF16)] * 4 + [jax.ShapeDtypeStruct(d, F32) for d in out_dims],
        compiler_params=pltpu.CompilerParams(
            vmem_limit_bytes=VMEM, dimension_semantics=("arbitrary",), collective_id=1, has_side_effects=True
        ),
        cost_estimate=cost(110),
        name="feed_forward_and_backward",
    )(
        lens, x, g, gain2, ctx, out_weight, up_weight, down_weight, out_far.reshape(width - own, dim), up_far, down_far,
        q, k, v, x, gain1, q, k, v, lse, w_all, conv_all, ck, ckt, cv, cvt,
    )

    share = dim // count
    own_conv = (own_heads, taps // count, hd)
    shapes = [
        ((1, share), F32), ((1, share), F32), ((share, own), F32), ((share, own), F32), ((share, own), F32),
        ((share, own), F32), (own_conv, F32), (own_conv, F32), ((share, units), F32), ((share, units), F32),
    ]
    lanes = 256
    lane_half = pl.BlockSpec((rows, lanes), lambda c: (0, c))
    lane_all = pl.BlockSpec((2 * rows, lanes), lambda c: (0, c))
    outs = pl.pallas_call(
        functools.partial(last_kernel, hd),
        grid=(dim // lanes,),
        in_specs=[pl.BlockSpec(memory_space=pltpu.SMEM)] + [lane_half] * 4 + [whole(d) for d in out_dims],
        out_specs=[lane_all] * 2 + [whole(d) for d, _ in shapes],
        out_shape=[jax.ShapeDtypeStruct((2 * rows, dim), BF16)] * 2 + [jax.ShapeDtypeStruct(d, t) for d, t in shapes],
        scratch_shapes=[pltpu.VMEM((lanes // 128, 2 * rows + 8, 128), F32)] * 2,
        compiler_params=params(),
        cost_estimate=cost(15),
        name="in_order",
    )(lens, mixed, mixed_peer, grad_rows, grad_peer, middle_share, last_share, conv_share)
    mixed, grad_tokens, gain1, gain2, query, key, value, out, kconv, vconv, up, down = outs
    return (
        mixed, grad_tokens, gain1.reshape(share), gain2.reshape(share), query, key, value, out.T,
        kconv, vconv, up, down.T,
    )


def solution(mesh):
    in_specs = (
        P("dp", None),
        P(),
        P(),
        P(None, "tensor"),
        P(None, "tensor"),
        P(None, "tensor"),
        P("tensor", None),
        P("tensor", None, None),
        P("tensor", None, None),
        P(None, "tensor"),
        P("tensor", None),
        P("dp"),
        P("dp", None),
        P("dp", None),
    )
    out_specs = (
        P("dp", None),
        P("dp", None),
        P("dp"),
        P("dp"),
        P("dp", "tensor"),
        P("dp", "tensor"),
        P("dp", "tensor"),
        P("tensor", "dp"),
        P("tensor", "dp", None),
        P("tensor", "dp", None),
        P("dp", "tensor"),
        P("tensor", "dp"),
    )
    return jax.shard_map(
        on_device, mesh=mesh, in_specs=in_specs, out_specs=out_specs, check_vma=False
    )
```

```python
import functools
import math

import jax
import jax.numpy as jnp
from jax import lax
from jax.experimental import pallas as pl
from jax.experimental.pallas import tpu as pltpu
from jax.sharding import PartitionSpec as P

F32 = jnp.float32
BF16 = jnp.bfloat16
GB = 128
TB = 3 * GB
NEG = -1e30
LOG2E = 1.0 / math.log(2.0)
VMEM = 60 * 1024 * 1024

ERF_P = 0.43
ERF_C = (
    0.24255178053871013,
    0.24376598744271377,
    0.2089868288055898,
    0.23281685899157548,
    -0.05797941172752005,
    0.3523368029188165,
    -0.2915198548110903,
    0.06904073943922798,
)


def nn(a, b):
    return lax.dot_general(a, b, (((1,), (0,)), ((), ())), preferred_element_type=F32)


def nt(a, b):
    return lax.dot_general(a, b, (((1,), (1,)), ((), ())), preferred_element_type=F32)


def tn(a, b):
    return lax.dot_general(a, b, (((0,), (0,)), ((), ())), preferred_element_type=F32)


def norm_rows(values):
    centred = values - jnp.mean(values, -1, keepdims=True)
    inv_std = lax.rsqrt(jnp.mean(centred * centred, -1, keepdims=True) + 1e-05)
    return centred * inv_std, inv_std


def norm_back(grad_out, gains, normed, inv_std):
    scaled = grad_out * gains
    return inv_std * (
        scaled
        - jnp.mean(scaled, -1, keepdims=True)
        - normed * jnp.mean(scaled * normed, -1, keepdims=True)
    )


def gelu_and_slope(h):
    t = 1.0 / (1.0 + (ERF_P * math.sqrt(0.5)) * jnp.abs(h))
    poly = t * (0.5 * ERF_C[-1]) + 0.5 * ERF_C[-2]
    for c in ERF_C[-3::-1]:
        poly = poly * t + 0.5 * c
    e = jnp.exp2((h * h) * (-0.5 * LOG2E))
    tail = e * (poly * t)
    cdf = jnp.where(h >= 0, 1.0 - tail, tail)
    return h * cdf, cdf + h * (e * (1.0 / math.sqrt(2.0 * math.pi)))


def item_starts(lens_ref, block, longest_here, half):
    places = block * GB + lax.broadcasted_iota(jnp.int32, (1, GB), 1)
    starts = jnp.zeros((1, GB), jnp.int32)
    end = jnp.int32(0)
    for i in range(lens_ref.shape[0] - 1):
        end = end + jnp.where((lens_ref[i] == half) == longest_here, lens_ref[i], 0)
        starts = jnp.where(places >= end, end, starts)
    return places, starts


def longest_first(lens_ref, half):
    first, ahead = jnp.int32(0), jnp.int32(1)
    for i in range(lens_ref.shape[0]):
        ahead = jnp.where(lens_ref[i] == half, 0, ahead)
        first = first + ahead * lens_ref[i]
    return 3 * first


def own_taps(source, half, block, first, longest_here):
    base = block * TB
    parts = []
    for c in range(source.shape[0]):
        for r in range(3):
            inside = source[c, pl.ds(first + base + r, GB, stride=3), :]
            low = source[c, pl.ds(base + r, GB, stride=3), :]
            high = source[c, pl.ds(half + base + r, GB, stride=3), :]
            place = base + r + 3 * lax.broadcasted_iota(jnp.int32, (GB, 1), 0)
            parts.append(jnp.where(longest_here, inside, jnp.where(place < first, low, high)))
    return jnp.concatenate(
        [jnp.concatenate(parts[3 * c : 3 * c + 3], axis=0) for c in range(source.shape[0])], axis=1
    )


def put_bias(bias_ref, places, starts, count):
    for kb in range(count):
        keys = kb * GB + lax.broadcasted_iota(jnp.int32, (GB, GB), 0)
        bias_ref[kb * GB : (kb + 1) * GB, :] = jnp.where((keys >= starts) & (keys < places), 0.0, NEG)


def each_head(heads, hd, work):
    def some(i, carry):
        for n in range(2):
            h = 2 * i + n
            work(h, pl.ds(pl.multiple_of(h * hd, hd), hd), pl.ds(h, 1))
        return carry

    lax.fori_loop(0, heads // 2, some, 0)


def key_rows(kb):
    return pl.ds(pl.multiple_of(kb * GB, GB), GB)


def remote(src, dst, sems, at, device):
    return pltpu.make_async_remote_copy(
        src_ref=src, dst_ref=dst, send_sem=sems.at[(0, *at)], recv_sem=sems.at[(1, *at)],
        device_id=device, device_id_type=pl.DeviceIdType.MESH,
    )


def greet(devices):
    barrier = pltpu.get_barrier_semaphore()
    for device in devices:
        pl.semaphore_signal(barrier, inc=1, device_id=device, device_id_type=pl.DeviceIdType.MESH)


def greeted(devices):
    pl.semaphore_wait(pltpu.get_barrier_semaphore(), len(devices))


def put_rows(ref, pieces, at=0):
    parities, count, rows, _ = ref.shape
    for piece in pieces:
        cols = piece.shape[1]
        for d in range(parities * count):
            ref[d % 2, d // 2, :, at : at + cols] = piece[d * rows : (d + 1) * rows].astype(ref.dtype)
        at += cols


class Swap:
    def __init__(self, staged, mine, theirs, sems, local_sems):
        self.staged, self.mine, self.theirs, self.sems, self.local_sems = staged, mine, theirs, sems, local_sems
        self.device = (lax.axis_index("dp"), lax.axis_index("tensor") ^ 1)
        self.blocks = mine.shape[0] // TB

    def rows(self, block):
        return pl.ds(pl.multiple_of(block * TB, TB), TB)

    def local(self, block):
        return pltpu.make_async_copy(
            self.staged.at[block], self.mine.at[self.rows(block)], self.local_sems.at[block]
        )

    def far(self, block):
        return remote(
            self.staged.at[block], self.theirs.at[self.rows(block)], self.sems, (block,), self.device
        )

    def send(self, block, values):
        self.staged[block] = values
        self.local(block).start()
        self.far(block).start()

    def finish(self):
        for block in range(self.blocks):
            self.local(block).wait()
            self.far(block).wait()


class Spread:
    def __init__(self, source, paired, landed, sums, sems):
        self.source, self.paired, self.landed, self.sums, self.sems = source, paired, landed, sums, sems
        self.me, self.peer = lax.axis_index("dp"), lax.axis_index("tensor")
        self.parity = lax.rem(self.me, 2)
        self.count = lax.axis_size("dp")

    def beside(self):
        return remote(
            self.source.at[1 - self.parity], self.paired, self.sems, (0,), (self.me ^ 1, self.peer)
        )

    def copy(self, s):
        there = lax.rem(self.me + 2 * s, self.count)
        return remote(self.paired.at[there // 2], self.landed.at[s], self.sems, (s,), (there, self.peer))

    def start(self):
        self.beside().start()

    def pass_on(self):
        self.beside().wait()

        def add(n, carry):
            pair = self.paired[n].astype(F32) + self.source[self.parity, n].astype(F32)
            self.paired[n] = pair.astype(BF16)
            return carry

        lax.fori_loop(0, self.count // 2, add, 0)

        def step(s, carry):
            self.copy(s).start()
            return carry

        lax.fori_loop(1, self.count // 2, step, 0)

    def total(self):
        def step(s, carry):
            self.copy(s).wait()
            return carry

        lax.fori_loop(1, self.count // 2, step, 0)
        self.sums[...] = self.paired[self.me // 2].astype(F32)

        def add(s, carry):
            self.sums[...] += self.landed[s].astype(F32)
            return carry

        lax.fori_loop(1, self.count // 2, add, 0)
        return self.sums


class Gather:
    def __init__(self, own, far, sems):
        self.own, self.far, self.sems = own, far, sems
        self.dp, self.tensor = lax.axis_index("dp"), lax.axis_index("tensor")
        self.peers = lax.axis_size("tensor")

    def devices(self):
        return [(self.dp, self.tensor ^ s) for s in range(1, self.peers)] + [
            (self.dp ^ m, self.tensor) for m in (1, 2, 4, 6)
        ]

    def eighth(self, array):
        rows = array.shape[0] // 8
        place = lax.rem(self.dp, 2) * 4 + lax.rem(self.dp, 8) // 2
        return array.at[pl.ds(pl.multiple_of(place * rows, rows), rows)]

    def half(self, array):
        rows = array.shape[0] // 2
        return array.at[pl.ds(pl.multiple_of(lax.rem(self.dp, 2) * rows, rows), rows)]

    def across(self, n, s):
        device = (self.dp, self.tensor ^ s)
        return remote(
            self.eighth(self.own[n]), self.eighth(self.far[n].at[s - 1]), self.sems, (n, 0, s - 1), device
        )

    def around(self, n, s, m):
        part = self.eighth(self.far[n].at[s - 1])
        return remote(part, part, self.sems, (n, m // 2, s - 1), (self.dp ^ m, self.tensor))

    def beside(self, n, s):
        part = self.half(self.far[n].at[s - 1])
        return remote(part, part, self.sems, (n, 4, s - 1), (self.dp ^ 1, self.tensor))

    def each(self, s=None):
        peers = range(1, self.peers) if s is None else (s,)
        return [(n, s) for s in peers for n in range(len(self.far))]

    def start(self):
        for n, s in self.each():
            self.across(n, s).start()

    def pass_around(self, s=None):
        for n, s in self.each(s):
            self.across(n, s).wait_recv()
            for m in (6, 4, 2):
                self.around(n, s, m).start()

    def pass_beside(self, s=None):
        for n, s in self.each(s):
            for m in (2, 4, 6):
                self.around(n, s, m).wait_recv()
            self.beside(n, s).start()

    def arrive(self):
        for n, s in self.each():
            self.beside(n, s).wait_recv()

    def finish(self):
        for n, s in self.each():
            self.across(n, s).wait_send()
            for m in (2, 4, 6):
                self.around(n, s, m).wait_send()
            self.beside(n, s).wait_send()


def attend_forward(
    heads, hd, count, places, starts, bias_ref, ck_ref, cvt_ref, q_ref, k_ref, v_ref, ctx_ref, put_lse
):
    scale = LOG2E / math.sqrt(hd)
    keys = slice(0, count * GB)
    put_bias(bias_ref, places, starts, count)

    def head(h, band, one):
        q = q_ref[band, :]
        own_score = jnp.sum(q.astype(F32) * k_ref[band, :].astype(F32), axis=0, keepdims=True) * scale
        s = nn(ck_ref[h, keys, :], q) * scale + jnp.concatenate([bias_ref[keys, :]] * 3, axis=1)
        top = jnp.maximum(own_score, jnp.max(s, axis=0, keepdims=True))
        p = jnp.exp2(s - top)
        own_prob = jnp.exp2(own_score - top)
        total = own_prob + jnp.sum(p, axis=0, keepdims=True)
        mixed = own_prob * v_ref[band, :].astype(F32) + nn(cvt_ref[band, keys], p.astype(BF16))
        ctx_ref[band, :] = (mixed * (1.0 / total)).astype(BF16)
        put_lse(one, top + jnp.log(total) * LOG2E)

    each_head(heads, hd, head)


def forward_kernel(
    heads, hd, lens_ref, x_ref, g_ref, gain_ref, pad_ref, query_ref, key_ref, value_ref, kconv_ref, vconv_ref,
    out_ref, up_ref, down_ref,
    q_ref, k_ref, v_ref, ctx_ref, lse_ref, x_all, g_all, ck_all, ckt_all, cv_all, cvt_all, w_all, conv_all,
    out_far, up_far, down_far,
    xs, gs, x_own, g_own, ck_ref, ckt_ref, cv_ref, cvt_ref, first_all, mask_rows, w_ref, conv_ref, bias_ref, first_sems, last_sems, local_sems,
):
    block = pl.program_id(0)
    blocks = pl.num_programs(0)
    own_heads, _, taps = kconv_ref.shape
    own = own_heads * hd
    dim = x_ref.shape[1]
    conv_cols = conv_ref.shape[2] // 2
    first_gather = Gather((w_ref.at[0], conv_ref.at[0]), (w_ref.at[1:], conv_ref.at[1:]), first_sems)
    last_gather = Gather((out_ref, up_ref, down_ref), (out_far, up_far, down_far), last_sems)
    kept = ((w_ref, w_all), (conv_ref, conv_all), (x_own, x_all), (g_own, g_all))
    kept += ((ck_ref, ck_all), (ckt_ref, ckt_all), (cv_ref, cv_all), (cvt_ref, cvt_all))
    keep_copies = [pltpu.make_async_copy(src, dst, local_sems.at[n]) for n, (src, dst) in enumerate(kept)]
    half = x_ref.shape[0] // 2
    blocks_there = half // TB
    longest_here = lax.rem(lax.axis_index("tensor"), 2) == 0
    first = longest_first(lens_ref, half // 3)

    @pl.when(block == 0)
    def _():
        greet(first_gather.devices())
        for n, src in enumerate((query_ref, key_ref, value_ref)):
            w_ref[0, n * own : (n + 1) * own, :] = src[...].T
        conv_ref[0] = jnp.zeros_like(conv_ref[0])
        for n, src in enumerate((kconv_ref, vconv_ref)):
            for h in range(own_heads):
                conv_ref[0, h * hd : (h + 1) * hd, n * conv_cols : n * conv_cols + taps] = src[h]
        greeted(first_gather.devices())
        first_gather.start()
        for src, dst in ((x_ref, xs), (g_ref, gs)):
            for c in range(dim // 128):
                dst[c, 0 : 2 * half, :] = src[:, c * 128 : (c + 1) * 128].astype(F32)
        pads = pad_ref[...].astype(F32).T
        for c in range(pads.shape[1]):
            xs[dim // 128, c * 128 : (c + 1) * 128, :] = jnp.broadcast_to(pads[:, c : c + 1], (128, 128))
        first_gather.pass_around()
        last_gather.start()

        def prepare(n, carry):
            x = own_taps(xs, half, n, first, longest_here)
            mask_rows[n] = jnp.broadcast_to(x[:, dim:].T[0:1], mask_rows.shape[1:])
            x = x[:, :dim]
            normed, _ = norm_rows(x)
            first_all[n] = (normed * gain_ref[...]).astype(BF16)
            rows = pl.ds(pl.multiple_of(n * TB, TB), TB)
            x_own[rows, :] = x.astype(BF16)
            g_own[rows, :] = own_taps(gs, half, n, first, longest_here).astype(BF16)
            return carry

        lax.fori_loop(0, half // TB // 2, prepare, 0)
        first_gather.pass_beside()
        lax.fori_loop(half // TB // 2, half // TB, prepare, 0)
        first_gather.arrive()
        first_gather.finish()
        for copy in keep_copies[:4]:
            copy.start()

    mask = mask_rows[block, 0:1]
    first_in = first_all[block]
    for slot in range(w_ref.shape[0]):
        at = slice(slot * own, (slot + 1) * own)
        part = nt(w_ref[slot], first_in)
        q_ref[at, :] = part[0:own].astype(BF16)
        k_ref[at, :] = (part[own : 2 * own] * mask).astype(BF16)
        v_ref[at, :] = (part[2 * own : 3 * own] * mask).astype(BF16)
    rows = key_rows(block)
    for h in range(heads):
        band = slice(h * hd, (h + 1) * hd)
        slot, i = divmod(h, own_heads)
        for n, src, plain, trans in ((0, k_ref, ck_ref, ckt_ref), (1, v_ref, cv_ref, cvt_ref)):
            grouped = jnp.concatenate([src[band, r * GB : (r + 1) * GB] for r in range(3)], axis=0)
            comp = nn(conv_ref[slot, i * hd : (i + 1) * hd, n * conv_cols : n * conv_cols + taps], grouped)
            trans[band, rows] = comp.astype(BF16)
            plain[h, rows, :] = comp.T.astype(BF16)
    places, starts = item_starts(lens_ref, block, longest_here, half // 3)
    lse_ref[heads:, :] = jnp.broadcast_to(mask, (lse_ref.shape[0] - heads, TB))

    @pl.when(block == blocks - 1)
    def _():
        for copy in keep_copies[4:]:
            copy.start()

    peers = w_ref.shape[0]
    for s in range(1, peers):
        pl.when(block == s - 1)(functools.partial(last_gather.pass_around, s))
        if s < peers - 1:
            pl.when(block == blocks_there - peers + 1 + s)(functools.partial(last_gather.pass_beside, s))

    @pl.when(block < blocks // 2)
    def _():
        lse_ref[0:heads, :] = jnp.zeros_like(lse_ref[0:heads, :])

    def put_lse(one, values):
        lse_ref[one, :] = values

    for n in range(blocks_there // 2, blocks_there):
        pl.when(block == n)(
            functools.partial(
                attend_forward, heads, hd, n + 1, places, starts, bias_ref, ck_ref, cvt_ref, q_ref, k_ref, v_ref,
                ctx_ref, put_lse,
            )
        )

    @pl.when(block == blocks - 1)
    def _():
        last_gather.pass_beside(w_ref.shape[0] - 1)

    @pl.when(block == blocks - 1)
    def _():
        last_gather.arrive()
        last_gather.finish()
        for copy in keep_copies:
            copy.wait()


def feed_forward(
    heads, hd, block, swap, x_ref, g_ref, gain_ref, ctx_ref, out_ref, up_ref, down_ref,
    out_far, up_far, down_far, resid_all, dctx_all, delta_all, grads_ref,
    acts, hidden_grads, pre, act_grads, ff_sum, out_sum, gain_sum,
):
    own, two = out_ref.shape[0], out_sum.shape[0]
    units = up_ref.shape[1]
    step = pre.shape[2]
    slots = up_far.shape[0] + 1
    gain = gain_ref[...]
    g_low = g_ref[...]
    resid = x_ref[...].astype(F32) + tn(ctx_ref[0:own, :], out_ref[...]) + tn(ctx_ref[own:, :], out_far[...])
    hat, inv_std = norm_rows(resid)
    second_in = (hat * gain).astype(BF16)

    def up(slot, cols=slice(None)):
        return up_ref[:, cols] if slot == 0 else up_far[slot - 1, :, cols]

    def down(slot, rows=slice(None)):
        return down_ref[rows, :] if slot == 0 else down_far[slot - 1, rows, :]

    def products(c):
        slot, at = divmod(c * step, units)
        part = slice(at, at + step)
        pre[c % 2] = nn(second_in, up(slot, part))
        act_grads[c % 2] = nt(g_low, down(slot, part))

    count = slots * units // step
    products(0)
    for c in range(count):
        if c + 1 < count:
            products(c + 1)
        act, slope = gelu_and_slope(pre[c % 2])
        act = act.astype(BF16)
        hidden_grad = (act_grads[c % 2] * slope).astype(BF16)
        part = slice(c * step, (c + 1) * step)
        acts[:, part] = act
        hidden_grads[:, part] = hidden_grad
        slot, at = divmod(c * step, units)
        if slot < 2:
            ff_sum[slot, 0, :, at : at + step] += tn(second_in, hidden_grad)
            ff_sum[slot, 1, :, at : at + step] += tn(g_low, act)
    parts = [slice(slot * units, (slot + 1) * units) for slot in range(slots)]
    ffn = sum(nn(acts[:, part], down(slot)) for slot, part in enumerate(parts))
    swap.send(block, (resid + ffn).astype(BF16))
    back = sum(nt(hidden_grads[:, part], up(slot)) for slot, part in enumerate(parts))
    gain_sum[...] += jnp.sum(back * hat, axis=0, keepdims=True)
    resid_grad = g_low.astype(F32) + norm_back(back, gain, hat, inv_std)
    attn_grad = resid_grad.astype(BF16)
    resid_all[block] = attn_grad
    out_sum[...] += nn(ctx_ref[0:two, :], attn_grad)
    dctx = jnp.concatenate([nt(out_ref[...], attn_grad), nt(out_far[...], attn_grad)], axis=0).astype(BF16)
    dctx_all[block] = dctx
    dots = dctx.astype(F32) * ctx_ref[...].astype(F32)
    for h in range(heads):
        delta_all[block, h : h + 1, :] = jnp.sum(dots[h * hd : (h + 1) * hd], axis=0, keepdims=True)

    @pl.when(block == 0)
    def _():
        pieces = []
        for slot in range(2):
            pieces += [ff_sum[slot, 0], ff_sum[slot, 1], out_sum[slot * own : (slot + 1) * own].T]
        put_rows(grads_ref, pieces + [jnp.broadcast_to(gain_sum[...], (GB, gain.shape[1])).T])


def attention_back(
    heads, hd, own_heads, lens_ref, block, swap, x_ref, gain_ref, w_ref, q_ref, k_ref, v_ref, stats_ref,
    lse_all, dctx_all, delta_all, resid_all, ck_ref, ckt_ref, cv_ref,
    bias_ref, convs_ref, dck_sum, dcv_sum, dq_sum, dqkv, weight_sum, kconv_sum, vconv_sum, gain_sum,
):
    own = own_heads * hd
    slots, _, dim = w_ref.shape
    slot_heads = heads // slots
    lanes = slot_heads * hd
    factor = 1.0 / math.sqrt(hd)
    scale = LOG2E * factor
    longest_here = lax.rem(lax.axis_index("tensor"), 2) == 0
    places, starts = item_starts(lens_ref, block, longest_here, ck_ref.shape[1])

    def attend(count):
        keys = slice(0, count * GB)
        put_bias(bias_ref, places, starts, count)

        def head(h, band, one):
            q, dctx = q_ref[band, :], dctx_all[block, band, :]
            s = nn(ck_ref[h, keys, :], q) * scale + jnp.concatenate([bias_ref[keys, :]] * 3, axis=1)
            p = jnp.exp2(s - lse_all[block, one, :])
            dp = nn(cv_ref[h, keys, :], dctx)
            ds = (p * (dp - delta_all[block, one, :])).astype(BF16)
            dcv_sum[h, keys, :] += nt(p.astype(BF16), dctx)
            dck_sum[h, keys, :] += nt(ds, q)
            dq_sum[band, :] = nn(ckt_ref[band, keys], ds)

        each_head(heads, hd, head)

    for n in range(ck_ref.shape[1] // GB):
        pl.when(block == n)(functools.partial(attend, n + 1))
    mask = stats_ref[heads : heads + 1, :]
    rows = key_rows(block)
    later = []
    for h in range(heads):
        band = slice(h * hd, (h + 1) * hd)
        one = slice(h, h + 1)
        q, k = q_ref[band, :].astype(F32), k_ref[band, :].astype(F32)
        v, dctx = v_ref[band, :].astype(F32), dctx_all[block, band, :].astype(F32)
        own_prob = jnp.exp2(jnp.sum(q * k, axis=0, keepdims=True) * scale - lse_all[block, one, :])
        own_dprob = jnp.sum(dctx * v, axis=0, keepdims=True)
        own_dscore = own_prob * (own_dprob - delta_all[block, one, :]) * factor
        slot, i = divmod(h, slot_heads)
        base = slot * 3 * lanes + i * hd
        dqkv[base : base + hd, :] = (dq_sum[band, :] * factor + own_dscore * k).astype(BF16)
        dck = (dck_sum[h, rows, :] * factor).astype(BF16)
        dcv = dcv_sum[h, rows, :].astype(BF16)
        for n, src, total, grad, beside in (
            (0, k_ref, kconv_sum, dck, own_dscore * q),
            (1, v_ref, vconv_sum, dcv, own_prob * dctx),
        ):
            spread = nt(convs_ref[n, h], grad)
            spread = jnp.concatenate([spread[r * hd : (r + 1) * hd] for r in range(3)], axis=1)
            at = base + (n + 1) * lanes
            dqkv[at : at + hd, :] = ((spread + beside) * mask).astype(BF16)
            if h < own_heads:
                grouped = jnp.concatenate([src[band, r * GB : (r + 1) * GB] for r in range(3)], axis=0)
                later.append((total, h, grouped, grad))
    hat, inv_std = norm_rows(x_ref[...].astype(F32))
    gain = gain_ref[...]
    first_in = (hat * gain).astype(BF16)
    back = tn(dqkv[...], w_ref[...].reshape(slots * 3 * lanes, dim))
    total = resid_all[block].astype(F32) + norm_back(back, gain, hat, inv_std)
    swap.send(block, total.astype(BF16))
    gain_sum[...] += jnp.sum(back * hat, axis=0, keepdims=True)
    weight_sum[...] += nn(dqkv[0 : 3 * own, :], first_in)
    for into, h, grouped, grad in later:
        into[h] += nn(grouped, grad)


def schedule(step, blocks):
    late = (step + 3) // (2 * blocks)
    started = (step + 2 * blocks - 1) // (2 * blocks)
    last = (step + 4) // (2 * blocks)
    forward = started * (1 - last) * (blocks - 1 - (step + 1) // 2)
    forward = forward + (1 - started) * (blocks - 1)
    backward = started * ((1 - late) * (blocks - step // 2) + late * (2 * blocks - 1 - step))
    backward = backward + (1 - started) * (blocks - 1)
    backward = jnp.minimum(backward, blocks - 1)
    is_forward = (1 - started) + started * (1 - late) * ((step % 2) * (1 - last) + last * (1 - late))
    return forward, backward, is_forward


def later_kernel(
    heads, hd, own_heads, lens_ref,
    x_ref, g_ref, gain2_ref, ctx_ref, out_ref, up_ref, down_ref, out_far, up_hbm, down_hbm,
    q_front, k_front, v_front,
    x_back, gain1_ref, q_ref, k_ref, v_ref, lse_ref, w_hbm, conv_hbm, ck_hbm, ckt_hbm, cv_hbm, cvt_hbm,
    mixed_ref, mixed_peer, tokens_ref, tokens_peer, middle_out, last_out, conv_out,
    up_far, down_far, w_ref, conv_ref, ck_ref, ckt_ref, cv_ref, cvt_ref,
    mixed_staged, acts, hidden_grads, pre, act_grads, ff_sum, out_sum, gain2_sum,
    ctx_block, lse_all, dctx_all, resid_all, delta_all,
    bias_ref, convs_ref, dck_sum, dcv_sum, dq_sum, dqkv, weight_sum, kconv_sum, vconv_sum, gain1_sum,
    middle_parts, middle_pair, middle_in, last_parts, last_pair, last_in, conv_parts, conv_pair, conv_in,
    middle_turn, last_turn, conv_turn, middle_sum, last_sum, conv_sum,
    mixed_sems, mixed_local, swap_sems, swap_local, middle_sems, last_sems, conv_sems, turn_sems, load_sems,
):
    step_id = pl.program_id(0)
    blocks = dctx_all.shape[0]
    forward_block, backward_block, is_forward = schedule(step_id, blocks)
    mixed_swap = Swap(mixed_staged, mixed_ref, mixed_peer, mixed_sems, mixed_local)
    swap = Swap(resid_all, tokens_ref, tokens_peer, swap_sems, swap_local)
    middle = Spread(middle_parts, middle_pair, middle_in, middle_sum, middle_sems)
    last = Spread(last_parts, last_pair, last_in, last_sum, last_sems)
    convs = Spread(conv_parts, conv_pair, conv_in, conv_sum, conv_sems)
    slots, _, dim = w_ref.shape
    taps = convs_ref.shape[2]
    conv_cols = conv_ref.shape[2] // 2
    slot_heads = heads // slots

    loads = [
        pltpu.make_async_copy(src, dst, load_sems.at[n])
        for n, (src, dst) in enumerate(
            (
                (up_hbm, up_far), (down_hbm, down_far), (w_hbm, w_ref), (conv_hbm, conv_ref), (ck_hbm, ck_ref), (ckt_hbm, ckt_ref), (cv_hbm, cv_ref),
                (cvt_hbm, cvt_ref),
            )
        )
    ]

    @pl.when(step_id == 0)
    def _():
        for load in loads:
            load.start()
        count = lax.axis_size("dp")
        me, peer = lax.axis_index("dp"), lax.axis_index("tensor")
        devices = [swap.device, (me ^ 1, peer)] + [(lax.rem(me + 2 * s, count), peer) for s in range(1, count // 2)]
        greet(devices)
        for ref in (ff_sum, out_sum, gain2_sum):
            ref[...] = jnp.zeros_like(ref)
        for load in loads[:2]:
            load.wait()
        greeted(devices)

    @pl.when(step_id == 2)
    def _():
        for load in loads[2:]:
            load.wait()
        for ref in (dck_sum, dcv_sum, weight_sum, kconv_sum, vconv_sum, gain1_sum):
            ref[...] = jnp.zeros_like(ref)
        for h in range(heads):
            slot, i = divmod(h, slot_heads)
            for n in range(2):
                conv = conv_ref[slot, i * hd : (i + 1) * hd, n * conv_cols : n * conv_cols + taps]
                convs_ref[n, h] = conv.astype(F32).T.astype(BF16)

    longest_here = lax.rem(lax.axis_index("tensor"), 2) == 0

    @pl.when(is_forward == 1)
    def _():
        places, starts = item_starts(lens_ref, forward_block, longest_here, ck_ref.shape[1])

        def put_lse(one, values):
            lse_all[forward_block, one, :] = values

        @pl.when(forward_block >= blocks // 2)
        def _():
            ctx_block[...] = ctx_ref[...]

        for n in range(blocks // 2):
            pl.when(forward_block == n)(
                functools.partial(
                    attend_forward, heads, hd, n + 1, places, starts, bias_ref, ck_ref, cvt_ref, q_front, k_front,
                    v_front, ctx_block, put_lse,
                )
            )
        feed_forward(
            heads, hd, forward_block, mixed_swap, x_ref, g_ref, gain2_ref, ctx_block, out_ref, up_ref, down_ref,
            out_far, up_far, down_far, resid_all, dctx_all, delta_all, middle_parts,
            acts, hidden_grads, pre, act_grads, ff_sum, out_sum, gain2_sum,
        )

        @pl.when(forward_block == 0)
        def _():
            middle.start()

    @pl.when(is_forward == 0)
    def _():
        @pl.when(backward_block >= blocks // 2)
        def _():
            lse_all[backward_block] = lse_ref[0:heads, :]

        attention_back(
            heads, hd, own_heads, lens_ref, backward_block, swap, x_back, gain1_ref, w_ref, q_ref, k_ref, v_ref, lse_ref,
            lse_all, dctx_all, delta_all, resid_all, ck_ref, ckt_ref, cv_ref,
            bias_ref, convs_ref, dck_sum, dcv_sum, dq_sum, dqkv, weight_sum, kconv_sum, vconv_sum, gain1_sum,
        )

    @pl.when((is_forward == 0) & (backward_block == blocks // 2 - 1))
    def _():
        middle.pass_on()

    def turned(n, ref):
        return remote(ref.at[0], ref.at[1], turn_sems, (n,), swap.device)

    def turn(n, ref, total):
        ref[0] = total[:, total.shape[1] - ref.shape[2] :].astype(BF16)
        turned(n, ref).start()

    @pl.when(step_id == 2 * blocks - 1)
    def _():
        put_rows(last_parts, [weight_sum[...].T, jnp.broadcast_to(gain1_sum[...], (GB, dim)).T])
        last.start()
        put_rows(
            conv_parts,
            [
                total[h]
                for slot in range(2)
                for total in (kconv_sum, vconv_sum)
                for h in range(slot * slot_heads, (slot + 1) * slot_heads)
            ],
        )
        convs.start()
        turn(0, middle_turn, middle.total())
        last.pass_on()
        convs.pass_on()
        sums = ((middle_out, middle_turn, middle), (last_out, last_turn, last), (conv_out, conv_turn, convs))
        for n, (_, ref, spread) in enumerate(sums):
            if n > 0:
                turn(n, ref, spread.total())
        for n, (out, ref, spread) in enumerate(sums):
            turned(n, ref).wait()
            total, cols = spread.sums, out.shape[1]
            split = total.shape[1] - cols
            kept = [total[:, :split]] + ([total[:, 2 * split :]] if cols > split else [])
            out[...] = ref[1].astype(F32) + jnp.concatenate(kept, axis=1)
        mixed_swap.finish()
        swap.finish()


def place_rows(lens_ref, longest_here, mine, theirs, natural, out_ref):
    half = mine.shape[0]
    first = longest_first(lens_ref, half // 3)

    def taps(block, r, other):
        rows = slice(block * TB + r * GB, block * TB + (r + 1) * GB)
        a, b = mine[rows, :].astype(F32), theirs[rows, :].astype(F32)
        return jnp.where(longest_here == other, b, a)

    parts = natural.shape[0]
    for block in range(half // TB):
        for r in range(3):
            others = taps(block, r, True)
            for c in range(parts):
                for base in (0, half):
                    natural[c, pl.ds(base + block * TB + r, GB, stride=3), :] = others[:, c * 128 : (c + 1) * 128]
    for block in range(half // TB):
        for r in range(3):
            longest = taps(block, r, False)
            for c in range(parts):
                natural[c, pl.ds(first + block * TB + r, GB, stride=3), :] = longest[:, c * 128 : (c + 1) * 128]
    for c in range(parts):
        out_ref[:, c * 128 : (c + 1) * 128] = natural[c, 0 : 2 * half, :].astype(BF16)


def last_kernel(
    hd, lens_ref, mixed_ref, mixed_peer, tokens_ref, tokens_peer, middle_ref, last_ref, conv_ref,
    mixed_out, tokens_out, gain1_out, gain2_out, query_out, key_out, value_out, out_out, kconv_out, vconv_out,
    up_out, down_out, natural_mixed, natural_tokens,
):
    longest_here = lax.rem(lax.axis_index("tensor"), 2) == 0
    place_rows(lens_ref, longest_here, mixed_ref, mixed_peer, natural_mixed, mixed_out)
    place_rows(lens_ref, longest_here, tokens_ref, tokens_peer, natural_tokens, tokens_out)

    @pl.when(pl.program_id(0) == 0)
    def _():
        units, own = up_out.shape[1], query_out.shape[1]
        up_out[...] = middle_ref[:, 0:units]
        down_out[...] = middle_ref[:, units : 2 * units]
        out_out[...] = middle_ref[:, 2 * units : 2 * units + own]
        gain2_out[...] = middle_ref[:, 2 * units + own :].T[0:1]
        for n, out in enumerate((query_out, key_out, value_out)):
            out[...] = last_ref[:, n * own : (n + 1) * own]
        gain1_out[...] = last_ref[:, 3 * own :].T[0:1]
        for n, out in enumerate((kconv_out, vconv_out)):
            for h in range(out.shape[0]):
                out[h] = conv_ref[:, n * own + h * hd : n * own + (h + 1) * hd]


def whole(shape):
    return pl.BlockSpec(shape, lambda *_: (0,) * len(shape))


def cost(micros):
    return pl.CostEstimate(flops=int(micros * 1e9), bytes_accessed=1 << 20, transcendentals=0)


def params():
    return pltpu.CompilerParams(vmem_limit_bytes=VMEM, dimension_semantics=("arbitrary",))


def on_device(
    tokens, first_gain, second_gain, query_weight, key_weight, value_weight, out_weight,
    key_conv, value_conv, up_weight, down_weight, pad_mask, item_lengths, cotangent,
):
    dim = tokens.shape[1]
    own_heads, taps, hd = key_conv.shape
    peers = lax.axis_size("tensor")
    heads = own_heads * peers
    width = heads * hd
    own = own_heads * hd
    units = up_weight.shape[1]
    lens = item_lengths[0]
    rows = tokens.shape[0] // 2
    blocks = rows // TB
    groups = rows // 3
    pads = pad_mask.reshape(-1, 128)
    key_conv, value_conv = key_conv.transpose(0, 2, 1), value_conv.transpose(0, 2, 1)
    conv_cols = -(-taps // 128) * 128
    stats = heads + 8
    gain1, gain2 = first_gain[None], second_gain[None]

    rows_spec = pl.BlockSpec((TB, dim), lambda b, *_: (b, 0))
    cols_spec = pl.BlockSpec((width, TB), lambda b, *_: (0, b))
    stat_spec = pl.BlockSpec((heads, TB), lambda b, *_: (0, b))
    lse_spec = pl.BlockSpec((stats, TB), lambda b, *_: (0, b))
    early = blocks // 2
    late_cols = pl.BlockSpec((width, TB), lambda b, *_: (0, jnp.maximum(b - early, 0)))
    anywhere = pl.BlockSpec(memory_space=pl.ANY)
    inside = pl.BlockSpec(memory_space=pltpu.VMEM)
    q, k, v, ctx, lse, x, g, ck, ckt, cv, cvt, w_all, conv_all, out_far, up_far, down_far = pl.pallas_call(
        functools.partial(forward_kernel, heads, hd),
        grid_spec=pltpu.PrefetchScalarGridSpec(
            num_scalar_prefetch=1,
            grid=(blocks,),
            in_specs=[inside, inside, whole((1, dim))] + [inside] * 6 + [anywhere] * 3,
            out_specs=[
                cols_spec, cols_spec, cols_spec, late_cols, lse_spec,
            ]
            + [anywhere] * 11,
            scratch_shapes=[
                pltpu.VMEM((dim // 128 + 1, 2 * rows + 8, 128), F32), pltpu.VMEM((dim // 128, 2 * rows + 8, 128), F32),
                pltpu.VMEM((rows, dim), BF16), pltpu.VMEM((rows, dim), BF16),
                pltpu.VMEM((heads, groups, hd), BF16), pltpu.VMEM((width, groups), BF16),
                pltpu.VMEM((heads, groups, hd), BF16), pltpu.VMEM((width, groups), BF16),
                pltpu.VMEM((blocks, TB, dim), BF16), pltpu.VMEM((blocks, 8, TB), F32),
                pltpu.VMEM((peers, 3 * own, dim), BF16), pltpu.VMEM((peers, own, 2 * conv_cols), BF16),
                pltpu.VMEM((groups, GB), F32),
                pltpu.SemaphoreType.DMA((2, 2, 5, peers - 1)), pltpu.SemaphoreType.DMA((2, 3, 5, peers - 1)),
                pltpu.SemaphoreType.DMA((8,)),
            ],
        ),
        out_shape=[jax.ShapeDtypeStruct((width, rows), BF16)] * 3
        + [
            jax.ShapeDtypeStruct((width, (blocks - early) * TB), BF16),
            jax.ShapeDtypeStruct((stats, rows), F32),
            jax.ShapeDtypeStruct((rows, dim), BF16),
            jax.ShapeDtypeStruct((rows, dim), BF16),
            jax.ShapeDtypeStruct((heads, groups, hd), BF16),
            jax.ShapeDtypeStruct((width, groups), BF16),
            jax.ShapeDtypeStruct((heads, groups, hd), BF16),
            jax.ShapeDtypeStruct((width, groups), BF16),
            jax.ShapeDtypeStruct((peers, 3 * own, dim), BF16),
            jax.ShapeDtypeStruct((peers, own, 2 * conv_cols), BF16),
            jax.ShapeDtypeStruct((peers - 1, own, dim), BF16),
            jax.ShapeDtypeStruct((peers - 1, dim, units), BF16),
            jax.ShapeDtypeStruct((peers - 1, units, dim), BF16),
        ],
        compiler_params=pltpu.CompilerParams(
            vmem_limit_bytes=VMEM, dimension_semantics=("arbitrary",), collective_id=0, has_side_effects=True
        ),
        cost_estimate=cost(55),
        name="attention_forward",
    )(
        lens, tokens, cotangent, gain1, pads, query_weight, key_weight, value_weight, key_conv, value_conv,
        out_weight, up_weight, down_weight,
    )

    count = lax.axis_size("dp")
    slot_cols = 2 * units + own
    mid_cols = 2 * slot_cols + GB
    last_cols = 6 * own + GB
    two = 2 * own_heads
    step = 256

    def forward_at(n):
        return schedule(n, blocks)[0]

    def backward_at(n):
        return schedule(n, blocks)[1]

    def left_at(n):
        return jnp.minimum(forward_at(n), early - 1)

    left_cols = pl.BlockSpec((width, TB), lambda n, *_: (0, left_at(n)))
    front_rows = pl.BlockSpec((TB, dim), lambda n, *_: (forward_at(n), 0))
    front_cols = pl.BlockSpec((width, TB), lambda n, *_: (0, jnp.maximum(forward_at(n) - early, 0)))
    back_rows = pl.BlockSpec((TB, dim), lambda n, *_: (backward_at(n), 0))
    back_cols = pl.BlockSpec((width, TB), lambda n, *_: (0, backward_at(n)))
    back_lse = pl.BlockSpec((stats, TB), lambda n, *_: (0, backward_at(n)))
    out_dims = [(dim // count, slot_cols + GB), (dim // count, 3 * own + GB), (taps // count, 2 * own)]
    swap_sems = [pltpu.SemaphoreType.DMA((2, blocks)), pltpu.SemaphoreType.DMA((blocks,))]
    spread_sems = pltpu.SemaphoreType.DMA((2, count // 2))
    split = [(dim // count, mid_cols), (dim // count, last_cols), (taps // count, 4 * own)]
    mixed, mixed_peer, grad_rows, grad_peer, middle_share, last_share, conv_share = pl.pallas_call(
        functools.partial(later_kernel, heads, hd, two),
        grid_spec=pltpu.PrefetchScalarGridSpec(
            num_scalar_prefetch=1,
            grid=(2 * blocks,),
            in_specs=[front_rows, front_rows, inside, front_cols]
            + [inside] * 4
            + [anywhere] * 2
            + [left_cols] * 3
            + [back_rows, inside, back_cols, back_cols, back_cols, back_lse]
            + [anywhere] * 6,
            out_specs=[anywhere] * 4 + [whole(d) for d in out_dims],
            scratch_shapes=[
                pltpu.VMEM((peers - 1, dim, units), BF16), pltpu.VMEM((peers - 1, units, dim), BF16),
                pltpu.VMEM((peers, 3 * own, dim), BF16), pltpu.VMEM((peers, own, 2 * conv_cols), BF16),
                pltpu.VMEM((heads, groups, hd), BF16), pltpu.VMEM((width, groups), BF16),
                pltpu.VMEM((heads, groups, hd), BF16), pltpu.VMEM((width, groups), BF16),
                pltpu.VMEM((blocks, TB, dim), BF16),
                pltpu.VMEM((TB, peers * units), BF16), pltpu.VMEM((TB, peers * units), BF16),
                pltpu.VMEM((2, TB, step), F32), pltpu.VMEM((2, TB, step), F32),
                pltpu.VMEM((2, 2, dim, units), F32), pltpu.VMEM((2 * own, dim), F32), pltpu.VMEM((1, dim), F32),
                pltpu.VMEM((width, TB), BF16), pltpu.VMEM((blocks, heads, TB), F32),
                pltpu.VMEM((blocks, width, TB), BF16), pltpu.VMEM((blocks, TB, dim), BF16),
                pltpu.VMEM((blocks, heads, TB), F32),
                pltpu.VMEM((groups, GB), F32),
                pltpu.VMEM((2, heads, taps, hd), BF16), pltpu.VMEM((heads, groups, hd), F32),
                pltpu.VMEM((heads, groups, hd), F32), pltpu.VMEM((width, TB), F32),
                pltpu.VMEM((3 * width, TB), BF16), pltpu.VMEM((6 * own, dim), F32),
                pltpu.VMEM((two, taps, hd), F32), pltpu.VMEM((two, taps, hd), F32),
                pltpu.VMEM((1, dim), F32),
            ]
            + [pltpu.VMEM((*lead, *d), BF16) for d in split for lead in ((2, count // 2), (count // 2,), (count // 2,))]
            + [pltpu.VMEM((2, *d), BF16) for d in out_dims]
            + [pltpu.VMEM(d, F32) for d in split]
            + swap_sems * 2
            + [spread_sems] * 3
            + [pltpu.SemaphoreType.DMA((2, 3)), pltpu.SemaphoreType.DMA((8,))],
        ),
        out_shape=[jax.ShapeDtypeStruct((rows, dim), BF16)] * 4 + [jax.ShapeDtypeStruct(d, F32) for d in out_dims],
        compiler_params=pltpu.CompilerParams(
            vmem_limit_bytes=VMEM, dimension_semantics=("arbitrary",), collective_id=1, has_side_effects=True
        ),
        cost_estimate=cost(110),
        name="feed_forward_and_backward",
    )(
        lens, x, g, gain2, ctx, out_weight, up_weight, down_weight, out_far.reshape(width - own, dim), up_far, down_far,
        q, k, v, x, gain1, q, k, v, lse, w_all, conv_all, ck, ckt, cv, cvt,
    )

    share = dim // count
    own_conv = (own_heads, taps // count, hd)
    shapes = [
        ((1, share), F32), ((1, share), F32), ((share, own), F32), ((share, own), F32), ((share, own), F32),
        ((share, own), F32), (own_conv, F32), (own_conv, F32), ((share, units), F32), ((share, units), F32),
    ]
    lanes = 256
    lane_half = pl.BlockSpec((rows, lanes), lambda c: (0, c))
    lane_all = pl.BlockSpec((2 * rows, lanes), lambda c: (0, c))
    outs = pl.pallas_call(
        functools.partial(last_kernel, hd),
        grid=(dim // lanes,),
        in_specs=[pl.BlockSpec(memory_space=pltpu.SMEM)] + [lane_half] * 4 + [whole(d) for d in out_dims],
        out_specs=[lane_all] * 2 + [whole(d) for d, _ in shapes],
        out_shape=[jax.ShapeDtypeStruct((2 * rows, dim), BF16)] * 2 + [jax.ShapeDtypeStruct(d, t) for d, t in shapes],
        scratch_shapes=[pltpu.VMEM((lanes // 128, 2 * rows + 8, 128), F32)] * 2,
        compiler_params=params(),
        cost_estimate=cost(15),
        name="in_order",
    )(lens, mixed, mixed_peer, grad_rows, grad_peer, middle_share, last_share, conv_share)
    mixed, grad_tokens, gain1, gain2, query, key, value, out, kconv, vconv, up, down = outs
    return (
        mixed, grad_tokens, gain1.reshape(share), gain2.reshape(share), query, key, value, out.T,
        kconv, vconv, up, down.T,
    )


def solution(mesh):
    in_specs = (
        P("dp", None),
        P(),
        P(),
        P(None, "tensor"),
        P(None, "tensor"),
        P(None, "tensor"),
        P("tensor", None),
        P("tensor", None, None),
        P("tensor", None, None),
        P(None, "tensor"),
        P("tensor", None),
        P("dp"),
        P("dp", None),
        P("dp", None),
    )
    out_specs = (
        P("dp", None),
        P("dp", None),
        P("dp"),
        P("dp"),
        P("dp", "tensor"),
        P("dp", "tensor"),
        P("dp", "tensor"),
        P("tensor", "dp"),
        P("tensor", "dp", None),
        P("tensor", "dp", None),
        P("dp", "tensor"),
        P("tensor", "dp"),
    )
    return jax.shard_map(
        on_device, mesh=mesh, in_specs=in_specs, out_specs=out_specs, check_vma=False
    )
```
